128 devices in a mesh: narrow: 16 (over z, y_lo, core), wide: 8 (over y_hi, x).
Axes of the slice: x: 4, y: 4 (y_hi: 2, y_lo: 2; y = y_hi * 2 + y_lo), z: 4, core: 2. Of those that a mesh axis runs over, the one named last changes fastest.
Arguments:
- features: bfloat16 [4096, 16384], P(None, ('narrow', 'wide')), may hold values from -6 to 6
- in_proj: bfloat16 [768, 4096], P(('narrow', 'wide')), may hold values from -0.09375 to 0.09375
- short_taps: float32 [3, 768], replicated, may hold values from -3 to 3
- long_filter: bfloat16 [256, 16384], P(None, ('narrow', 'wide')), may hold values from -4 to 4
- out_grad: bfloat16 [256, 16384], P(None, ('narrow', 'wide')), may hold values from -11 to 11
Outputs:
- mixed_out: bfloat16 [256, 16384], P(None, ('narrow', 'wide'))
- feat_grad: bfloat16 [4096, 16384], P(None, ('narrow', 'wide'))
- filter_grad: bfloat16 [256, 16384], P(None, ('narrow', 'wide'))
- taps_grad: float32 [3, 768], replicated
- proj_grad: float32 [768, 4096], P(('narrow', 'wide'))
The draws below stay inside these ranges and needn't reach their ends.
All inputs are finite; a program needn't handle non-finite values.
Results may differ from the reference program's by a relative error of at most 0.013.
Values may be sent and summed in bfloat16 or wider, within the bound.
A program may use at most 128 MiB of HBM per device.

```python
import math
import jax
import jax.numpy as jnp

CH = 256
D = 4096
TOKENS = 16384


def draw_long_filter(key, part):
    key = jax.random.fold_in(key, 11)
    key_slow, key_fast, key_pick, key_noise = jax.random.split(key, 4)
    span = float(TOKENS)
    position = jnp.arange(TOKENS, dtype=jnp.float32)[None, :]
    slow_rate = jnp.exp(jax.random.uniform(key_slow, (CH, 1), minval=math.log(0.3 / span), maxval=math.log(2.0 / span)))
    picked = jax.random.uniform(key_pick, (CH, 1)) < 0.5
    noise = jnp.clip(jax.random.normal(key_noise, (CH, TOKENS)), -6.0, 6.0)
    fast_rate = jnp.exp(jax.random.uniform(key_fast, (CH, 1), minval=math.log(1.0 / 40.0), maxval=math.log(1.0 / 30.0)))
    rate = jnp.where(picked, fast_rate, slow_rate)
    amplitude = jnp.sqrt(1.0 - jnp.exp(-2.0 * rate))
    return (noise * amplitude * jnp.exp(-rate * position)).astype(jnp.bfloat16)


def draw_out_grad(key, part):
    key = jax.random.fold_in(key, 23)
    key_noise = jax.random.fold_in(key, 0)
    position = jnp.arange(TOKENS, dtype=jnp.float32)[None, :] / float(TOKENS)
    rising = 0.6 * jnp.exp(math.log(3.0) * position)
    noise = jnp.clip(jax.random.normal(key_noise, (CH, TOKENS)), -6.0, 6.0)
    return (noise * rising).astype(jnp.bfloat16)


def level_of(stream_key, extent, cuts, least, top_value):
    gain = 1.0
    for axis_at, blocks in cuts:
        steps = jax.random.uniform(jax.random.fold_in(jax.random.fold_in(stream_key, 6), axis_at), (blocks,), jnp.float32, least / len(cuts), top_value / len(cuts))
        gain = gain * jnp.repeat(jnp.exp(steps), extent[axis_at] // blocks).reshape((-1,) + (1,) * (len(extent) - 1 - axis_at))
    return gain


def gaussian(stream_key, extent, scale, limit, cuts=(), kind=jnp.bfloat16):
    entries = scale * jax.random.normal(stream_key, extent, jnp.float32)
    if cuts:
        entries = entries * level_of(stream_key, extent, cuts, -0.22, 0.18)
    return jnp.clip(entries, -limit, limit).astype(kind)


def setup_inputs(seed: int = 0) -> dict:
    arg_keys = jax.random.split(jax.random.key(seed), 6)
    features = gaussian(arg_keys[0], (D, TOKENS), 1.0, 6.0, ((1, 128),))
    in_proj = gaussian(arg_keys[1], (3 * CH, D), D ** -0.5, 0.09375, ((0, 128),))
    short_taps = gaussian(arg_keys[2], (3, 3 * CH), 0.7, 3.0, (), jnp.float32)
    long_filter = draw_long_filter(jax.random.fold_in(arg_keys[5], 71), 0)
    out_grad = draw_out_grad(jax.random.fold_in(arg_keys[5], 71), 0)
    return {"features": features, "in_proj": in_proj, "short_taps": short_taps, "long_filter": long_filter, "out_grad": out_grad}


def delayed(block, offset):
    return jnp.pad(block, ((0, 0), (offset, 0)))[:, :block.shape[1]]


def advanced(block, offset):
    return jnp.pad(block, ((0, 0), (0, offset)))[:, offset:]


def reference(features, in_proj, short_taps, long_filter, out_grad):
    length = features.shape[1]
    channels = out_grad.shape[0]
    projected = jnp.dot(in_proj, features, preferred_element_type=jnp.float32)
    taps = short_taps.astype(jnp.float32)
    featured = taps[0][:, None] * projected + taps[1][:, None] * delayed(projected, 1) + taps[2][:, None] * delayed(projected, 2)
    query_part = featured[:channels]
    key_part = featured[channels:2 * channels]
    value_part = featured[2 * channels:]
    gated = (key_part * value_part).astype(jnp.bfloat16)
    conv_grad = (out_grad.astype(jnp.float32) * query_part).astype(jnp.bfloat16)
    total = 2 * length
    filter_spec = jnp.fft.rfft(long_filter.astype(jnp.float32), n=total, axis=1)
    gated_spec = jnp.fft.rfft(gated.astype(jnp.float32), n=total, axis=1)
    cot_spec = jnp.fft.rfft(conv_grad.astype(jnp.float32), n=total, axis=1)
    convolved = jnp.fft.irfft(filter_spec * gated_spec, n=total, axis=1)[:, :length].astype(jnp.bfloat16)
    gate_grad = jnp.fft.irfft(jnp.conj(filter_spec) * cot_spec, n=total, axis=1)[:, :length].astype(jnp.bfloat16)
    filter_grad = jnp.fft.irfft(jnp.conj(gated_spec) * cot_spec, n=total, axis=1)[:, :length].astype(jnp.bfloat16)
    mixed_out = (query_part * convolved.astype(jnp.float32)).astype(jnp.bfloat16)
    gate_wide = gate_grad.astype(jnp.float32)
    feat_deriv = jnp.concatenate([out_grad.astype(jnp.float32) * convolved.astype(jnp.float32), gate_wide * value_part, gate_wide * key_part], axis=0)
    proj_deriv = (taps[0][:, None] * feat_deriv + taps[1][:, None] * advanced(feat_deriv, 1) + taps[2][:, None] * advanced(feat_deriv, 2)).astype(jnp.bfloat16)
    taps_grad = jnp.stack([jnp.sum(feat_deriv * delayed(projected, offset), axis=1) for offset in range(3)], axis=0)
    proj_grad = jnp.dot(proj_deriv, features.T, preferred_element_type=jnp.float32)
    feat_grad = jnp.dot(in_proj.T, proj_deriv, preferred_element_type=jnp.float32).astype(jnp.bfloat16)
    return mixed_out, feat_grad, filter_grad, taps_grad, proj_grad
```

```python
import math

import jax
import jax.numpy as jnp
from jax import lax
from jax.experimental import pallas as pl
from jax.experimental.pallas import tpu as pltpu
from jax.sharding import PartitionSpec as P

MESH = pl.DeviceIdType.MESH
BF = jnp.bfloat16
F32 = jnp.float32
ORDERS = (("x", "y", "z"), ("y", "z", "x"), ("z", "x", "y"))
AXES = ("narrow", "wide")


def place(pos):
    y = pos["y"]
    return (pos["z"] * 4 + lax.rem(y, 2) * 2 + pos["c"], (y // 2) * 4 + pos["x"])


def position():
    n = lax.axis_index("narrow")
    w = lax.axis_index("wide")
    pos = {
        "x": lax.rem(w, 4),
        "y": (w // 4) * 2 + lax.rem(n // 2, 2),
        "z": n // 4,
        "c": lax.rem(n, 2),
    }
    return n, w, pos


def shifted(pos, axis, by):
    other = dict(pos)
    other[axis] = lax.rem(pos[axis] + by + 4, 4)
    return place(other)


def other_core(pos):
    other = dict(pos)
    other["c"] = 1 - pos["c"]
    return place(other)


def shard_id(s):
    return (s // 8, lax.rem(s, 8))


def remote(src, dst, send, recv, device):
    return pltpu.make_async_remote_copy(
        src_ref=src, dst_ref=dst, send_sem=send, recv_sem=recv, device_id=device, device_id_type=MESH
    )


def greet(devices):
    barrier = pltpu.get_barrier_semaphore()
    for device in devices:
        pl.semaphore_signal(barrier, inc=1, device_id=device, device_id_type=MESH)
    pl.semaphore_wait(barrier, len(devices))


def piece_index(cls, z, yh, yl, x):
    at = {"x": x, "y": yh * 2 + yl, "z": z}
    d0, d1, d2 = ORDERS[cls]
    return (at[d2], at[d1], at[d0])


def one_hot(rows, cols, test):
    r = lax.broadcasted_iota(jnp.int32, (rows, cols), 0)
    c = lax.broadcasted_iota(jnp.int32, (rows, cols), 1)
    return jnp.where(test(r, c), 1.0, 0.0).astype(BF)


def gather_kernel(
    proj_ref, feat_ref, out_ref, halo_ref, g_ref, fo_ref,
    stage, land, blk, rows, hland, fh,
    s0, r0, ss, rs, ds, dr, hs, hr, fs, fr,
):
    n, w, pos = position()
    c = pos["c"]
    s = n * 8 + w
    right_shard = shard_id(lax.rem(s + 1, 128))
    left_shard = shard_id(lax.rem(s + 127, 128))
    wide_peers = [(n, lax.rem(w + i, 8)) for i in range(1, 8)]
    core = other_core(pos)
    for q in range(8):
        stage[q, 0:6, :] = proj_ref[:, q * 512 : (q + 1) * 512].astype(F32)
        stage[q, 6:8, :] = jnp.zeros((2, 512), F32)
    greet(
        wide_peers
        + [shifted(pos, a, d) for a in "yz" for d in (1, -1)]
        + [core, right_shard, left_shard]
    )
    first = []
    for i in range(1, 8):
        q = lax.rem(w + i, 8)
        cp = remote(stage.at[q], land.at[w], s0.at[i], r0.at[i], (n, q))
        cp.start()
        first.append(cp)
    fcp = remote(feat_ref, fo_ref, fs, fr, core)
    land[w] = stage[w]
    for cp in first:
        cp.wait_recv()
    for q in range(8):
        blk[q * 6 : (q + 1) * 6, :] = land[q, 0:6, :]

    index = [[pos[a] for a in reversed(order)] for order in ORDERS]
    for cls in range(3):
        i2, i1, i0 = index[cls]
        g_ref[cls, c, i2, i1, i0] = blk[cls * 16 : (cls + 1) * 16, :].astype(BF)

    def unit(cls, phase, j):
        i2, i1, _ = index[cls]
        if phase == 0:
            return g_ref.at[cls, c, i2, i1, j]
        if phase == 1:
            return g_ref.at[cls, c, i2, j]
        return g_ref.at[cls, c, j]

    def half(ref, phase, k):
        if phase == 0:
            return ref.at[:, pl.ds(k * 256, 256)]
        return ref.at[pl.ds(k * 2, 2)]

    started = [first[k] for k in range(7)]
    d2d = []

    def cross(cls, j, k):
        ref = g_ref.at[cls, c, j]
        cp = remote(ref, ref, ds.at[cls, k], dr.at[cls, k], core)
        cp.start()
        d2d.append(cp)

    for phase in range(3):
        legs = []
        for cls in range(3):
            axis = ORDERS[cls][phase]
            i = pos[axis]
            right, left = shifted(pos, axis, 1), shifted(pos, axis, -1)
            mine = unit(cls, phase, i)
            a = remote(mine, mine, ss.at[cls, phase, 0], rs.at[cls, phase, 0], right)
            b = remote(mine, mine, ss.at[cls, phase, 1], rs.at[cls, phase, 1], left)
            a.start()
            b.start()
            legs.append((a, b, right, left, i))
            if phase == 2:
                cross(cls, i, 0)
        if phase == 0:
            sel = one_hot(
                16, 128, lambda r, l: ((r < 2) & (l == r + 126)) | ((r >= 2) & (r < 4) & (l == r - 2))
            )
            rows[...] = lax.dot_general(
                sel, feat_ref[...], (((1,), (1,)), ((), ())), preferred_element_type=F32
            ).astype(BF)
            ha = remote(rows, hland.at[0], hs.at[0], hr.at[0], right_shard)
            hb = remote(rows, hland.at[1], hs.at[1], hr.at[1], left_shard)
            ha.start()
            hb.start()
            fcp.start()
            fh[:, 0:128] = feat_ref[...]
        if phase == 2:
            ha.wait_recv()
            hb.wait_recv()
            row = lax.broadcasted_iota(jnp.int32, (16, 4096), 0)
            both = jnp.where(row < 2, hland[0].astype(F32), hland[1].astype(F32)).astype(BF)
            lo = jnp.where(s > 0, 0, 2)
            hi = jnp.where(s < 127, 4, 2)
            spread = one_hot(16, 128, lambda r, l: (r == l) & (r >= lo) & (r < hi))
            fh[:, 128:256] = lax.dot_general(
                both, spread, (((0,), (0,)), ((), ())), preferred_element_type=F32
            ).astype(BF)
        second = []
        for cls in range(3):
            a, b, right, left, i = legs[cls]
            started += [a, b]
            a.wait_recv()
            got = unit(cls, phase, lax.rem(i + 3, 4))
            e = half(got, phase, 0)
            e = remote(e, e, ss.at[cls, phase, 2], rs.at[cls, phase, 2], right)
            e.start()
            b.wait_recv()
            got = unit(cls, phase, lax.rem(i + 1, 4))
            f = half(got, phase, 1)
            f = remote(f, f, ss.at[cls, phase, 3], rs.at[cls, phase, 3], left)
            f.start()
            second.append((e, f))
            if phase == 2:
                cross(cls, lax.rem(i + 3, 4), 1)
                cross(cls, lax.rem(i + 1, 4), 2)
        for cls in range(3):
            e, f = second[cls]
            started += [e, f]
            e.wait_recv()
            f.wait_recv()
            if phase == 2:
                cross(cls, lax.rem(legs[cls][4] + 2, 4), 3)
    for cp in d2d:
        cp.wait_recv()

    for cls in range(3):
        acc = None
        for yh in range(2):
            for x in range(4):
                lhs = wide_block(g_ref, cls, yh, x)
                q = yh * 4 + x
                term = jnp.dot(lhs, fh[q * 512 : (q + 1) * 512, :], preferred_element_type=F32)
                acc = term if acc is None else acc + term
        for m in range(16):
            out_ref[m * 48 + cls * 16 : m * 48 + cls * 16 + 16, :] = acc[m * 16 : (m + 1) * 16, 0:128]
            halo_ref[m * 48 + cls * 16 : m * 48 + cls * 16 + 16, :] = acc[m * 16 : (m + 1) * 16, 128:256]

    fcp.wait_recv()
    for cp in started + d2d + [ha, hb, fcp]:
        cp.wait_send()


def wide_block(g_ref, cls, yh, x):
    parts = []
    for z in range(4):
        for yl in range(2):
            for core in range(2):
                i2, i1, i0 = piece_index(cls, z, yh, yl, x)
                parts.append(g_ref[cls, core, i2, i1, i0])
    return jnp.concatenate(parts, axis=0)


VM = pl.BlockSpec(memory_space=pltpu.VMEM)


def gather_project(in_proj, features):
    sem = pltpu.SemaphoreType.DMA
    return pl.pallas_call(
        gather_kernel,
        out_shape=(
            jax.ShapeDtypeStruct((768, 128), F32),
            jax.ShapeDtypeStruct((768, 128), F32),
            jax.ShapeDtypeStruct((3, 2, 4, 4, 4, 16, 512), BF),
            jax.ShapeDtypeStruct((4096, 128), BF),
        ),
        in_specs=[VM, VM],
        out_specs=(VM, VM, VM, VM),
        scratch_shapes=[
            pltpu.VMEM((8, 8, 512), F32),
            pltpu.VMEM((8, 8, 512), F32),
            pltpu.VMEM((48, 512), F32),
            pltpu.VMEM((16, 4096), BF),
            pltpu.VMEM((2, 16, 4096), BF),
            pltpu.VMEM((4096, 256), BF),
            sem((8,)), sem((8,)),
            sem((3, 3, 4)), sem((3, 3, 4)),
            sem((3, 4)), sem((3, 4)),
            sem((2,)), sem((2,)),
            sem, sem,
        ],
        compiler_params=pltpu.CompilerParams(
            collective_id=1, has_side_effects=True, vmem_limit_bytes=48 * 1024 * 1024
        ),
        name="gather_project",
    )(in_proj, features)


def reduce_kernel(
    pd_ref, feat_ref, fo_ref, g_ref, taps_ref, grad_ref, fgrad_ref, tout_ref,
    pdo, pdc, p, ra3, rb3, rc3, rd3, ra2, rb2, rc2, rd2, ra1, rb1, rc1, rd1,
    blk, stage, land, tl,
    ps, pr, ss, rs, s0, r0, tsn, trc,
):
    n, w, pos = position()
    c = pos["c"]
    core = other_core(pos)
    wide_peers = [(n, lax.rem(w + i, 8)) for i in range(1, 8)]
    greet(
        wide_peers
        + [shifted(pos, a, d) for a in "yz" for d in (1, 2, 3)]
        + [core]
    )
    pcp = remote(pd_ref, pdo, ps, pr, core)
    pcp.start()

    sent = [pcp]

    def tap_send(k, peers, slot):
        cps = []
        for i, device in enumerate(peers):
            cp = remote(tl.at[k, slot], tl.at[k, slot], tsn.at[k, i], trc.at[k, i], device)
            cp.start()
            cps.append(cp)
        return cps

    def tap_sum(k, cps, count):
        for cp in cps:
            cp.wait_recv()
        sent.extend(cps)
        total = tl[k, 0]
        for i in range(1, count):
            total = total + tl[k, i]
        return total

    tl[0, c] = taps_ref[...]
    tcp = tap_send(0, [core], c)

    index = [[pos[a] for a in reversed(order)] for order in ORDERS]
    pcp.wait_recv()
    for cls in range(3):
        for z in range(4):
            for yl in range(2):
                at = pl.ds(pl.multiple_of((z * 4 + yl * 2 + c) * 48 + cls * 16, 16), 16)
                to = cls * 128 + z * 32 + yl * 16
                pdc[to : to + 16, 0:128] = pd_ref[at, :]
                pdc[to : to + 16, 128:256] = pdo[at, :]

    for yh in range(2):
        for x in range(4):
            cols = slice((yh * 4 + x) * 512, (yh * 4 + x + 1) * 512)
            rhs = jnp.concatenate([feat_ref[cols, :], fo_ref[cols, :]], axis=1)
            for cls in range(3):
                part = lax.dot_general(
                    pdc[cls * 128 : (cls + 1) * 128, :], rhs, (((1,), (1,)), ((), ())),
                    preferred_element_type=F32,
                ).astype(BF)
                for z in range(4):
                    for yl in range(2):
                        i2, i1, i0 = piece_index(cls, z, yh, yl, x)
                        k = z * 32 + yl * 16
                        p[cls, i2, i1, i0] = part[k : k + 16, :]

    def unit(cls, phase, j):
        i2, i1, _ = index[cls]
        if phase == 0:
            return p.at[cls, i2, i1, j]
        if phase == 1:
            return p.at[cls, i2, j]
        return p.at[cls, j]

    def half(ref, phase, k):
        if phase == 0:
            return ref.at[:, pl.ds(k * 256, 256)]
        return ref.at[pl.ds(k * 2, 2)]

    bufs = {2: (ra3, rb3, rc3, rd3), 1: (ra2, rb2, rc2, rd2), 0: (ra1, rb1, rc1, rd1)}

    def add(dst, src):
        dst[...] = (dst[...].astype(F32) + src[...].astype(F32)).astype(BF)

    def feat_part(qs):
        for q in qs:
            total = None
            for cls in range(3):
                lhs = jnp.concatenate(
                    [pd_ref[m * 48 + cls * 16 : m * 48 + cls * 16 + 16, :] for m in range(16)], axis=0
                )
                term = lax.dot_general(
                    lhs, wide_block(g_ref, cls, q // 4, q % 4), (((0,), (0,)), ((), ())),
                    preferred_element_type=F32,
                )
                total = term if total is None else total + term
            fgrad_ref[q * 512 : (q + 1) * 512, :] = total.T.astype(BF)

    for phase in (2, 1, 0):
        ra, rb, rc, rd = bufs[phase]
        legs = []
        for cls in range(3):
            axis = ORDERS[cls][phase]
            i = pos[axis]
            right, left = shifted(pos, axis, 1), shifted(pos, axis, -1)
            far = unit(cls, phase, lax.rem(i + 2, 4))
            up = unit(cls, phase, lax.rem(i + 1, 4))
            down = unit(cls, phase, lax.rem(i + 3, 4))

            def cp(k, src, dst, device):
                r = remote(src, dst, ss.at[cls, phase, k], rs.at[cls, phase, k], device)
                r.start()
                sent.append(r)
                return r

            a = cp(0, half(far, phase, 0), ra.at[cls], right)
            b = cp(1, half(far, phase, 1), rb.at[cls], left)
            d = cp(2, half(up, phase, 1), half(rc.at[cls], phase, 1), right)
            e = cp(3, half(down, phase, 0), half(rd.at[cls], phase, 0), left)
            legs.append((cp, a, b, d, e, up, down, right, left, i))
        if phase == 2:
            feat_part(range(4))
        if phase == 1:
            feat_part(range(6, 8))
        more = []
        for cls in range(3):
            cp, a, b, d, e, up, down, right, left, i = legs[cls]

            def cp(k, src, dst, device):
                r = remote(src, dst, ss.at[cls, phase, k], rs.at[cls, phase, k], device)
                r.start()
                sent.append(r)
                return r

            a.wait_recv()
            add(half(up, phase, 0), ra.at[cls])
            f = cp(4, half(up, phase, 0), half(rc.at[cls], phase, 0), right)
            b.wait_recv()
            add(half(down, phase, 1), rb.at[cls])
            g = cp(5, half(down, phase, 1), half(rd.at[cls], phase, 1), left)
            more.append((f, g))
        if phase == 2:
            t1 = tap_sum(0, tcp, 2)
            tl[1, pos["x"]] = t1
            tcp = tap_send(1, [shifted(pos, "x", d) for d in (1, 2, 3)], pos["x"])
            feat_part(range(4, 6))
        if phase == 1:
            t1 = tap_sum(1, tcp, 4)
            tl[2, pos["y"]] = t1
            tcp = tap_send(2, [shifted(pos, "y", d) for d in (1, 2, 3)], pos["y"])
        if phase == 0:
            t1 = tap_sum(2, tcp, 4)
            tl[3, pos["z"]] = t1
            tcp = tap_send(3, [shifted(pos, "z", d) for d in (1, 2, 3)], pos["z"])
        for cls in range(3):
            _, a, b, d, e, up, down, right, left, i = legs[cls]
            f, g = more[cls]
            for k in (d, e, f, g):
                k.wait_recv()
            mine = unit(cls, phase, i)
            total = mine[...].astype(F32) + rc[cls].astype(F32) + rd[cls].astype(F32)
            if phase == 0:
                blk[cls * 16 : (cls + 1) * 16, :] = total
            else:
                mine[...] = total.astype(BF)

    for q in range(8):
        stage[q, 0:6, :] = blk[q * 6 : (q + 1) * 6, :]
        stage[q, 6:8, :] = jnp.zeros((2, 512), F32)
    last = []
    for i in range(1, 8):
        q = lax.rem(w + i, 8)
        r = remote(stage.at[q], land.at[w], s0.at[i], r0.at[i], (n, q))
        r.start()
        last.append(r)
    land[w] = stage[w]
    tout_ref[...] = tap_sum(3, tcp, 4)
    for r in last:
        r.wait_recv()
    for q in range(8):
        grad_ref[:, q * 512 : (q + 1) * 512] = land[q, 0:6, :]
    for r in sent + last:
        r.wait_send()


def reduce_grads(pd, features, fo, g, taps):
    sem = pltpu.SemaphoreType.DMA
    return pl.pallas_call(
        reduce_kernel,
        out_shape=(
            jax.ShapeDtypeStruct((6, 4096), F32),
            jax.ShapeDtypeStruct((4096, 128), BF),
            jax.ShapeDtypeStruct((8, 768), F32),
        ),
        in_specs=[VM] * 5,
        out_specs=(VM,) * 3,
        scratch_shapes=[
            pltpu.VMEM((768, 128), BF),
            pltpu.VMEM((384, 256), BF),
            pltpu.VMEM((3, 4, 4, 4, 16, 512), BF),
            pltpu.VMEM((3, 2, 4, 16, 512), BF), pltpu.VMEM((3, 2, 4, 16, 512), BF),
            pltpu.VMEM((3, 4, 4, 16, 512), BF), pltpu.VMEM((3, 4, 4, 16, 512), BF),
            pltpu.VMEM((3, 2, 16, 512), BF), pltpu.VMEM((3, 2, 16, 512), BF),
            pltpu.VMEM((3, 4, 16, 512), BF), pltpu.VMEM((3, 4, 16, 512), BF),
            pltpu.VMEM((3, 16, 256), BF), pltpu.VMEM((3, 16, 256), BF),
            pltpu.VMEM((3, 16, 512), BF), pltpu.VMEM((3, 16, 512), BF),
            pltpu.VMEM((48, 512), F32),
            pltpu.VMEM((8, 8, 512), F32),
            pltpu.VMEM((8, 8, 512), F32),
            pltpu.VMEM((4, 4, 8, 768), F32),
            sem, sem,
            sem((3, 3, 6)), sem((3, 3, 6)),
            sem((8,)), sem((8,)),
            sem((4, 3)), sem((4, 3)),
        ],
        compiler_params=pltpu.CompilerParams(
            collective_id=2, has_side_effects=True, vmem_limit_bytes=56 * 1024 * 1024
        ),
        name="reduce_grads",
    )(pd, features, fo, g, taps)

def lanes(rows):
    return lax.broadcasted_iota(jnp.int32, (rows, 128), 1)


def toeplitz_conv(h_ref, ch, rhs):
    width = rhs.shape[1]
    groups = width // 128
    lane = lanes(128)
    row = lax.broadcasted_iota(jnp.int32, (128, 128), 0)
    upper = lane >= row

    def rolled(k):
        taps = jnp.broadcast_to(h_ref[ch, pl.ds(k, 1), :], (128, 128))
        return pltpu.roll(taps, 0, 1, stride=1, stride_axis=0)

    def step(i, carry):
        acc, top = carry
        m = 63 - i
        mid = rolled(2 * m)
        low = jnp.where(m > 0, rolled(jnp.maximum(2 * m - 1, 0)), 0.0)
        odd = jnp.where(upper, top, mid).astype(BF)
        even = jnp.where(upper, mid, low).astype(BF)
        lhs = jnp.concatenate([even, odd], axis=1)
        term = jnp.dot(lhs, rhs, preferred_element_type=F32)
        parts = []
        for g in range(groups):
            part = pltpu.roll(acc[:, g * 128 : (g + 1) * 128], 2, 1)
            parts.append(jnp.where(lane < 2, 0.0, part) + term[:, g * 128 : (g + 1) * 128])
        return jnp.concatenate(parts, axis=1) if groups > 1 else parts[0], low

    acc, _ = lax.fori_loop(0, 64, step, (jnp.zeros((128, width), F32), rolled(127)))
    return acc


def stacked(x):
    later = jnp.where(lanes(128) < 1, 0.0, pltpu.roll(x, 1, 1))
    return jnp.concatenate([x.astype(BF), later.astype(BF)], axis=0)


def middle_kernel(
    p_ref, halo_ref, taps_ref, og_ref, lf_ref,
    mixed_ref, fgout_ref, pd_ref, tp_ref,
    send, land, send2, land2, ogn, hf, gf, feat, featn,
    ss, rs, ss2, rs2, os, orr,
):
    n, w, pos = position()
    s = n * 8 + w
    barrier = pltpu.get_barrier_semaphore()

    @pl.loop(1, 128)
    def _(i):
        pl.semaphore_signal(
            barrier, inc=1, device_id=shard_id(lax.rem(s + i, 128)), device_id_type=MESH
        )

    lane = lanes(256)
    for part in range(3):
        at = slice(part * 256, (part + 1) * 256)
        p = p_ref[at, :]
        halo = halo_ref[at, :]
        t0, t1, t2 = taps_ref[at, 0:1], taps_ref[at, 1:2], taps_ref[at, 2:3]
        p1 = jnp.where(lane < 1, pltpu.roll(halo, 127, 1), pltpu.roll(p, 1, 1))
        p2 = jnp.where(lane < 2, halo, pltpu.roll(p, 2, 1))
        feat[part] = t0 * p + t1 * p1 + t2 * p2
        n1 = jnp.where(lane < 1, pltpu.roll(p, 1, 1), pltpu.roll(halo, 127, 1))
        featn[part] = t0 * pltpu.roll(halo, 126, 1) + t1 * n1 + t2 * pltpu.roll(p, 2, 1)
    og = og_ref[...].astype(F32)
    gated = (feat[1] * feat[2]).astype(BF).astype(F32)
    cot = (og * feat[0]).astype(BF).astype(F32)
    lf = lf_ref[...].astype(F32)
    for r in range(2):
        at = slice(r * 128, (r + 1) * 128)
        send[pl.ds(r, 128, stride=8), :] = gated[at]
        send[pl.ds(2 + r, 128, stride=8), :] = cot[at]
        send[pl.ds(4 + r, 128, stride=8), :] = lf[at]
        send[pl.ds(6 + r, 128, stride=8), :] = jnp.zeros((128, 128), F32)
    pl.semaphore_wait(barrier, 127)

    def tile(i):
        return pl.ds(pl.multiple_of(i * 8, 8), 8)

    def exchange(src, dst, a, b):
        @pl.loop(1, 128)
        def _(i):
            t = lax.rem(s + i, 128)
            remote(src.at[tile(t)], dst.at[tile(s)], a, b, shard_id(t)).start()

        dst[tile(s), :] = src[tile(s), :]
        whole = pl.ds(0, 127 * 8)
        return remote(src.at[whole], dst.at[whole], a, b, (n, w))

    go = exchange(send, land, ss, rs)
    ocp = remote(og_ref, ogn, os, orr, shard_id(lax.rem(s + 127, 128)))
    ocp.start()
    go.wait_recv()

    anti = one_hot(128, 128, lambda r, l: r + l == 127)
    dims = lambda a, b: (((a,), (b,)), ((), ()))
    row = lax.broadcasted_iota(jnp.int32, (128, 128), 0)
    lane1 = lanes(128)
    ahead = jnp.zeros((128, 128), F32)
    for ch in range(2):
        gate_in = land[pl.ds(ch, 128, stride=8), :]
        cot_in = land[pl.ds(2 + ch, 128, stride=8), :].astype(BF)
        hf[ch] = land[pl.ds(4 + ch, 128, stride=8), :]
        gf[ch] = gate_in
        xg = lax.dot_general(anti, gate_in.astype(BF), dims(1, 1), preferred_element_type=F32)
        xc = lax.dot_general(cot_in, anti, dims(0, 0), preferred_element_type=F32)
        xc2 = stacked(xc)
        out = toeplitz_conv(hf, ch, jnp.concatenate([stacked(xg), xc2], axis=1)).astype(BF)
        conv = lax.dot_general(out[:, 0:128], anti, dims(0, 0), preferred_element_type=F32)
        gg = lax.dot_general(anti, out[:, 128:256], dims(1, 1), preferred_element_type=F32)
        fg = toeplitz_conv(gf, ch, xc2).astype(BF)
        fg = lax.dot_general(anti, fg, dims(1, 1), preferred_element_type=F32)
        send2[pl.ds(ch, 128, stride=8), :] = conv
        send2[pl.ds(2 + ch, 128, stride=8), :] = gg
        send2[pl.ds(5 + ch, 128, stride=8), :] = fg
        for k, value in ((ch, conv), (2 + ch, gg)):
            nxt = jnp.where(row < 127, pltpu.roll(value, 127, 0), 0.0)
            moved = pltpu.roll(nxt, 2 * k, 1) if k else nxt
            ahead = jnp.where((lane1 >= 2 * k) & (lane1 < 2 * k + 2), moved, ahead)
    send2[pl.ds(4, 128, stride=8), :] = ahead
    send2[pl.ds(7, 128, stride=8), :] = jnp.zeros((128, 128), F32)

    back = exchange(send2, land2, ss2, rs2)
    ocp.wait_recv()
    back.wait_recv()

    def channels(r):
        return jnp.concatenate(
            [land2[pl.ds(r, 128, stride=8), :], land2[pl.ds(r + 1, 128, stride=8), :]], axis=0
        )

    conv, gg = channels(0), channels(2)
    fgout_ref[...] = channels(5).astype(BF)
    ahead = land2[pl.ds(4, 128, stride=8), :]
    convn = jnp.concatenate([ahead, pltpu.roll(ahead, 126, 1)], axis=0)
    ggn = jnp.concatenate([pltpu.roll(ahead, 124, 1), pltpu.roll(ahead, 122, 1)], axis=0)
    mixed_ref[...] = (feat[0] * conv).astype(BF)
    ogv = ogn[...].astype(F32)
    last = s == 127
    sums = []
    for part in range(3):
        at = slice(part * 256, (part + 1) * 256)
        if part == 0:
            fd, fdn = og * conv, ogv * convn
        else:
            fd, fdn = gg * feat[3 - part], ggn * featn[3 - part]
        fdn = jnp.where(last, 0.0, fdn)
        t0, t1, t2 = taps_ref[at, 0:1], taps_ref[at, 1:2], taps_ref[at, 2:3]
        f1 = jnp.where(lane < 127, pltpu.roll(fd, 127, 1), pltpu.roll(fdn, 127, 1))
        f2 = jnp.where(lane < 126, pltpu.roll(fd, 126, 1), pltpu.roll(fdn, 126, 1))
        pd_ref[at, :] = (t0 * fd + t1 * f1 + t2 * f2).astype(BF)
        p = p_ref[at, :]
        halo = halo_ref[at, :]
        p1 = jnp.where(lane < 1, pltpu.roll(halo, 127, 1), pltpu.roll(p, 1, 1))
        p2 = jnp.where(lane < 2, halo, pltpu.roll(p, 2, 1))
        total = jnp.zeros((256, 128), F32)
        for k, q in enumerate((p, p1, p2)):
            total = jnp.where(lane == k, jnp.sum(fd * q, axis=1, keepdims=True), total)
        sums.append(total)
    for part in range(3):
        tp_ref[:, part * 256 : (part + 1) * 256] = sums[part].T[0:8, :]
    go.wait_send()
    back.wait_send()
    ocp.wait_send()


def middle(projected, halo, taps, out_grad, long_filter):
    sem = pltpu.SemaphoreType.DMA
    return pl.pallas_call(
        middle_kernel,
        out_shape=(
            jax.ShapeDtypeStruct((256, 128), BF),
            jax.ShapeDtypeStruct((256, 128), BF),
            jax.ShapeDtypeStruct((768, 128), BF),
            jax.ShapeDtypeStruct((8, 768), F32),
        ),
        in_specs=[VM] * 5,
        out_specs=(VM,) * 4,
        scratch_shapes=[
            pltpu.VMEM((1024, 128), F32), pltpu.VMEM((1024, 128), F32),
            pltpu.VMEM((1024, 128), F32), pltpu.VMEM((1024, 128), F32),
            pltpu.VMEM((256, 128), BF),
            pltpu.VMEM((2, 128, 128), F32), pltpu.VMEM((2, 128, 128), F32),
            pltpu.VMEM((3, 256, 128), F32), pltpu.VMEM((3, 256, 128), F32),
            sem, sem, sem, sem, sem, sem,
        ],
        compiler_params=pltpu.CompilerParams(
            collective_id=3, has_side_effects=True, vmem_limit_bytes=32 * 1024 * 1024
        ),
        name="middle",
    )(projected, halo, taps, out_grad, long_filter)


def local(features, in_proj, short_taps, long_filter, out_grad):
    projected, halo, g, fo = gather_project(in_proj, features)
    mixed, filter_grad, pd, tp = middle(projected, halo, short_taps.T, out_grad, long_filter)
    proj_grad, feat_grad, taps_grad = reduce_grads(pd, features, fo, g, tp)
    return mixed, feat_grad, filter_grad, taps_grad[0:3], proj_grad


def solution(mesh):
    tokens = P(None, AXES)
    rows = P(AXES, None)
    return jax.shard_map(
        local,
        mesh=mesh,
        in_specs=(tokens, rows, P(), tokens, tokens),
        out_specs=(tokens, tokens, tokens, P(), rows),
        check_vma=False,
    )
```

```python
import math

import jax
import jax.numpy as jnp
from jax import lax
from jax.experimental import pallas as pl
from jax.experimental.pallas import tpu as pltpu
from jax.sharding import PartitionSpec as P

MESH = pl.DeviceIdType.MESH
BF = jnp.bfloat16
F32 = jnp.float32
ORDERS = (("x", "y", "z"), ("y", "z", "x"), ("z", "x", "y"))
AXES = ("narrow", "wide")


def place(pos):
    y = pos["y"]
    return (pos["z"] * 4 + lax.rem(y, 2) * 2 + pos["c"], (y // 2) * 4 + pos["x"])


def position():
    n = lax.axis_index("narrow")
    w = lax.axis_index("wide")
    pos = {
        "x": lax.rem(w, 4),
        "y": (w // 4) * 2 + lax.rem(n // 2, 2),
        "z": n // 4,
        "c": lax.rem(n, 2),
    }
    return n, w, pos


def shifted(pos, axis, by):
    other = dict(pos)
    other[axis] = lax.rem(pos[axis] + by + 4, 4)
    return place(other)


def other_core(pos):
    other = dict(pos)
    other["c"] = 1 - pos["c"]
    return place(other)


def shard_id(s):
    return (s // 8, lax.rem(s, 8))


def remote(src, dst, send, recv, device):
    return pltpu.make_async_remote_copy(
        src_ref=src, dst_ref=dst, send_sem=send, recv_sem=recv, device_id=device, device_id_type=MESH
    )


def greet(devices):
    barrier = pltpu.get_barrier_semaphore()
    for device in devices:
        pl.semaphore_signal(barrier, inc=1, device_id=device, device_id_type=MESH)
    pl.semaphore_wait(barrier, len(devices))


def piece_index(cls, z, yh, yl, x):
    at = {"x": x, "y": yh * 2 + yl, "z": z}
    d0, d1, d2 = ORDERS[cls]
    return (at[d2], at[d1], at[d0])


def dims(a, b):
    return (((a,), (b,)), ((), ()))


def lanes(rows):
    return lax.broadcasted_iota(jnp.int32, (rows, 128), 1)


def one_hot(rows, cols, test):
    r = lax.broadcasted_iota(jnp.int32, (rows, cols), 0)
    c = lax.broadcasted_iota(jnp.int32, (rows, cols), 1)
    return jnp.where(test(r, c), 1.0, 0.0).astype(BF)


def wide_block(g_ref, cls, yh, x):
    parts = []
    for z in range(4):
        for yl in range(2):
            for core in range(2):
                i2, i1, i0 = piece_index(cls, z, yh, yl, x)
                parts.append(g_ref[cls, core, i2, i1, i0])
    return jnp.concatenate(parts, axis=0)


def half(ref, phase, k):
    if phase == 0:
        return ref.at[:, pl.ds(k * 256, 256)]
    return ref.at[pl.ds(k * 2, 2)]


def build_toeplitz(tt, h_ref, ch):
    lane = lanes(128)
    row = lax.broadcasted_iota(jnp.int32, (128, 128), 0)
    upper = lane >= row

    def rolled(k):
        taps = jnp.broadcast_to(h_ref[ch, pl.ds(k, 1), :], (128, 128))
        return pltpu.roll(taps, 0, 1, stride=1, stride_axis=0)

    @pl.loop(0, 8)
    def _(g):
        prev = jnp.where(g > 0, rolled(jnp.maximum(16 * g - 1, 0)), 0.0)
        at = pl.ds(pl.multiple_of(g * 128, 128), 128)
        for i in range(16):
            cur = rolled(16 * g + i)
            tt[at, i * 128 : (i + 1) * 128] = jnp.where(upper, cur, prev).astype(BF)
            prev = cur


def spread_blocks(xs, col, x):
    lane = lanes(128)
    for i in range(16):
        moved = pltpu.roll(x, i, 1) if i else x
        xs[i * 128 : (i + 1) * 128, col * 128 : (col + 1) * 128] = jnp.where(lane < i, 0.0, moved).astype(BF)


def toeplitz_product(tt, xs, cols):
    lane = lanes(128)
    out = jnp.dot(tt[...], xs[:, 0 : cols * 128], preferred_element_type=F32)
    results = []
    for c in range(cols):
        at = slice(c * 128, (c + 1) * 128)
        acc = out[896:1024, at]
        for g in range(6, -1, -1):
            acc = jnp.where(lane < 16, 0.0, pltpu.roll(acc, 16, 1)) + out[g * 128 : (g + 1) * 128, at]
        results.append(acc.astype(BF))
    return results


def hyena_kernel(
    proj_hbm, feat_hbm, taps_hbm, og_hbm, lf_hbm,
    mixed_ref, fgrad_ref, fgout_ref, tout_ref, grad_ref,
    proj_ref, feat_ref, taps_ref, og_ref, lf_ref,
    stage, land, blk, rows, hland, fh, g_ref, fo_ref, p_ref, halo_ref, tcol,
    rowbuf, send_f, land_f, send_a, land_a, send_b, land_b, send_c, land_c,
    ogn, hf, gf, feat, featn, tt0, tt1, xs, xc, pd_ref,
    pdo, pdc, p, ra3, rb3, rc3, rd3, ra2, rb2, rc2, rd2, ra1, rb1, rc1, rd1,
    stage2, land2, tl,
    ins, s0, r0, ss, rs, ds, dr, hs, hr, fs, fr, xsend, xrecv, os, orr,
    ps, pr, ss2, rs2, s02, r02, tsn, trc, near,
):
    n, w, pos = position()
    c = pos["c"]
    s = n * 8 + w
    right_shard = shard_id(lax.rem(s + 1, 128))
    left_shard = shard_id(lax.rem(s + 127, 128))
    wide_peers = [(n, lax.rem(w + i, 8)) for i in range(1, 8)]
    line = {a: [shifted(pos, a, d) for d in (1, 2, 3)] for a in "xyz"}
    core = other_core(pos)
    copies = [
        pltpu.make_async_copy(a, b, ins.at[k])
        for k, (a, b) in enumerate(
            ((proj_hbm, proj_ref), (feat_hbm, feat_ref), (taps_hbm, taps_ref), (og_hbm, og_ref), (lf_hbm, lf_ref))
        )
    ]
    for cp in copies:
        cp.start()
    barrier = pltpu.get_barrier_semaphore()
    greeted = wide_peers + line["y"] + line["z"] + [core, right_shard, left_shard]
    for device in greeted:
        pl.semaphore_signal(barrier, inc=1, device_id=device, device_id_type=MESH)
    copies[0].wait()
    for q in range(8):
        stage[q, 0:6, :] = proj_ref[:, q * 512 : (q + 1) * 512].astype(F32)
        stage[q, 6:8, :] = jnp.zeros((2, 512), F32)
    pl.semaphore_wait(barrier, len(greeted))

    def tell(k, devices):
        for device in devices:
            pl.semaphore_signal(near.at[k], inc=1, device_id=device, device_id_type=MESH)

    started = []

    def push(src, dst, a, b, device):
        cp = remote(src, dst, a, b, device)
        cp.start()
        started.append(cp)
        return cp

    first = []
    for i in range(1, 8):
        q = lax.rem(w + i, 8)
        first.append(push(stage.at[q], land.at[w], s0.at[i], r0.at[i], (n, q)))
    tell(0, line["x"])
    land[w] = stage[w]
    for cp in first:
        cp.wait_recv()
    for q in range(8):
        blk[q * 6 : (q + 1) * 6, :] = land[q, 0:6, :]

    index = [[pos[a] for a in reversed(order)] for order in ORDERS]
    for cls in range(3):
        i2, i1, i0 = index[cls]
        g_ref[cls, c, i2, i1, i0] = blk[cls * 16 : (cls + 1) * 16, :].astype(BF)

    def unit(ref, cls, phase, j):
        i2, i1, _ = index[cls]
        if phase == 0:
            return ref.at[i2, i1, j]
        if phase == 1:
            return ref.at[i2, j]
        return ref.at[j]

    d2d = []

    def cross(cls, j, k):
        ref = g_ref.at[cls, c, j]
        d2d.append(push(ref, ref, ds.at[cls, k], dr.at[cls, k], core))

    def exchange(src, dst, k):
        ww = [lax.rem(w + j, 8) for j in range(8)]
        for j in range(1, 8):
            remote(src.at[n * 8 + ww[j]], dst.at[s], xsend.at[k], xrecv.at[k], (n, ww[j])).start()

        @pl.loop(1, 16)
        def _(i):
            nn = lax.rem(n + i, 16)
            for j in range(8):
                remote(src.at[nn * 8 + ww[j]], dst.at[s], xsend.at[k], xrecv.at[k], (nn, ww[j])).start()

        dst[s] = src[s]
        whole = pl.ds(0, 127)
        cp = remote(src.at[whole], dst.at[whole], xsend.at[k], xrecv.at[k], (n, w))
        started.append(cp)
        return cp

    def pack(buf, parts):
        for r, value in parts.items():
            rowbuf[pl.ds(r, 128, stride=8), :] = value
        buf[...] = rowbuf[...].reshape(128, 8, 128).astype(BF)

    def unpack(buf):
        rowbuf[...] = buf[...].astype(F32).reshape(1024, 128)

    def plane(r):
        return rowbuf[pl.ds(r, 128, stride=8), :]

    fcp = lfx = None
    for phase in range(3):
        legs = []
        for cls in range(3):
            axis = ORDERS[cls][phase]
            i = pos[axis]
            right, left = shifted(pos, axis, 1), shifted(pos, axis, -1)
            mine = unit(g_ref.at[cls, c], cls, phase, i)
            a = push(mine, mine, ss.at[cls, phase, 0], rs.at[cls, phase, 0], right)
            b = push(mine, mine, ss.at[cls, phase, 1], rs.at[cls, phase, 1], left)
            legs.append((a, b, right, left, i))
            if phase == 2:
                cross(cls, i, 0)
        if phase == 0:
            copies[1].wait()
            sel = one_hot(
                16, 128, lambda r, l: ((r < 2) & (l == r + 126)) | ((r >= 2) & (r < 4) & (l == r - 2))
            )
            rows[...] = lax.dot_general(
                sel, feat_ref[...], dims(1, 1), preferred_element_type=F32
            ).astype(BF)
            ha = push(rows, hland.at[0], hs.at[0], hr.at[0], right_shard)
            hb = push(rows, hland.at[1], hs.at[1], hr.at[1], left_shard)
            fcp = push(feat_ref, fo_ref, fs, fr, core)
            pl.semaphore_wait(near.at[0], 3)
            tell(1, line["y"])
        if phase == 1:
            fh[:, 0:128] = feat_ref[...]
            pl.semaphore_wait(near.at[1], 3)
            tell(2, [core])
            for k in range(2, 5):
                copies[k].wait()
            lf = lf_ref[...].astype(F32)
            zero = jnp.zeros((128, 128), F32)
            pack(send_f, {0: lf[0:128], 1: lf[128:256], **{r: zero for r in range(2, 8)}})
            ocp = push(og_ref, ogn, os, orr, left_shard)
            tc = jnp.concatenate([taps_ref[...], jnp.zeros((125, 768), F32)], axis=0)
            for k in range(6):
                tcol[k * 128 : (k + 1) * 128, :] = tc[:, k * 128 : (k + 1) * 128].T
        if phase == 2:
            pl.semaphore_wait(near.at[2], 1)
            lfx = exchange(send_f, land_f, 0)
            ha.wait_recv()
            hb.wait_recv()
            row = lax.broadcasted_iota(jnp.int32, (16, 4096), 0)
            both = jnp.where(row < 2, hland[0].astype(F32), hland[1].astype(F32)).astype(BF)
            lo = jnp.where(s > 0, 0, 2)
            hi = jnp.where(s < 127, 4, 2)
            spread = one_hot(16, 128, lambda r, l: (r == l) & (r >= lo) & (r < hi))
            fh[:, 128:256] = lax.dot_general(
                both, spread, dims(0, 0), preferred_element_type=F32
            ).astype(BF)
        second = []
        for cls in range(3):
            a, b, right, left, i = legs[cls]
            a.wait_recv()
            got = half(unit(g_ref.at[cls, c], cls, phase, lax.rem(i + 3, 4)), phase, 0)
            e = push(got, got, ss.at[cls, phase, 2], rs.at[cls, phase, 2], right)
            b.wait_recv()
            got = half(unit(g_ref.at[cls, c], cls, phase, lax.rem(i + 1, 4)), phase, 1)
            f = push(got, got, ss.at[cls, phase, 3], rs.at[cls, phase, 3], left)
            second.append((e, f))
            if phase == 2:
                cross(cls, lax.rem(i + 3, 4), 1)
                cross(cls, lax.rem(i + 1, 4), 2)
        if phase == 2:
            lfx.wait_recv()
            unpack(land_f)
            for ch in range(2):
                hf[ch] = plane(ch)
            build_toeplitz(tt0, hf, 0)
            build_toeplitz(tt1, hf, 1)
        for cls in range(3):
            e, f = second[cls]
            e.wait_recv()
            f.wait_recv()
            if phase == 2:
                cross(cls, lax.rem(legs[cls][4] + 2, 4), 3)
    for cp in d2d:
        cp.wait_recv()

    for cls in range(3):
        acc = None
        for q in range(8):
            lhs = wide_block(g_ref, cls, q // 4, q % 4)
            term = jnp.dot(lhs, fh[q * 512 : (q + 1) * 512, :], preferred_element_type=F32)
            acc = term if acc is None else acc + term
        for m in range(16):
            at = slice(m * 48 + cls * 16, m * 48 + cls * 16 + 16)
            p_ref[at, :] = acc[m * 16 : (m + 1) * 16, 0:128]
            halo_ref[at, :] = acc[m * 16 : (m + 1) * 16, 128:256]

    lane = lanes(256)
    for part in range(3):
        at = slice(part * 256, (part + 1) * 256)
        v = p_ref[at, :]
        halo = halo_ref[at, :]
        t0, t1, t2 = tcol[at, 0:1], tcol[at, 1:2], tcol[at, 2:3]
        v1 = jnp.where(lane < 1, pltpu.roll(halo, 127, 1), pltpu.roll(v, 1, 1))
        v2 = jnp.where(lane < 2, halo, pltpu.roll(v, 2, 1))
        feat[part] = t0 * v + t1 * v1 + t2 * v2
        n1 = jnp.where(lane < 1, pltpu.roll(v, 1, 1), pltpu.roll(halo, 127, 1))
        featn[part] = t0 * pltpu.roll(halo, 126, 1) + t1 * n1 + t2 * pltpu.roll(v, 2, 1)
    og = og_ref[...].astype(F32)
    gated = feat[1] * feat[2]
    cot = og * feat[0]
    pack(send_a, {0: gated[0:128], 1: gated[128:256], 2: cot[0:128], 3: cot[128:256]})
    go = exchange(send_a, land_a, 1)
    go.wait_recv()
    unpack(land_a)

    anti = one_hot(128, 128, lambda r, l: r + l == 127)
    row = lax.broadcasted_iota(jnp.int32, (128, 128), 0)
    lane1 = lanes(128)
    ahead = jnp.zeros((128, 128), F32)
    cots = []
    for ch in range(2):
        gf[ch] = plane(ch)
        cots.append(plane(2 + ch).astype(BF))
    for ch in range(2):
        xg = lax.dot_general(anti, gf[ch].astype(BF), dims(1, 1), preferred_element_type=F32)
        back = lax.dot_general(cots[ch], anti, dims(0, 0), preferred_element_type=F32)
        spread_blocks(xs, 1, xg)
        spread_blocks(xs, 0, back)
        xc[ch] = xs[:, 0:128]
        yc, yg = toeplitz_product(tt0 if ch == 0 else tt1, xs, 2)
        conv = lax.dot_general(yg, anti, dims(0, 0), preferred_element_type=F32)
        gg = lax.dot_general(anti, yc, dims(1, 1), preferred_element_type=F32)
        rowbuf[pl.ds(ch, 128, stride=8), :] = conv
        rowbuf[pl.ds(2 + ch, 128, stride=8), :] = gg
        for k, value in ((ch, conv), (2 + ch, gg)):
            nxt = jnp.where(row < 127, pltpu.roll(value, 127, 0), 0.0)
            moved = pltpu.roll(nxt, 2 * k, 1) if k else nxt
            ahead = jnp.where((lane1 >= 2 * k) & (lane1 < 2 * k + 2), moved, ahead)
    pack(send_b, {4: ahead})
    ret = exchange(send_b, land_b, 2)
    build_toeplitz(tt0, gf, 0)
    build_toeplitz(tt1, gf, 1)
    ocp.wait_recv()
    ret.wait_recv()
    unpack(land_b)

    def channels(r):
        return jnp.concatenate([plane(r), plane(r + 1)], axis=0)

    conv, gg = channels(0), channels(2)
    ahead = plane(4)
    convn = jnp.concatenate([ahead, pltpu.roll(ahead, 126, 1)], axis=0)
    ggn = jnp.concatenate([pltpu.roll(ahead, 124, 1), pltpu.roll(ahead, 122, 1)], axis=0)
    mixed_ref[...] = (feat[0] * conv).astype(BF)
    ogv = ogn[...].astype(F32)
    last = s == 127

    def derivative(part):
        if part == 0:
            return og * conv
        return gg * feat[3 - part]

    for part in range(3):
        at = slice(part * 256, (part + 1) * 256)
        fd = derivative(part)
        fdn = ogv * convn if part == 0 else ggn * featn[3 - part]
        fdn = jnp.where(last, 0.0, fdn)
        t0, t1, t2 = tcol[at, 0:1], tcol[at, 1:2], tcol[at, 2:3]
        f1 = jnp.where(lane < 127, pltpu.roll(fd, 127, 1), pltpu.roll(fdn, 127, 1))
        f2 = jnp.where(lane < 126, pltpu.roll(fd, 126, 1), pltpu.roll(fdn, 126, 1))
        pd_ref[at, :] = (t0 * fd + t1 * f1 + t2 * f2).astype(BF)
    pcp = push(pd_ref, pdo, ps, pr, core)

    for part in range(3):
        at = slice(part * 256, (part + 1) * 256)
        fd = derivative(part)
        v = p_ref[at, :]
        halo = halo_ref[at, :]
        v1 = jnp.where(lane < 1, pltpu.roll(halo, 127, 1), pltpu.roll(v, 1, 1))
        v2 = jnp.where(lane < 2, halo, pltpu.roll(v, 2, 1))
        total = jnp.zeros((256, 128), F32)
        for k, q in enumerate((v, v1, v2)):
            total = jnp.where(lane == k, jnp.sum(fd * q, axis=1, keepdims=True), total)
        tl[0, c, :, at] = total.T[0:8, :]

    def tap_send(k, peers, slot):
        return [
            push(tl.at[k, slot], tl.at[k, slot], tsn.at[k, i], trc.at[k, i], device)
            for i, device in enumerate(peers)
        ]

    def tap_sum(k, cps, count):
        for cp in cps:
            cp.wait_recv()
        total = tl[k, 0]
        for i in range(1, count):
            total = total + tl[k, i]
        return total

    tcp = tap_send(0, [core], c)
    fcp.wait_recv()
    pcp.wait_recv()
    for cls in range(3):
        for z in range(4):
            for yl in range(2):
                at = pl.ds(pl.multiple_of((z * 4 + yl * 2 + c) * 48 + cls * 16, 16), 16)
                to = cls * 128 + z * 32 + yl * 16
                pdc[to : to + 16, 0:128] = pd_ref[at, :]
                pdc[to : to + 16, 128:256] = pdo[at, :]

    for yh in range(2):
        for x in range(4):
            cols = slice((yh * 4 + x) * 512, (yh * 4 + x + 1) * 512)
            rhs = jnp.concatenate([feat_ref[cols, :], fo_ref[cols, :]], axis=1)
            for cls in range(3):
                part = lax.dot_general(
                    pdc[cls * 128 : (cls + 1) * 128, :], rhs, dims(1, 1), preferred_element_type=F32
                ).astype(BF)
                for z in range(4):
                    for yl in range(2):
                        i2, i1, i0 = piece_index(cls, z, yh, yl, x)
                        k = z * 32 + yl * 16
                        p[cls, i2, i1, i0] = part[k : k + 16, :]

    bufs = {2: (ra3, rb3, rc3, rd3), 1: (ra2, rb2, rc2, rd2), 0: (ra1, rb1, rc1, rd1)}

    def add(dst, src):
        dst[...] = (dst[...].astype(F32) + src[...].astype(F32)).astype(BF)

    def feat_part(qs):
        for q in qs:
            total = None
            for cls in range(3):
                lhs = jnp.concatenate(
                    [pd_ref[m * 48 + cls * 16 : m * 48 + cls * 16 + 16, :] for m in range(16)], axis=0
                )
                term = lax.dot_general(
                    lhs, wide_block(g_ref, cls, q // 4, q % 4), dims(0, 0), preferred_element_type=F32
                )
                total = term if total is None else total + term
            fgrad_ref[q * 512 : (q + 1) * 512, :] = total.T.astype(BF)

    fgx = None
    for phase in (2, 1, 0):
        ra, rb, rc, rd = bufs[phase]
        legs = []
        for cls in range(3):
            axis = ORDERS[cls][phase]
            i = pos[axis]
            right, left = shifted(pos, axis, 1), shifted(pos, axis, -1)
            far, up, down = (unit(p.at[cls], cls, phase, lax.rem(i + d, 4)) for d in (2, 1, 3))
            sem = [(ss2.at[cls, phase, k], rs2.at[cls, phase, k]) for k in range(6)]
            a = push(half(far, phase, 0), ra.at[cls], *sem[0], right)
            b = push(half(far, phase, 1), rb.at[cls], *sem[1], left)
            d = push(half(up, phase, 1), half(rc.at[cls], phase, 1), *sem[2], right)
            e = push(half(down, phase, 0), half(rd.at[cls], phase, 0), *sem[3], left)
            legs.append((sem, a, b, d, e, up, down, right, left, i))
        if phase == 2:
            feat_part(range(2))
        if phase == 1:
            feat_part(range(5, 7))
        if phase == 0:
            feat_part(range(7, 8))
        more = []
        for cls in range(3):
            sem, a, b, d, e, up, down, right, left, i = legs[cls]
            a.wait_recv()
            add(half(up, phase, 0), ra.at[cls])
            f = push(half(up, phase, 0), half(rc.at[cls], phase, 0), *sem[4], right)
            b.wait_recv()
            add(half(down, phase, 1), rb.at[cls])
            g = push(half(down, phase, 1), half(rd.at[cls], phase, 1), *sem[5], left)
            more.append((f, g))
        if phase == 2:
            tl[1, pos["x"]] = tap_sum(0, tcp, 2)
            tcp = tap_send(1, line["x"], pos["x"])
            for ch in range(2):
                (y,) = toeplitz_product(tt0 if ch == 0 else tt1, xc.at[ch], 1)
                rowbuf[pl.ds(ch, 128, stride=8), :] = lax.dot_general(
                    anti, y, dims(1, 1), preferred_element_type=F32
                )
            pack(send_c, {})
            fgx = exchange(send_c, land_c, 3)
            feat_part(range(2, 5))
        if phase == 1:
            tl[2, pos["y"]] = tap_sum(1, tcp, 4)
            tcp = tap_send(2, line["y"], pos["y"])
        if phase == 0:
            tl[3, pos["z"]] = tap_sum(2, tcp, 4)
            tcp = tap_send(3, line["z"], pos["z"])
        for cls in range(3):
            sem, a, b, d, e, up, down, right, left, i = legs[cls]
            for k in (d, e) + more[cls]:
                k.wait_recv()
            mine = unit(p.at[cls], cls, phase, i)
            total = mine[...].astype(F32) + rc[cls].astype(F32) + rd[cls].astype(F32)
            if phase == 0:
                blk[cls * 16 : (cls + 1) * 16, :] = total
            else:
                mine[...] = total.astype(BF)

    for q in range(8):
        stage2[q, 0:6, :] = blk[q * 6 : (q + 1) * 6, :]
        stage2[q, 6:8, :] = jnp.zeros((2, 512), F32)
    final = []
    for i in range(1, 8):
        q = lax.rem(w + i, 8)
        final.append(push(stage2.at[q], land2.at[w], s02.at[i], r02.at[i], (n, q)))
    land2[w] = stage2[w]
    tout_ref[...] = tap_sum(3, tcp, 4)[0:3]
    fgx.wait_recv()
    unpack(land_c)
    fgout_ref[...] = channels(0).astype(BF)
    for cp in final:
        cp.wait_recv()
    for q in range(8):
        grad_ref[:, q * 512 : (q + 1) * 512] = land2[q, 0:6, :]
    for cp in started:
        cp.wait_send()


VM = pl.BlockSpec(memory_space=pltpu.VMEM)
ANY = pl.BlockSpec(memory_space=pl.ANY)


def hyena(in_proj, features, taps, out_grad, long_filter):
    sem = pltpu.SemaphoreType.DMA
    vm = pltpu.VMEM
    tile = (128, 8, 128)
    return pl.pallas_call(
        hyena_kernel,
        out_shape=(
            jax.ShapeDtypeStruct((256, 128), BF),
            jax.ShapeDtypeStruct((4096, 128), BF),
            jax.ShapeDtypeStruct((256, 128), BF),
            jax.ShapeDtypeStruct((3, 768), F32),
            jax.ShapeDtypeStruct((6, 4096), F32),
        ),
        in_specs=[ANY] * 5,
        out_specs=(VM,) * 5,
        scratch_shapes=[
            vm((6, 4096), BF), vm((4096, 128), BF), vm((3, 768), F32), vm((256, 128), BF), vm((256, 128), BF),
            vm((8, 8, 512), F32), vm((8, 8, 512), F32), vm((48, 512), F32),
            vm((16, 4096), BF), vm((2, 16, 4096), BF), vm((4096, 256), BF),
            vm((3, 2, 4, 4, 4, 16, 512), BF), vm((4096, 128), BF),
            vm((768, 128), F32), vm((768, 128), F32), vm((768, 128), F32),
            vm((1024, 128), F32),
        ]
        + [vm(tile, BF)] * 8
        + [
            vm((256, 128), BF), vm((2, 128, 128), F32), vm((2, 128, 128), F32),
            vm((3, 256, 128), F32), vm((3, 256, 128), F32),
            vm((1024, 2048), BF), vm((1024, 2048), BF), vm((2048, 256), BF), vm((2, 2048, 128), BF),
            vm((768, 128), BF),
            vm((768, 128), BF), vm((384, 256), BF), vm((3, 4, 4, 4, 16, 512), BF),
            vm((3, 2, 4, 16, 512), BF), vm((3, 2, 4, 16, 512), BF),
            vm((3, 4, 4, 16, 512), BF), vm((3, 4, 4, 16, 512), BF),
            vm((3, 2, 16, 512), BF), vm((3, 2, 16, 512), BF),
            vm((3, 4, 16, 512), BF), vm((3, 4, 16, 512), BF),
            vm((3, 16, 256), BF), vm((3, 16, 256), BF),
            vm((3, 16, 512), BF), vm((3, 16, 512), BF),
            vm((8, 8, 512), F32), vm((8, 8, 512), F32), vm((4, 4, 8, 768), F32),
            sem((5,)), sem((8,)), sem((8,)),
            sem((3, 3, 4)), sem((3, 3, 4)), sem((3, 4)), sem((3, 4)),
            sem((2,)), sem((2,)), sem, sem, sem((4,)), sem((4,)), sem, sem,
            sem, sem, sem((3, 3, 6)), sem((3, 3, 6)), sem((8,)), sem((8,)), sem((4, 3)), sem((4, 3)),
            pltpu.SemaphoreType.REGULAR((3,)),
        ],
        compiler_params=pltpu.CompilerParams(
            collective_id=1, has_side_effects=True, vmem_limit_bytes=58 * 1024 * 1024
        ),
        name="hyena",
    )(in_proj, features, taps, out_grad, long_filter)


def local(features, in_proj, short_taps, long_filter, out_grad):
    return hyena(in_proj, features, short_taps, out_grad, long_filter)


def solution(mesh):
    tokens = P(None, AXES)
    rows = P(AXES, None)
    return jax.shard_map(
        local,
        mesh=mesh,
        in_specs=(tokens, rows, P(), tokens, tokens),
        out_specs=(tokens, tokens, tokens, P(), rows),
        check_vma=False,
    )
```

```python
import math

import jax
import jax.numpy as jnp
from jax import lax
from jax.experimental import pallas as pl
from jax.experimental.pallas import tpu as pltpu
from jax.sharding import PartitionSpec as P

MESH = pl.DeviceIdType.MESH
BF = jnp.bfloat16
F32 = jnp.float32
ORDERS = (("x", "y", "z"), ("y", "z", "x"), ("z", "x", "y"))
AXES = ("narrow", "wide")


def place(pos):
    y = pos["y"]
    return (pos["z"] * 4 + lax.rem(y, 2) * 2 + pos["c"], (y // 2) * 4 + pos["x"])


def position():
    n = lax.axis_index("narrow")
    w = lax.axis_index("wide")
    pos = {
        "x": lax.rem(w, 4),
        "y": (w // 4) * 2 + lax.rem(n // 2, 2),
        "z": n // 4,
        "c": lax.rem(n, 2),
    }
    return n, w, pos


def shifted(pos, axis, by):
    other = dict(pos)
    other[axis] = lax.rem(pos[axis] + by + 4, 4)
    return place(other)


def other_core(pos):
    other = dict(pos)
    other["c"] = 1 - pos["c"]
    return place(other)


def shard_id(s):
    return (s // 8, lax.rem(s, 8))


def remote(src, dst, send, recv, device):
    return pltpu.make_async_remote_copy(
        src_ref=src, dst_ref=dst, send_sem=send, recv_sem=recv, device_id=device, device_id_type=MESH
    )


def greet(devices):
    barrier = pltpu.get_barrier_semaphore()
    for device in devices:
        pl.semaphore_signal(barrier, inc=1, device_id=device, device_id_type=MESH)
    pl.semaphore_wait(barrier, len(devices))


def piece_index(cls, z, yh, yl, x):
    at = {"x": x, "y": yh * 2 + yl, "z": z}
    d0, d1, d2 = ORDERS[cls]
    return (at[d2], at[d1], at[d0])


def dims(a, b):
    return (((a,), (b,)), ((), ()))


def lanes(rows):
    return lax.broadcasted_iota(jnp.int32, (rows, 128), 1)


def one_hot(rows, cols, test):
    r = lax.broadcasted_iota(jnp.int32, (rows, cols), 0)
    c = lax.broadcasted_iota(jnp.int32, (rows, cols), 1)
    return jnp.where(test(r, c), 1.0, 0.0).astype(BF)


def wide_block(g_ref, cls, yh, x):
    parts = []
    for z in range(4):
        for yl in range(2):
            for core in range(2):
                i2, i1, i0 = piece_index(cls, z, yh, yl, x)
                parts.append(g_ref[cls, core, i2, i1, i0])
    return jnp.concatenate(parts, axis=0)


def half(ref, phase, k):
    if phase == 0:
        return ref.at[:, pl.ds(k * 256, 256)]
    return ref.at[pl.ds(k * 2, 2)]


def build_toeplitz(tt, h_ref, ch):
    lane = lanes(128)
    row = lax.broadcasted_iota(jnp.int32, (128, 128), 0)
    upper = lane >= row

    def rolled(k):
        taps = jnp.broadcast_to(h_ref[ch, pl.ds(k, 1), :], (128, 128))
        return pltpu.roll(taps, 0, 1, stride=1, stride_axis=0)

    @pl.loop(0, 8)
    def _(g):
        prev = jnp.where(g > 0, rolled(jnp.maximum(16 * g - 1, 0)), 0.0)
        at = pl.ds(pl.multiple_of(g * 128, 128), 128)
        for i in range(16):
            cur = rolled(16 * g + i)
            tt[at, i * 128 : (i + 1) * 128] = jnp.where(upper, cur, prev).astype(BF)
            prev = cur


def spread_blocks(xs, col, x):
    lane = lanes(128)
    for i in range(16):
        moved = pltpu.roll(x, i, 1) if i else x
        xs[i * 128 : (i + 1) * 128, col * 128 : (col + 1) * 128] = jnp.where(lane < i, 0.0, moved).astype(BF)


def toeplitz_product(tt, xs, cols):
    lane = lanes(128)
    out = jnp.dot(tt[...], xs[:, 0 : cols * 128], preferred_element_type=F32)
    results = []
    for c in range(cols):
        at = slice(c * 128, (c + 1) * 128)
        acc = out[896:1024, at]
        for g in range(6, -1, -1):
            acc = jnp.where(lane < 16, 0.0, pltpu.roll(acc, 16, 1)) + out[g * 128 : (g + 1) * 128, at]
        results.append(acc.astype(BF))
    return results


def hyena_kernel(
    proj_hbm, feat_hbm, taps_hbm, og_hbm, lf_hbm,
    mixed_hbm, fgrad_hbm, fgout_hbm, tout_hbm, grad_hbm,
    mixed_ref, fgrad_ref, fgout_ref, tout_ref, grad_ref, outs,
    proj_ref, feat_ref, taps_ref, og_ref, lf_ref,
    stage, land, blk, rows, hland, fh, g_ref, fo_ref, p_ref, halo_ref, tcol,
    rowbuf, send_f, land_f, send_a, land_a, send_b, land_b, send_c, land_c,
    ogn, hf, gf, feat, featn, tt0, tt1, xs, xc, pd_ref,
    pdo, pdc, p, ra3, rb3, rc3, rd3, ra2, rb2, rc2, rd2, ra1, rb1, rc1, rd1,
    stage2, land2, tl, pdt,
    ins, s0, r0, ss, rs, ds, dr, hs, hr, fs, fr, xsend, xrecv, os, orr,
    ps, pr, ss2, rs2, s02, r02, tsn, trc, near,
):
    n, w, pos = position()
    c = pos["c"]
    s = n * 8 + w
    right_shard = shard_id(lax.rem(s + 1, 128))
    left_shard = shard_id(lax.rem(s + 127, 128))
    wide_peers = [(n, lax.rem(w + i, 8)) for i in range(1, 8)]
    line = {a: [shifted(pos, a, d) for d in (1, 2, 3)] for a in "xyz"}
    core = other_core(pos)
    copies = [
        pltpu.make_async_copy(a, b, ins.at[k])
        for k, (a, b) in enumerate(
            ((proj_hbm, proj_ref), (feat_hbm, feat_ref), (taps_hbm, taps_ref), (og_hbm, og_ref), (lf_hbm, lf_ref))
        )
    ]
    for cp in copies:
        cp.start()
    barrier = pltpu.get_barrier_semaphore()
    greeted = wide_peers + line["y"] + line["z"] + [core, right_shard, left_shard]
    for device in greeted:
        pl.semaphore_signal(barrier, inc=1, device_id=device, device_id_type=MESH)
    copies[0].wait()
    for q in range(8):
        stage[q, 0:6, :] = proj_ref[:, q * 512 : (q + 1) * 512].astype(F32)
        stage[q, 6:8, :] = jnp.zeros((2, 512), F32)
    pl.semaphore_wait(barrier, len(greeted))

    def tell(k, devices):
        for device in devices:
            pl.semaphore_signal(near.at[k], inc=1, device_id=device, device_id_type=MESH)

    started = []
    stores = []

    def store(k, src, dst):
        cp = pltpu.make_async_copy(src, dst, outs.at[k])
        cp.start()
        stores.append(cp)

    def push(src, dst, a, b, device):
        cp = remote(src, dst, a, b, device)
        cp.start()
        started.append(cp)
        return cp

    first = []
    for i in range(1, 8):
        q = lax.rem(w + i, 8)
        first.append(push(stage.at[q], land.at[w], s0.at[i], r0.at[i], (n, q)))
    tell(0, line["x"])
    land[w] = stage[w]
    for cp in first:
        cp.wait_recv()
    for q in range(8):
        blk[q * 6 : (q + 1) * 6, :] = land[q, 0:6, :]

    index = [[pos[a] for a in reversed(order)] for order in ORDERS]
    for cls in range(3):
        i2, i1, i0 = index[cls]
        g_ref[cls, c, i2, i1, i0] = blk[cls * 16 : (cls + 1) * 16, :].astype(BF)

    d2d = []

    def cross(cls, j, k):
        ref = g_ref.at[cls, c, j]
        d2d.append(push(ref, ref, ds.at[cls, k], dr.at[cls, k], core))

    def exchange(src, dst, k):
        ww = [lax.rem(w + j, 8) for j in range(8)]
        for j in range(1, 8):
            remote(src.at[n * 8 + ww[j]], dst.at[s], xsend.at[k], xrecv.at[k], (n, ww[j])).start()

        @pl.loop(1, 16)
        def _(i):
            nn = lax.rem(n + i, 16)
            for j in range(8):
                remote(src.at[nn * 8 + ww[j]], dst.at[s], xsend.at[k], xrecv.at[k], (nn, ww[j])).start()

        dst[s] = src[s]
        whole = pl.ds(0, 127)
        cp = remote(src.at[whole], dst.at[whole], xsend.at[k], xrecv.at[k], (n, w))
        started.append(cp)
        return cp

    def pack(buf, parts):
        for r, value in parts.items():
            rowbuf[pl.ds(r, 128, stride=8), :] = value
        buf[...] = rowbuf[...].reshape(128, 8, 128).astype(BF)

    def unpack(buf):
        rowbuf[...] = buf[...].astype(F32).reshape(1024, 128)

    def plane(r):
        return rowbuf[pl.ds(r, 128, stride=8), :]

    def piece(cls, i2, i1, i0):
        return g_ref.at[cls, c, i2, i1, i0]

    def row_of(cls, i2, i1):
        return g_ref.at[cls, c, i2, i1]

    def near_by(cls, phase):
        axis = ORDERS[cls][phase]
        return shifted(pos, axis, 1), shifted(pos, axis, -1)

    def ring(cls, phase, k, ref, device):
        return push(ref, ref, ss.at[cls, phase, k], rs.at[cls, phase, k], device)

    def off(i, d):
        return lax.rem(i + d, 4)

    legs = []
    for cls in range(3):
        i2, i1, i0 = index[cls]
        right, left = near_by(cls, 0)
        mine = piece(cls, i2, i1, i0)
        legs.append((ring(cls, 0, 0, mine, right), ring(cls, 0, 1, mine, left)))
    pl.semaphore_wait(near.at[0], 3)
    tell(1, line["y"])
    copies[1].wait()
    sel = one_hot(
        16, 128, lambda r, l: ((r < 2) & (l == r + 126)) | ((r >= 2) & (r < 4) & (l == r - 2))
    )
    rows[...] = lax.dot_general(sel, feat_ref[...], dims(1, 1), preferred_element_type=F32).astype(BF)
    halves = []
    for cls in range(3):
        i2, i1, i0 = index[cls]
        right, left = near_by(cls, 0)
        legs[cls][0].wait_recv()
        e = ring(cls, 0, 2, half(piece(cls, i2, i1, off(i0, 3)), 0, 0), right)
        legs[cls][1].wait_recv()
        f = ring(cls, 0, 3, half(piece(cls, i2, i1, off(i0, 1)), 0, 1), left)
        halves.append((e, f))
    pl.semaphore_wait(near.at[1], 3)
    tell(2, [core])
    legs = []
    far = [[None] * 4 for _ in range(3)]

    def spread_row(cls, d):
        i2, i1, _ = index[cls]
        right, left = near_by(cls, 2)
        ref = row_of(cls, i2, off(i1, d))
        far[cls][d] = (ring(cls, 2, 2 * d, ref, right), ring(cls, 2, 2 * d + 1, ref, left))

    for cls in range(3):
        i2, i1, _ = index[cls]
        for cp in halves[cls]:
            cp.wait_recv()
        right, left = near_by(cls, 1)
        mine = row_of(cls, i2, i1)
        legs.append((ring(cls, 1, 0, mine, right), ring(cls, 1, 1, mine, left)))
    for cls in range(3):
        spread_row(cls, 0)
    for k in range(2, 5):
        copies[k].wait()
    lf = lf_ref[...].astype(F32)
    zero = jnp.zeros((128, 128), F32)
    pack(send_f, {0: lf[0:128], 1: lf[128:256], **{r: zero for r in range(2, 8)}})
    halves = []
    for cls in range(3):
        i2, i1, _ = index[cls]
        right, left = near_by(cls, 1)
        legs[cls][0].wait_recv()
        e = ring(cls, 1, 2, half(row_of(cls, i2, off(i1, 3)), 1, 0), right)
        legs[cls][1].wait_recv()
        f = ring(cls, 1, 3, half(row_of(cls, i2, off(i1, 1)), 1, 1), left)
        halves.append((e, f))
    for cls in range(3):
        spread_row(cls, 3)
        spread_row(cls, 1)
    pl.semaphore_wait(near.at[2], 1)
    for cls in range(3):
        for cp in halves[cls]:
            cp.wait_recv()
        spread_row(cls, 2)
    for cls in range(3):
        cross(cls, index[cls][0], 0)
    lfx = exchange(send_f, land_f, 0)
    relays = []
    for d, k in ((0, 0), (3, 1), (1, 0), (2, 1)):
        for cls in range(3):
            i2, i1, _ = index[cls]
            far[cls][d][k].wait_recv()
            ref = row_of(cls, off(i2, 1 if k else 3), off(i1, d))
            relays.append(ring(cls, 2, 8 + d, ref, near_by(cls, 2)[k]))
    ha = push(rows, hland.at[0], hs.at[0], hr.at[0], right_shard)
    hb = push(rows, hland.at[1], hs.at[1], hr.at[1], left_shard)
    for cls in range(3):
        for d, k in ((0, 1), (3, 0), (1, 1), (2, 0)):
            far[cls][d][k].wait_recv()
        cross(cls, off(index[cls][0], 3), 1)
        cross(cls, off(index[cls][0], 1), 2)
    fh[:, 0:128] = feat_ref[...]
    tc = jnp.concatenate([taps_ref[...], jnp.zeros((125, 768), F32)], axis=0)
    for k in range(6):
        tcol[k * 128 : (k + 1) * 128, :] = tc[:, k * 128 : (k + 1) * 128].T
    lfx.wait_recv()
    unpack(land_f)
    for ch in range(2):
        hf[ch] = plane(ch)
    build_toeplitz(tt0, hf, 0)
    for cp in relays:
        cp.wait_recv()
    for cls in range(3):
        cross(cls, off(index[cls][0], 2), 3)
    build_toeplitz(tt1, hf, 1)
    ha.wait_recv()
    hb.wait_recv()
    fcp = push(feat_ref, fo_ref, fs, fr, core)
    ocp = push(og_ref, ogn, os, orr, left_shard)
    row = lax.broadcasted_iota(jnp.int32, (16, 4096), 0)
    both = jnp.where(row < 2, hland[0].astype(F32), hland[1].astype(F32)).astype(BF)
    lo = jnp.where(s > 0, 0, 2)
    hi = jnp.where(s < 127, 4, 2)
    spread = one_hot(16, 128, lambda r, l: (r == l) & (r >= lo) & (r < hi))
    fh[:, 128:256] = lax.dot_general(both, spread, dims(0, 0), preferred_element_type=F32).astype(BF)
    for cp in d2d:
        cp.wait_recv()

    for cls in range(3):
        acc = None
        for q in range(8):
            lhs = wide_block(g_ref, cls, q // 4, q % 4)
            term = jnp.dot(lhs, fh[q * 512 : (q + 1) * 512, :], preferred_element_type=F32)
            acc = term if acc is None else acc + term
        for m in range(16):
            at = slice(m * 48 + cls * 16, m * 48 + cls * 16 + 16)
            p_ref[at, :] = acc[m * 16 : (m + 1) * 16, 0:128]
            halo_ref[at, :] = acc[m * 16 : (m + 1) * 16, 128:256]

    lane = lanes(256)
    for part in range(3):
        at = slice(part * 256, (part + 1) * 256)
        v = p_ref[at, :]
        halo = halo_ref[at, :]
        t0, t1, t2 = tcol[at, 0:1], tcol[at, 1:2], tcol[at, 2:3]
        v1 = jnp.where(lane < 1, pltpu.roll(halo, 127, 1), pltpu.roll(v, 1, 1))
        v2 = jnp.where(lane < 2, halo, pltpu.roll(v, 2, 1))
        feat[part] = t0 * v + t1 * v1 + t2 * v2
        n1 = jnp.where(lane < 1, pltpu.roll(v, 1, 1), pltpu.roll(halo, 127, 1))
        featn[part] = t0 * pltpu.roll(halo, 126, 1) + t1 * n1 + t2 * pltpu.roll(v, 2, 1)
    og = og_ref[...].astype(F32)
    gated = feat[1] * feat[2]
    cot = og * feat[0]
    pack(send_a, {0: gated[0:128], 1: gated[128:256], 2: cot[0:128], 3: cot[128:256]})
    go = exchange(send_a, land_a, 1)
    go.wait_recv()
    unpack(land_a)

    anti = one_hot(128, 128, lambda r, l: r + l == 127)
    row = lax.broadcasted_iota(jnp.int32, (128, 128), 0)
    lane1 = lanes(128)
    ahead = jnp.zeros((128, 128), F32)
    cots = []
    for ch in range(2):
        gf[ch] = plane(ch)
        cots.append(plane(2 + ch).astype(BF))
    for ch in range(2):
        xg = lax.dot_general(anti, gf[ch].astype(BF), dims(1, 1), preferred_element_type=F32)
        back = lax.dot_general(cots[ch], anti, dims(0, 0), preferred_element_type=F32)
        spread_blocks(xs, 1, xg)
        spread_blocks(xs, 0, back)
        xc[ch] = xs[:, 0:128]
        yc, yg = toeplitz_product(tt0 if ch == 0 else tt1, xs, 2)
        conv = lax.dot_general(yg, anti, dims(0, 0), preferred_element_type=F32)
        gg = lax.dot_general(anti, yc, dims(1, 1), preferred_element_type=F32)
        rowbuf[pl.ds(ch, 128, stride=8), :] = conv
        rowbuf[pl.ds(2 + ch, 128, stride=8), :] = gg
        for k, value in ((ch, conv), (2 + ch, gg)):
            nxt = jnp.where(row < 127, pltpu.roll(value, 127, 0), 0.0)
            moved = pltpu.roll(nxt, 2 * k, 1) if k else nxt
            ahead = jnp.where((lane1 >= 2 * k) & (lane1 < 2 * k + 2), moved, ahead)
    pack(send_b, {4: ahead})
    ret = exchange(send_b, land_b, 2)
    build_toeplitz(tt0, gf, 0)
    build_toeplitz(tt1, gf, 1)
    for ch in range(2):
        (y,) = toeplitz_product(tt0 if ch == 0 else tt1, xc.at[ch], 1)
        rowbuf[pl.ds(ch, 128, stride=8), :] = lax.dot_general(anti, y, dims(1, 1), preferred_element_type=F32)
    pack(send_c, {})
    ocp.wait_recv()
    ret.wait_recv()
    unpack(land_b)

    def channels(r):
        return jnp.concatenate([plane(r), plane(r + 1)], axis=0)

    conv, gg = channels(0), channels(2)
    ahead = plane(4)
    convn = jnp.concatenate([ahead, pltpu.roll(ahead, 126, 1)], axis=0)
    ggn = jnp.concatenate([pltpu.roll(ahead, 124, 1), pltpu.roll(ahead, 122, 1)], axis=0)
    mixed_ref[...] = (feat[0] * conv).astype(BF)
    store(0, mixed_ref, mixed_hbm)
    ogv = ogn[...].astype(F32)
    last = s == 127

    def derivative(part):
        if part == 0:
            return og * conv
        return gg * feat[3 - part]

    for part in range(3):
        at = slice(part * 256, (part + 1) * 256)
        fd = derivative(part)
        fdn = ogv * convn if part == 0 else ggn * featn[3 - part]
        fdn = jnp.where(last, 0.0, fdn)
        t0, t1, t2 = tcol[at, 0:1], tcol[at, 1:2], tcol[at, 2:3]
        f1 = jnp.where(lane < 127, pltpu.roll(fd, 127, 1), pltpu.roll(fdn, 127, 1))
        f2 = jnp.where(lane < 126, pltpu.roll(fd, 126, 1), pltpu.roll(fdn, 126, 1))
        pd_ref[at, :] = (t0 * fd + t1 * f1 + t2 * f2).astype(BF)
    pcp = push(pd_ref, pdo, ps, pr, core)

    for part in range(3):
        at = slice(part * 256, (part + 1) * 256)
        fd = derivative(part)
        v = p_ref[at, :]
        halo = halo_ref[at, :]
        v1 = jnp.where(lane < 1, pltpu.roll(halo, 127, 1), pltpu.roll(v, 1, 1))
        v2 = jnp.where(lane < 2, halo, pltpu.roll(v, 2, 1))
        total = jnp.zeros((256, 128), F32)
        for k, q in enumerate((v, v1, v2)):
            total = jnp.where(lane == k, jnp.sum(fd * q, axis=1, keepdims=True), total)
        tl[0, c, :, at] = total.T[0:8, :]

    def tap_send(k, peers, slot):
        return [
            push(tl.at[k, slot], tl.at[k, slot], tsn.at[k, i], trc.at[k, i], device)
            for i, device in enumerate(peers)
        ]

    def tap_sum(k, cps, count):
        for cp in cps:
            cp.wait_recv()
        total = tl[k, 0]
        for i in range(1, count):
            total = total + tl[k, i]
        return total

    tcp = tap_send(0, [core], c)
    fgx = exchange(send_c, land_c, 3)
    fcp.wait_recv()
    pcp.wait_recv()
    for cls in range(3):
        for z in range(4):
            for yl in range(2):
                at = pl.ds(pl.multiple_of((z * 4 + yl * 2 + c) * 48 + cls * 16, 16), 16)
                to = cls * 128 + z * 32 + yl * 16
                pdc[to : to + 16, 0:128] = pd_ref[at, :]
                pdc[to : to + 16, 128:256] = pdo[at, :]

    for yh in range(2):
        for x in range(4):
            cols = slice((yh * 4 + x) * 512, (yh * 4 + x + 1) * 512)
            rhs = jnp.concatenate([feat_ref[cols, :], fo_ref[cols, :]], axis=1)
            for cls in range(3):
                part = lax.dot_general(
                    pdc[cls * 128 : (cls + 1) * 128, :], rhs, dims(1, 1), preferred_element_type=F32
                ).astype(BF)
                for z in range(4):
                    for yl in range(2):
                        i2, i1, i0 = piece_index(cls, z, yh, yl, x)
                        k = z * 32 + yl * 16
                        p[cls, i2, i1, i0] = part[k : k + 16, :]

    def add(dst, src):
        dst[...] = (dst[...].astype(F32) + src[...].astype(F32)).astype(BF)

    def feat_part(qs):
        for q in qs:
            total = None
            for cls in range(3):
                term = lax.dot_general(
                    pdt[:, cls * 256 : (cls + 1) * 256], wide_block(g_ref, cls, q // 4, q % 4), dims(1, 0),
                    preferred_element_type=F32,
                )
                total = term if total is None else total + term
            fgrad_ref[q * 512 : (q + 1) * 512, :] = total.T.astype(BF)

    def back(cls, phase, k, src, dst, device):
        return push(src, dst, ss2.at[cls, phase, k], rs2.at[cls, phase, k], device)

    def prow(cls, d2, d1):
        i2, i1, _ = index[cls]
        return p.at[cls, off(i2, d2), off(i1, d1)]

    relay = ((2, 1), (0, 3))
    hops, came = [], []
    for cls in range(3):
        hops.append({})
        came.append({})
    for j in range(2):
        for cls in range(3):
            right, left = near_by(cls, 2)
            hops[cls][0, j] = back(cls, 2, j, prow(cls, 2, relay[j][0]), ra3.at[cls, j], right)
            hops[cls][1, j] = back(cls, 2, 2 + j, prow(cls, 2, relay[j][1]), rb3.at[cls, j], left)
    for j in range(2):
        for cls in range(3):
            right, left = near_by(cls, 2)
            d = relay[j][0]
            came[cls][1, d] = back(cls, 2, 8 + d, prow(cls, 3, d), rd3.at[cls, d], left)
            d = relay[j][1]
            came[cls][0, d] = back(cls, 2, 4 + d, prow(cls, 1, d), rc3.at[cls, d], right)
    pdt[...] = jnp.concatenate(
        [
            pd_ref[m * 48 + cls * 16 : m * 48 + cls * 16 + 16, :].astype(F32)
            for cls in range(3)
            for m in range(16)
        ],
        axis=0,
    ).T.astype(BF)
    feat_part(range(1))
    for j in range(2):
        for cls in range(3):
            right, left = near_by(cls, 2)
            d = relay[j][0]
            hops[cls][0, j].wait_recv()
            add(prow(cls, 1, d), ra3.at[cls, j])
            came[cls][0, d] = back(cls, 2, 4 + d, prow(cls, 1, d), rc3.at[cls, d], right)
            d = relay[j][1]
            hops[cls][1, j].wait_recv()
            add(prow(cls, 3, d), rb3.at[cls, j])
            came[cls][1, d] = back(cls, 2, 8 + d, prow(cls, 3, d), rd3.at[cls, d], left)
    tl[1, pos["x"]] = tap_sum(0, tcp, 2)
    tcp = tap_send(1, line["x"], pos["x"])
    feat_part(range(1, 3))

    def finish_row(cls, d):
        came[cls][0, d].wait_recv()
        came[cls][1, d].wait_recv()
        mine = prow(cls, 0, d)
        total = mine[...].astype(F32) + rc3[cls, d].astype(F32) + rd3[cls, d].astype(F32)
        mine[...] = total.astype(BF)

    legs = [{} for _ in range(3)]
    for cls in range(3):
        right, left = near_by(cls, 1)
        finish_row(cls, 2)
        far_row = prow(cls, 0, 2)
        legs[cls][0] = back(cls, 1, 0, half(far_row, 1, 0), ra2.at[cls], right)
        legs[cls][1] = back(cls, 1, 1, half(far_row, 1, 1), rb2.at[cls], left)
    for cls in range(3):
        right, left = near_by(cls, 1)
        finish_row(cls, 1)
        legs[cls][2] = back(cls, 1, 2, half(prow(cls, 0, 1), 1, 1), half(rc2.at[cls], 1, 1), right)
        finish_row(cls, 3)
        legs[cls][3] = back(cls, 1, 3, half(prow(cls, 0, 3), 1, 0), half(rd2.at[cls], 1, 0), left)
    for cls in range(3):
        finish_row(cls, 0)
    for cls in range(3):
        right, left = near_by(cls, 1)
        legs[cls][0].wait_recv()
        add(half(prow(cls, 0, 1), 1, 0), ra2.at[cls])
        legs[cls][4] = back(cls, 1, 4, half(prow(cls, 0, 1), 1, 0), half(rc2.at[cls], 1, 0), right)
        legs[cls][1].wait_recv()
        add(half(prow(cls, 0, 3), 1, 1), rb2.at[cls])
        legs[cls][5] = back(cls, 1, 5, half(prow(cls, 0, 3), 1, 1), half(rd2.at[cls], 1, 1), left)
    tl[2, pos["y"]] = tap_sum(1, tcp, 4)
    tcp = tap_send(2, line["y"], pos["y"])
    feat_part(range(3, 5))
    low = [{} for _ in range(3)]

    def part_of(cls, d):
        i2, i1, i0 = index[cls]
        return p.at[cls, i2, i1, off(i0, d)]

    for cls in range(3):
        right, left = near_by(cls, 0)
        for k in range(2, 6):
            legs[cls][k].wait_recv()
        mine = prow(cls, 0, 0)
        total = mine[...].astype(F32) + rc2[cls].astype(F32) + rd2[cls].astype(F32)
        mine[...] = total.astype(BF)
        low[cls][0] = back(cls, 0, 0, half(part_of(cls, 2), 0, 0), ra1.at[cls], right)
        low[cls][1] = back(cls, 0, 1, half(part_of(cls, 2), 0, 1), rb1.at[cls], left)
        low[cls][2] = back(cls, 0, 2, half(part_of(cls, 1), 0, 1), half(rc1.at[cls], 0, 1), right)
        low[cls][3] = back(cls, 0, 3, half(part_of(cls, 3), 0, 0), half(rd1.at[cls], 0, 0), left)
    tl[3, pos["z"]] = tap_sum(2, tcp, 4)
    tcp = tap_send(3, line["z"], pos["z"])
    feat_part(range(5, 7))
    for cls in range(3):
        right, left = near_by(cls, 0)
        low[cls][0].wait_recv()
        add(half(part_of(cls, 1), 0, 0), ra1.at[cls])
        low[cls][4] = back(cls, 0, 4, half(part_of(cls, 1), 0, 0), half(rc1.at[cls], 0, 0), right)
        low[cls][1].wait_recv()
        add(half(part_of(cls, 3), 0, 1), rb1.at[cls])
        low[cls][5] = back(cls, 0, 5, half(part_of(cls, 3), 0, 1), half(rd1.at[cls], 0, 1), left)
    feat_part(range(7, 8))
    store(1, fgrad_ref, fgrad_hbm)
    for cls in range(3):
        for k in range(2, 6):
            low[cls][k].wait_recv()
        blk[cls * 16 : (cls + 1) * 16, :] = (
            part_of(cls, 0)[...].astype(F32) + rc1[cls].astype(F32) + rd1[cls].astype(F32)
        )

    for q in range(8):
        stage2[q, 0:6, :] = blk[q * 6 : (q + 1) * 6, :]
        stage2[q, 6:8, :] = jnp.zeros((2, 512), F32)
    final = []
    for i in range(1, 8):
        q = lax.rem(w + i, 8)
        final.append(push(stage2.at[q], land2.at[w], s02.at[i], r02.at[i], (n, q)))
    land2[w] = stage2[w]
    tout_ref[...] = tap_sum(3, tcp, 4)[0:3]
    store(3, tout_ref, tout_hbm)
    fgx.wait_recv()
    unpack(land_c)
    fgout_ref[...] = channels(0).astype(BF)
    store(2, fgout_ref, fgout_hbm)
    for cp in final:
        cp.wait_recv()
    for q in range(8):
        grad_ref[:, q * 512 : (q + 1) * 512] = land2[q, 0:6, :]
    store(4, grad_ref, grad_hbm)
    for cp in started:
        cp.wait_send()
    for cp in stores:
        cp.wait()


ANY = pl.BlockSpec(memory_space=pl.ANY)


def hyena(in_proj, features, taps, out_grad, long_filter):
    sem = pltpu.SemaphoreType.DMA
    vm = pltpu.VMEM
    tile = (128, 8, 128)
    return pl.pallas_call(
        hyena_kernel,
        out_shape=(
            jax.ShapeDtypeStruct((256, 128), BF),
            jax.ShapeDtypeStruct((4096, 128), BF),
            jax.ShapeDtypeStruct((256, 128), BF),
            jax.ShapeDtypeStruct((3, 768), F32),
            jax.ShapeDtypeStruct((6, 4096), F32),
        ),
        in_specs=[ANY] * 5,
        out_specs=(ANY,) * 5,
        scratch_shapes=[
            vm((256, 128), BF), vm((4096, 128), BF), vm((256, 128), BF), vm((3, 768), F32), vm((6, 4096), F32), sem((5,)),
            vm((6, 4096), BF), vm((4096, 128), BF), vm((3, 768), F32), vm((256, 128), BF), vm((256, 128), BF),
            vm((8, 8, 512), F32), vm((8, 8, 512), F32), vm((48, 512), F32),
            vm((16, 4096), BF), vm((2, 16, 4096), BF), vm((4096, 256), BF),
            vm((3, 2, 4, 4, 4, 16, 512), BF), vm((4096, 128), BF),
            vm((768, 128), F32), vm((768, 128), F32), vm((768, 128), F32),
            vm((1024, 128), F32),
        ]
        + [vm(tile, BF)] * 8
        + [
            vm((256, 128), BF), vm((2, 128, 128), F32), vm((2, 128, 128), F32),
            vm((3, 256, 128), F32), vm((3, 256, 128), F32),
            vm((1024, 2048), BF), vm((1024, 2048), BF), vm((2048, 256), BF), vm((2, 2048, 128), BF),
            vm((768, 128), BF),
            vm((768, 128), BF), vm((384, 256), BF), vm((3, 4, 4, 4, 16, 512), BF),
            vm((3, 2, 4, 16, 512), BF), vm((3, 2, 4, 16, 512), BF),
            vm((3, 4, 4, 16, 512), BF), vm((3, 4, 4, 16, 512), BF),
            vm((3, 2, 16, 512), BF), vm((3, 2, 16, 512), BF),
            vm((3, 4, 16, 512), BF), vm((3, 4, 16, 512), BF),
            vm((3, 16, 256), BF), vm((3, 16, 256), BF),
            vm((3, 16, 512), BF), vm((3, 16, 512), BF),
            vm((8, 8, 512), F32), vm((8, 8, 512), F32), vm((4, 4, 8, 768), F32), vm((128, 768), BF),
            sem((5,)), sem((8,)), sem((8,)),
            sem((3, 3, 12)), sem((3, 3, 12)), sem((3, 4)), sem((3, 4)),
            sem((2,)), sem((2,)), sem, sem, sem((4,)), sem((4,)), sem, sem,
            sem, sem, sem((3, 3, 12)), sem((3, 3, 12)), sem((8,)), sem((8,)), sem((4, 3)), sem((4, 3)),
            pltpu.SemaphoreType.REGULAR((3,)),
        ],
        compiler_params=pltpu.CompilerParams(
            collective_id=1, has_side_effects=True, vmem_limit_bytes=58 * 1024 * 1024
        ),
        name="hyena",
    )(in_proj, features, taps, out_grad, long_filter)


def copy_kernel(*refs):
    sources, targets, held, (came, left) = refs[:5], refs[5:10], refs[10:15], refs[15:]
    inward = [pltpu.make_async_copy(sources[k], held[k], came.at[k]) for k in range(5)]
    outward = [pltpu.make_async_copy(held[k], targets[k], left.at[k]) for k in range(5)]
    for cp in inward:
        cp.start()
    for k in range(5):
        inward[k].wait()
        outward[k].start()
    for cp in outward:
        cp.wait()


def settle(arrays):
    return pl.pallas_call(
        copy_kernel,
        out_shape=tuple(jax.ShapeDtypeStruct(a.shape, a.dtype) for a in arrays),
        in_specs=[ANY] * 5,
        out_specs=(ANY,) * 5,
        scratch_shapes=[pltpu.VMEM(a.shape, a.dtype) for a in arrays]
        + [pltpu.SemaphoreType.DMA((5,)), pltpu.SemaphoreType.DMA((5,))],
        name="settle",
    )(*arrays)


def local(features, in_proj, short_taps, long_filter, out_grad):
    return settle(hyena(in_proj, features, short_taps, out_grad, long_filter))


def solution(mesh):
    tokens = P(None, AXES)
    rows = P(AXES, None)
    return jax.shard_map(
        local,
        mesh=mesh,
        in_specs=(tokens, rows, P(), tokens, tokens),
        out_specs=(tokens, tokens, tokens, P(), rows),
        check_vma=False,
    )
```

```python
import math

import jax
import jax.numpy as jnp
from jax import lax
from jax.experimental import pallas as pl
from jax.experimental.pallas import tpu as pltpu
from jax.sharding import PartitionSpec as P

MESH = pl.DeviceIdType.MESH
BF = jnp.bfloat16
F32 = jnp.float32
ORDERS = (("x", "y", "z"), ("y", "z", "x"), ("z", "x", "y"))
AXES = ("narrow", "wide")


def place(pos):
    y = pos["y"]
    return (pos["z"] * 4 + lax.rem(y, 2) * 2 + pos["c"], (y // 2) * 4 + pos["x"])


def position():
    n = lax.axis_index("narrow")
    w = lax.axis_index("wide")
    pos = {
        "x": lax.rem(w, 4),
        "y": (w // 4) * 2 + lax.rem(n // 2, 2),
        "z": n // 4,
        "c": lax.rem(n, 2),
    }
    return n, w, pos


def shifted(pos, axis, by):
    other = dict(pos)
    other[axis] = lax.rem(pos[axis] + by + 4, 4)
    return place(other)


def other_core(pos):
    other = dict(pos)
    other["c"] = 1 - pos["c"]
    return place(other)


def shard_id(s):
    return (s // 8, lax.rem(s, 8))


def remote(src, dst, send, recv, device):
    return pltpu.make_async_remote_copy(
        src_ref=src, dst_ref=dst, send_sem=send, recv_sem=recv, device_id=device, device_id_type=MESH
    )


def greet(devices):
    barrier = pltpu.get_barrier_semaphore()
    for device in devices:
        pl.semaphore_signal(barrier, inc=1, device_id=device, device_id_type=MESH)
    pl.semaphore_wait(barrier, len(devices))


def piece_index(cls, z, yh, yl, x):
    at = {"x": x, "y": yh * 2 + yl, "z": z}
    d0, d1, d2 = ORDERS[cls]
    return (at[d2], at[d1], at[d0])


def dims(a, b):
    return (((a,), (b,)), ((), ()))


def lanes(rows):
    return lax.broadcasted_iota(jnp.int32, (rows, 128), 1)


def one_hot(rows, cols, test):
    r = lax.broadcasted_iota(jnp.int32, (rows, cols), 0)
    c = lax.broadcasted_iota(jnp.int32, (rows, cols), 1)
    return jnp.where(test(r, c), 1.0, 0.0).astype(BF)


def wide_block(g_ref, cls, yh, x):
    parts = []
    for z in range(4):
        for yl in range(2):
            for core in range(2):
                i2, i1, i0 = piece_index(cls, z, yh, yl, x)
                parts.append(g_ref[cls, core, i2, i1, i0])
    return jnp.concatenate(parts, axis=0)


def half(ref, phase, k):
    if phase == 0:
        return ref.at[:, pl.ds(k * 256, 256)]
    return ref.at[pl.ds(k * 2, 2)]


def build_toeplitz(tt, h_ref, ch):
    lane = lanes(128)
    row = lax.broadcasted_iota(jnp.int32, (128, 128), 0)
    upper = lane >= row

    def rolled(k):
        taps = jnp.broadcast_to(h_ref[ch, pl.ds(k, 1), :], (128, 128))
        return pltpu.roll(taps, 0, 1, stride=1, stride_axis=0)

    @pl.loop(0, 8)
    def _(g):
        prev = jnp.where(g > 0, rolled(jnp.maximum(16 * g - 1, 0)), 0.0)
        at = pl.ds(pl.multiple_of(g * 128, 128), 128)
        for i in range(16):
            cur = rolled(16 * g + i)
            tt[at, i * 128 : (i + 1) * 128] = jnp.where(upper, cur, prev).astype(BF)
            prev = cur


def spread_blocks(xs, col, x):
    lane = lanes(128)
    for i in range(16):
        moved = pltpu.roll(x, i, 1) if i else x
        xs[i * 128 : (i + 1) * 128, col * 128 : (col + 1) * 128] = jnp.where(lane < i, 0.0, moved).astype(BF)


def toeplitz_product(tt, xs, cols):
    lane = lanes(128)
    out = jnp.dot(tt[...], xs[:, 0 : cols * 128], preferred_element_type=F32)
    results = []
    for c in range(cols):
        at = slice(c * 128, (c + 1) * 128)
        acc = out[896:1024, at]
        for g in range(6, -1, -1):
            acc = jnp.where(lane < 16, 0.0, pltpu.roll(acc, 16, 1)) + out[g * 128 : (g + 1) * 128, at]
        results.append(acc.astype(BF))
    return results


def hyena_kernel(
    proj_hbm, feat_hbm, taps_hbm, og_hbm, lf_hbm,
    mixed_hbm, fgrad_hbm, fgout_hbm, tout_hbm, grad_hbm,
    mixed_ref, fgrad_ref, fgout_ref, tout_ref, grad_ref, outs,
    proj_ref, feat_ref, taps_ref, og_ref, lf_ref,
    stage, land, blk, rows, hland, fh, g_ref, fo_ref, p_ref, halo_ref, tcol,
    rowbuf, send_f, land_f, send_a, land_a, send_b, land_b, send_c, land_c,
    ogn, hf, gf, feat, featn, tt0, tt1, xs, xc, pd_ref,
    pdo, pdc, p, ra3, rb3, rc3, rd3, ra2, rb2, rc2, rd2, rz, mid_f, mid_c,
    stage2, land2, tl, pdt,
    ins, s0, r0, ss, rs, ds, dr, hs, hr, fs, fr, xsend, xrecv, os, orr,
    ps, pr, ss2, rs2, s02, r02, tsn, trc, near, xs1, xr1, xs2, xr2,
):
    n, w, pos = position()
    c = pos["c"]
    s = n * 8 + w
    right_shard = shard_id(lax.rem(s + 1, 128))
    left_shard = shard_id(lax.rem(s + 127, 128))
    wide_peers = [(n, lax.rem(w + i, 8)) for i in range(1, 8)]
    line = {a: [shifted(pos, a, d) for d in (1, 2, 3)] for a in "xyz"}
    core = other_core(pos)
    copies = [
        pltpu.make_async_copy(a, b, ins.at[k])
        for k, (a, b) in enumerate(
            ((proj_hbm, proj_ref), (feat_hbm, feat_ref), (taps_hbm, taps_ref), (og_hbm, og_ref), (lf_hbm, lf_ref))
        )
    ]
    for cp in copies:
        cp.start()
    barrier = pltpu.get_barrier_semaphore()
    greeted = wide_peers + line["y"] + line["z"] + [core, right_shard, left_shard]
    for device in greeted:
        pl.semaphore_signal(barrier, inc=1, device_id=device, device_id_type=MESH)
    copies[0].wait()
    for q in range(8):
        stage[q, 0:6, :] = proj_ref[:, q * 512 : (q + 1) * 512].astype(F32)
        stage[q, 6:8, :] = jnp.zeros((2, 512), F32)
    pl.semaphore_wait(barrier, len(greeted))

    def tell(k, devices):
        for device in devices:
            pl.semaphore_signal(near.at[k], inc=1, device_id=device, device_id_type=MESH)

    started = []
    stores = []

    def store(k, src, dst):
        cp = pltpu.make_async_copy(src, dst, outs.at[k])
        cp.start()
        stores.append(cp)

    def push(src, dst, a, b, device):
        cp = remote(src, dst, a, b, device)
        cp.start()
        started.append(cp)
        return cp

    first = []
    for i in range(1, 8):
        q = lax.rem(w + i, 8)
        first.append(push(stage.at[q], land.at[w], s0.at[i], r0.at[i], (n, q)))
    tell(0, line["x"])
    land[w] = stage[w]
    for cp in first:
        cp.wait_recv()
    for q in range(8):
        blk[q * 6 : (q + 1) * 6, :] = land[q, 0:6, :]

    index = [[pos[a] for a in reversed(order)] for order in ORDERS]
    for cls in range(3):
        i2, i1, i0 = index[cls]
        g_ref[cls, c, i2, i1, i0] = blk[cls * 16 : (cls + 1) * 16, :].astype(BF)

    d2d = []

    def cross(cls, j, k):
        ref = g_ref.at[cls, c, j]
        d2d.append(push(ref, ref, ds.at[cls, k], dr.at[cls, k], core))

    def exchange(src, dst, k):
        ww = [lax.rem(w + j, 8) for j in range(8)]
        for j in range(1, 8):
            remote(src.at[n * 8 + ww[j]], dst.at[s], xsend.at[k], xrecv.at[k], (n, ww[j])).start()

        @pl.loop(1, 16)
        def _(i):
            nn = lax.rem(n + i, 16)
            for j in range(8):
                remote(src.at[nn * 8 + ww[j]], dst.at[s], xsend.at[k], xrecv.at[k], (nn, ww[j])).start()

        dst[s] = src[s]
        whole = pl.ds(0, 127)
        cp = remote(src.at[whole], dst.at[whole], xsend.at[k], xrecv.at[k], (n, w))
        started.append(cp)
        return cp

    def hand(src, mid, k):
        cps = []
        for i in range(1, 8):
            q = lax.rem(w + i, 8)
            cps.append(push(src.at[:, q], mid.at[w], xs1.at[k, i], xr1.at[k, i], (n, q)))
        mid[w] = src[:, w]
        return cps

    def pass_on(cps, mid, dst, k):
        for cp in cps:
            cp.wait_recv()
        out = []
        for i in range(1, 16):
            m = lax.rem(n + i, 16)
            out.append(push(mid.at[:, m], dst.at[n], xs2.at[k, i], xr2.at[k, i], (m, w)))
        dst[n] = mid[:, n]
        return out

    def pack(buf, parts):
        for r, value in parts.items():
            rowbuf[pl.ds(r, 128, stride=8), :] = value
        buf[...] = rowbuf[...].reshape(buf.shape).astype(BF)

    def unpack(buf):
        rowbuf[...] = buf[...].astype(F32).reshape(1024, 128)

    def plane(r):
        return rowbuf[pl.ds(r, 128, stride=8), :]

    def piece(cls, i2, i1, i0):
        return g_ref.at[cls, c, i2, i1, i0]

    def row_of(cls, i2, i1):
        return g_ref.at[cls, c, i2, i1]

    def near_by(cls, phase):
        axis = ORDERS[cls][phase]
        return shifted(pos, axis, 1), shifted(pos, axis, -1)

    def ring(cls, phase, k, ref, device):
        return push(ref, ref, ss.at[cls, phase, k], rs.at[cls, phase, k], device)

    def off(i, d):
        return lax.rem(i + d, 4)

    legs = []
    for cls in range(3):
        mine = piece(cls, *index[cls])
        legs.append([ring(cls, 0, d, mine, shifted(pos, ORDERS[cls][0], d)) for d in (1, 2, 3)])
    pl.semaphore_wait(near.at[0], 3)
    tell(1, line["y"])
    firsts, legs = legs, []
    far = [[None] * 4 for _ in range(3)]

    def spread_row(cls, d):
        i2, i1, _ = index[cls]
        right, left = near_by(cls, 2)
        ref = row_of(cls, i2, off(i1, d))
        far[cls][d] = (ring(cls, 2, 2 * d, ref, right), ring(cls, 2, 2 * d + 1, ref, left))

    for cls in range(3):
        i2, i1, _ = index[cls]
        for cp in firsts[cls]:
            cp.wait_recv()
        right, left = near_by(cls, 1)
        mine = row_of(cls, i2, i1)
        legs.append((ring(cls, 1, 0, mine, right), ring(cls, 1, 1, mine, left)))
    for cls in range(3):
        spread_row(cls, 0)
    pl.semaphore_wait(near.at[1], 3)
    tell(2, [core])
    copies[4].wait()
    lf = lf_ref[...].astype(F32)
    zero = jnp.zeros((128, 128), F32)
    pack(send_f, {0: lf[0:128], 1: lf[128:256], **{r: zero for r in range(2, 8)}})
    lf_half = hand(send_f, mid_f, 0)
    halves = []
    for cls in range(3):
        i2, i1, _ = index[cls]
        right, left = near_by(cls, 1)
        legs[cls][0].wait_recv()
        e = ring(cls, 1, 2, half(row_of(cls, i2, off(i1, 3)), 1, 0), right)
        legs[cls][1].wait_recv()
        f = ring(cls, 1, 3, half(row_of(cls, i2, off(i1, 1)), 1, 1), left)
        halves.append((e, f))
    for cls in range(3):
        spread_row(cls, 3)
        spread_row(cls, 1)
    pl.semaphore_wait(near.at[2], 1)
    for cls in range(3):
        for cp in halves[cls]:
            cp.wait_recv()
        spread_row(cls, 2)
    for cls in range(3):
        cross(cls, index[cls][0], 0)
    lfx = pass_on(lf_half, mid_f, land_f, 0)
    copies[1].wait()
    sel = one_hot(
        16, 128, lambda r, l: ((r < 2) & (l == r + 126)) | ((r >= 2) & (r < 4) & (l == r - 2))
    )
    rows[...] = lax.dot_general(sel, feat_ref[...], dims(1, 1), preferred_element_type=F32).astype(BF)
    ha = push(rows, hland.at[0], hs.at[0], hr.at[0], right_shard)
    hb = push(rows, hland.at[1], hs.at[1], hr.at[1], left_shard)
    relays = []
    for d, k in ((0, 0), (3, 1), (1, 0), (2, 1)):
        for cls in range(3):
            i2, i1, _ = index[cls]
            far[cls][d][k].wait_recv()
            ref = row_of(cls, off(i2, 1 if k else 3), off(i1, d))
            relays.append(ring(cls, 2, 8 + d, ref, near_by(cls, 2)[k]))
    for cls in range(3):
        for d, k in ((0, 1), (3, 0), (1, 1), (2, 0)):
            far[cls][d][k].wait_recv()
        cross(cls, off(index[cls][0], 3), 1)
        cross(cls, off(index[cls][0], 1), 2)
    fh[:, 0:128] = feat_ref[...]
    copies[2].wait()
    tc = jnp.concatenate([taps_ref[...], jnp.zeros((125, 768), F32)], axis=0)
    for k in range(6):
        tcol[k * 128 : (k + 1) * 128, :] = tc[:, k * 128 : (k + 1) * 128].T
    for cp in lfx:
        cp.wait_recv()
    unpack(land_f)
    for ch in range(2):
        hf[ch] = plane(ch)
    build_toeplitz(tt0, hf, 0)
    ha.wait_recv()
    hb.wait_recv()
    row = lax.broadcasted_iota(jnp.int32, (16, 4096), 0)
    both = jnp.where(row < 2, hland[0].astype(F32), hland[1].astype(F32)).astype(BF)
    lo = jnp.where(s > 0, 0, 2)
    hi = jnp.where(s < 127, 4, 2)
    spread = one_hot(16, 128, lambda r, l: (r == l) & (r >= lo) & (r < hi))
    fh[:, 128:256] = lax.dot_general(both, spread, dims(0, 0), preferred_element_type=F32).astype(BF)
    for cp in relays:
        cp.wait_recv()
    for cls in range(3):
        cross(cls, off(index[cls][0], 2), 3)
    fcp = push(feat_ref, fo_ref, fs, fr, core)
    copies[3].wait()
    ocp = push(og_ref, ogn, os, orr, left_shard)
    for cp in d2d:
        cp.wait_recv()

    for cls in range(3):
        acc = None
        for q in range(8):
            lhs = wide_block(g_ref, cls, q // 4, q % 4)
            term = jnp.dot(lhs, fh[q * 512 : (q + 1) * 512, :], preferred_element_type=F32)
            acc = term if acc is None else acc + term
        for m in range(16):
            at = slice(m * 48 + cls * 16, m * 48 + cls * 16 + 16)
            p_ref[at, :] = acc[m * 16 : (m + 1) * 16, 0:128]
            halo_ref[at, :] = acc[m * 16 : (m + 1) * 16, 128:256]

    lane = lanes(256)
    for part in range(3):
        at = slice(part * 256, (part + 1) * 256)
        v = p_ref[at, :]
        halo = halo_ref[at, :]
        t0, t1, t2 = tcol[at, 0:1], tcol[at, 1:2], tcol[at, 2:3]
        v1 = jnp.where(lane < 1, pltpu.roll(halo, 127, 1), pltpu.roll(v, 1, 1))
        v2 = jnp.where(lane < 2, halo, pltpu.roll(v, 2, 1))
        feat[part] = t0 * v + t1 * v1 + t2 * v2
        n1 = jnp.where(lane < 1, pltpu.roll(v, 1, 1), pltpu.roll(halo, 127, 1))
        featn[part] = t0 * pltpu.roll(halo, 126, 1) + t1 * n1 + t2 * pltpu.roll(v, 2, 1)
    og = og_ref[...].astype(F32)
    gated = feat[1] * feat[2]
    cot = og * feat[0]
    pack(send_a, {0: gated[0:128], 1: gated[128:256], 2: cot[0:128], 3: cot[128:256]})
    go = exchange(send_a, land_a, 1)
    build_toeplitz(tt1, hf, 1)
    go.wait_recv()
    unpack(land_a)

    anti = one_hot(128, 128, lambda r, l: r + l == 127)
    row = lax.broadcasted_iota(jnp.int32, (128, 128), 0)
    lane1 = lanes(128)
    ahead = jnp.zeros((128, 128), F32)
    cots = []
    for ch in range(2):
        gf[ch] = plane(ch)
        cots.append(plane(2 + ch).astype(BF))
    for ch in range(2):
        xg = lax.dot_general(anti, gf[ch].astype(BF), dims(1, 1), preferred_element_type=F32)
        back = lax.dot_general(cots[ch], anti, dims(0, 0), preferred_element_type=F32)
        spread_blocks(xs, 1, xg)
        spread_blocks(xs, 0, back)
        xc[ch] = xs[:, 0:128]
        yc, yg = toeplitz_product(tt0 if ch == 0 else tt1, xs, 2)
        conv = lax.dot_general(yg, anti, dims(0, 0), preferred_element_type=F32)
        gg = lax.dot_general(anti, yc, dims(1, 1), preferred_element_type=F32)
        rowbuf[pl.ds(ch, 128, stride=8), :] = conv
        rowbuf[pl.ds(2 + ch, 128, stride=8), :] = gg
        for k, value in ((ch, conv), (2 + ch, gg)):
            nxt = jnp.where(row < 127, pltpu.roll(value, 127, 0), 0.0)
            moved = pltpu.roll(nxt, 2 * k, 1) if k else nxt
            ahead = jnp.where((lane1 >= 2 * k) & (lane1 < 2 * k + 2), moved, ahead)
    pack(send_b, {4: ahead})
    ret = exchange(send_b, land_b, 2)
    build_toeplitz(tt0, gf, 0)
    ocp.wait_recv()
    ret.wait_recv()
    unpack(land_b)

    def channels(r):
        return jnp.concatenate([plane(r), plane(r + 1)], axis=0)

    conv, gg = channels(0), channels(2)
    ahead = plane(4)
    convn = jnp.concatenate([ahead, pltpu.roll(ahead, 126, 1)], axis=0)
    ggn = jnp.concatenate([pltpu.roll(ahead, 124, 1), pltpu.roll(ahead, 122, 1)], axis=0)
    mixed_ref[...] = (feat[0] * conv).astype(BF)
    store(0, mixed_ref, mixed_hbm)
    ogv = ogn[...].astype(F32)
    last = s == 127

    def derivative(part):
        if part == 0:
            return og * conv
        return gg * feat[3 - part]

    for part in range(3):
        at = slice(part * 256, (part + 1) * 256)
        fd = derivative(part)
        fdn = ogv * convn if part == 0 else ggn * featn[3 - part]
        fdn = jnp.where(last, 0.0, fdn)
        t0, t1, t2 = tcol[at, 0:1], tcol[at, 1:2], tcol[at, 2:3]
        f1 = jnp.where(lane < 127, pltpu.roll(fd, 127, 1), pltpu.roll(fdn, 127, 1))
        f2 = jnp.where(lane < 126, pltpu.roll(fd, 126, 1), pltpu.roll(fdn, 126, 1))
        pd_ref[at, :] = (t0 * fd + t1 * f1 + t2 * f2).astype(BF)
    pcp = push(pd_ref, pdo, ps, pr, core)

    for part in range(3):
        at = slice(part * 256, (part + 1) * 256)
        fd = derivative(part)
        v = p_ref[at, :]
        halo = halo_ref[at, :]
        v1 = jnp.where(lane < 1, pltpu.roll(halo, 127, 1), pltpu.roll(v, 1, 1))
        v2 = jnp.where(lane < 2, halo, pltpu.roll(v, 2, 1))
        total = jnp.zeros((256, 128), F32)
        for k, q in enumerate((v, v1, v2)):
            total = jnp.where(lane == k, jnp.sum(fd * q, axis=1, keepdims=True), total)
        tl[0, c, :, at] = total.T[0:8, :]

    def tap_send(k, peers, slot):
        return [
            push(tl.at[k, slot], tl.at[k, slot], tsn.at[k, i], trc.at[k, i], device)
            for i, device in enumerate(peers)
        ]

    def tap_sum(k, cps, count):
        for cp in cps:
            cp.wait_recv()
        total = tl[k, 0]
        for i in range(1, count):
            total = total + tl[k, i]
        return total

    tcp = tap_send(0, [core], c)
    fcp.wait_recv()
    pcp.wait_recv()
    for cls in range(3):
        for z in range(4):
            for yl in range(2):
                at = pl.ds(pl.multiple_of((z * 4 + yl * 2 + c) * 48 + cls * 16, 16), 16)
                to = cls * 128 + z * 32 + yl * 16
                pdc[to : to + 16, 0:128] = pd_ref[at, :]
                pdc[to : to + 16, 128:256] = pdo[at, :]

    for yh in range(2):
        for x in range(4):
            cols = slice((yh * 4 + x) * 512, (yh * 4 + x + 1) * 512)
            rhs = jnp.concatenate([feat_ref[cols, :], fo_ref[cols, :]], axis=1)
            for cls in range(3):
                part = lax.dot_general(
                    pdc[cls * 128 : (cls + 1) * 128, :], rhs, dims(1, 1), preferred_element_type=F32
                ).astype(BF)
                for z in range(4):
                    for yl in range(2):
                        i2, i1, i0 = piece_index(cls, z, yh, yl, x)
                        k = z * 32 + yl * 16
                        p[cls, i2, i1, i0] = part[k : k + 16, :]

    def add(dst, src):
        dst[...] = (dst[...].astype(F32) + src[...].astype(F32)).astype(BF)

    def feat_part(qs):
        for q in qs:
            total = None
            for cls in range(3):
                term = lax.dot_general(
                    pdt[:, cls * 256 : (cls + 1) * 256], wide_block(g_ref, cls, q // 4, q % 4), dims(1, 0),
                    preferred_element_type=F32,
                )
                total = term if total is None else total + term
            fgrad_ref[q * 512 : (q + 1) * 512, :] = total.T.astype(BF)

    def back(cls, phase, k, src, dst, device):
        return push(src, dst, ss2.at[cls, phase, k], rs2.at[cls, phase, k], device)

    def prow(cls, d2, d1):
        i2, i1, _ = index[cls]
        return p.at[cls, off(i2, d2), off(i1, d1)]

    relay = ((2, 1), (0, 3))
    hops, came = [], []
    for cls in range(3):
        hops.append({})
        came.append({})
    for j in range(2):
        for cls in range(3):
            right, left = near_by(cls, 2)
            hops[cls][0, j] = back(cls, 2, j, prow(cls, 2, relay[j][0]), ra3.at[cls, j], right)
            hops[cls][1, j] = back(cls, 2, 2 + j, prow(cls, 2, relay[j][1]), rb3.at[cls, j], left)
    for j in range(2):
        for cls in range(3):
            right, left = near_by(cls, 2)
            d = relay[j][0]
            came[cls][1, d] = back(cls, 2, 8 + d, prow(cls, 3, d), rd3.at[cls, d], left)
            d = relay[j][1]
            came[cls][0, d] = back(cls, 2, 4 + d, prow(cls, 1, d), rc3.at[cls, d], right)
    pdt[...] = jnp.concatenate(
        [
            pd_ref[m * 48 + cls * 16 : m * 48 + cls * 16 + 16, :].astype(F32)
            for cls in range(3)
            for m in range(16)
        ],
        axis=0,
    ).T.astype(BF)
    build_toeplitz(tt1, gf, 1)
    for j in range(2):
        for cls in range(3):
            right, left = near_by(cls, 2)
            d = relay[j][0]
            hops[cls][0, j].wait_recv()
            add(prow(cls, 1, d), ra3.at[cls, j])
            came[cls][0, d] = back(cls, 2, 4 + d, prow(cls, 1, d), rc3.at[cls, d], right)
            d = relay[j][1]
            hops[cls][1, j].wait_recv()
            add(prow(cls, 3, d), rb3.at[cls, j])
            came[cls][1, d] = back(cls, 2, 8 + d, prow(cls, 3, d), rd3.at[cls, d], left)
    tl[1, pos["x"]] = tap_sum(0, tcp, 2)
    tcp = tap_send(1, line["x"], pos["x"])
    for ch in range(2):
        (y,) = toeplitz_product(tt0 if ch == 0 else tt1, xc.at[ch], 1)
        rowbuf[pl.ds(ch, 128, stride=8), :] = lax.dot_general(anti, y, dims(1, 1), preferred_element_type=F32)
    pack(send_c, {})
    fg_half = hand(send_c, mid_c, 1)
    feat_part(range(2))

    def finish_row(cls, d):
        came[cls][0, d].wait_recv()
        came[cls][1, d].wait_recv()
        mine = prow(cls, 0, d)
        total = mine[...].astype(F32) + rc3[cls, d].astype(F32) + rd3[cls, d].astype(F32)
        mine[...] = total.astype(BF)

    legs = [{} for _ in range(3)]
    for cls in range(3):
        right, left = near_by(cls, 1)
        finish_row(cls, 2)
        far_row = prow(cls, 0, 2)
        legs[cls][0] = back(cls, 1, 0, half(far_row, 1, 0), ra2.at[cls], right)
        legs[cls][1] = back(cls, 1, 1, half(far_row, 1, 1), rb2.at[cls], left)
    for cls in range(3):
        right, left = near_by(cls, 1)
        finish_row(cls, 1)
        legs[cls][2] = back(cls, 1, 2, half(prow(cls, 0, 1), 1, 1), half(rc2.at[cls], 1, 1), right)
        finish_row(cls, 3)
        legs[cls][3] = back(cls, 1, 3, half(prow(cls, 0, 3), 1, 0), half(rd2.at[cls], 1, 0), left)
    for cls in range(3):
        finish_row(cls, 0)
    for cls in range(3):
        right, left = near_by(cls, 1)
        legs[cls][0].wait_recv()
        add(half(prow(cls, 0, 1), 1, 0), ra2.at[cls])
        legs[cls][4] = back(cls, 1, 4, half(prow(cls, 0, 1), 1, 0), half(rc2.at[cls], 1, 0), right)
        legs[cls][1].wait_recv()
        add(half(prow(cls, 0, 3), 1, 1), rb2.at[cls])
        legs[cls][5] = back(cls, 1, 5, half(prow(cls, 0, 3), 1, 1), half(rd2.at[cls], 1, 1), left)
    tl[2, pos["y"]] = tap_sum(1, tcp, 4)
    tcp = tap_send(2, line["y"], pos["y"])
    fgx = pass_on(fg_half, mid_c, land_c, 1)
    feat_part(range(2, 6))
    low = []

    def part_of(cls, d):
        i2, i1, i0 = index[cls]
        return p.at[cls, i2, i1, off(i0, d)]

    for cls in range(3):
        for k in range(2, 6):
            legs[cls][k].wait_recv()
        mine = prow(cls, 0, 0)
        total = mine[...].astype(F32) + rc2[cls].astype(F32) + rd2[cls].astype(F32)
        mine[...] = total.astype(BF)
        low.append(
            [
                back(cls, 0, d, part_of(cls, d), rz.at[cls, d - 1], shifted(pos, ORDERS[cls][0], d))
                for d in (1, 2, 3)
            ]
        )
    tl[3, pos["z"]] = tap_sum(2, tcp, 4)
    tcp = tap_send(3, line["z"], pos["z"])
    feat_part(range(6, 8))
    store(1, fgrad_ref, fgrad_hbm)
    for cls in range(3):
        total = part_of(cls, 0)[...].astype(F32)
        for k in range(3):
            low[cls][k].wait_recv()
            total = total + rz[cls, k].astype(F32)
        blk[cls * 16 : (cls + 1) * 16, :] = total

    for q in range(8):
        stage2[q, 0:6, :] = blk[q * 6 : (q + 1) * 6, :]
        stage2[q, 6:8, :] = jnp.zeros((2, 512), F32)
    final = []
    for i in range(1, 8):
        q = lax.rem(w + i, 8)
        final.append(push(stage2.at[q], land2.at[w], s02.at[i], r02.at[i], (n, q)))
    land2[w] = stage2[w]
    tout_ref[...] = tap_sum(3, tcp, 4)[0:3]
    store(3, tout_ref, tout_hbm)
    for cp in fgx:
        cp.wait_recv()
    unpack(land_c)
    fgout_ref[...] = channels(0).astype(BF)
    store(2, fgout_ref, fgout_hbm)
    for cp in final:
        cp.wait_recv()
    for q in range(8):
        grad_ref[:, q * 512 : (q + 1) * 512] = land2[q, 0:6, :]
    store(4, grad_ref, grad_hbm)
    for cp in started:
        cp.wait_send()
    for cp in stores:
        cp.wait()


ANY = pl.BlockSpec(memory_space=pl.ANY)


def hyena(in_proj, features, taps, out_grad, long_filter):
    sem = pltpu.SemaphoreType.DMA
    vm = pltpu.VMEM
    tile = (128, 8, 128)
    cut = (16, 8, 8, 128)
    return pl.pallas_call(
        hyena_kernel,
        out_shape=(
            jax.ShapeDtypeStruct((256, 128), BF),
            jax.ShapeDtypeStruct((4096, 128), BF),
            jax.ShapeDtypeStruct((256, 128), BF),
            jax.ShapeDtypeStruct((3, 768), F32),
            jax.ShapeDtypeStruct((6, 4096), F32),
        ),
        in_specs=[ANY] * 5,
        out_specs=(ANY,) * 5,
        scratch_shapes=[
            vm((256, 128), BF), vm((4096, 128), BF), vm((256, 128), BF), vm((3, 768), F32), vm((6, 4096), F32), sem((5,)),
            vm((6, 4096), BF), vm((4096, 128), BF), vm((3, 768), F32), vm((256, 128), BF), vm((256, 128), BF),
            vm((8, 8, 512), F32), vm((8, 8, 512), F32), vm((48, 512), F32),
            vm((16, 4096), BF), vm((2, 16, 4096), BF), vm((4096, 256), BF),
            vm((3, 2, 4, 4, 4, 16, 512), BF), vm((4096, 128), BF),
            vm((768, 128), F32), vm((768, 128), F32), vm((768, 128), F32),
            vm((1024, 128), F32),
        ]
        + [vm(cut, BF)] * 2
        + [vm(tile, BF)] * 4
        + [vm(cut, BF)] * 2
        + [
            vm((256, 128), BF), vm((2, 128, 128), F32), vm((2, 128, 128), F32),
            vm((3, 256, 128), F32), vm((3, 256, 128), F32),
            vm((1024, 2048), BF), vm((1024, 2048), BF), vm((2048, 256), BF), vm((2, 2048, 128), BF),
            vm((768, 128), BF),
            vm((768, 128), BF), vm((384, 256), BF), vm((3, 4, 4, 4, 16, 512), BF),
            vm((3, 2, 4, 16, 512), BF), vm((3, 2, 4, 16, 512), BF),
            vm((3, 4, 4, 16, 512), BF), vm((3, 4, 4, 16, 512), BF),
            vm((3, 2, 16, 512), BF), vm((3, 2, 16, 512), BF),
            vm((3, 4, 16, 512), BF), vm((3, 4, 16, 512), BF),
            vm((3, 3, 16, 512), BF), vm((8, 16, 8, 128), BF), vm((8, 16, 8, 128), BF),
            vm((8, 8, 512), F32), vm((8, 8, 512), F32), vm((4, 4, 8, 768), F32), vm((128, 768), BF),
            sem((5,)), sem((8,)), sem((8,)),
            sem((3, 3, 12)), sem((3, 3, 12)), sem((3, 4)), sem((3, 4)),
            sem((2,)), sem((2,)), sem, sem, sem((4,)), sem((4,)), sem, sem,
            sem, sem, sem((3, 3, 12)), sem((3, 3, 12)), sem((8,)), sem((8,)), sem((4, 3)), sem((4, 3)),
            pltpu.SemaphoreType.REGULAR((3,)),
            sem((2, 8)), sem((2, 8)), sem((2, 16)), sem((2, 16)),
        ],
        compiler_params=pltpu.CompilerParams(
            collective_id=1, has_side_effects=True, vmem_limit_bytes=58 * 1024 * 1024
        ),
        name="hyena",
    )(in_proj, features, taps, out_grad, long_filter)


def copy_kernel(*refs):
    sources, targets, held, (came, left) = refs[:5], refs[5:10], refs[10:15], refs[15:]
    inward = [pltpu.make_async_copy(sources[k], held[k], came.at[k]) for k in range(5)]
    outward = [pltpu.make_async_copy(held[k], targets[k], left.at[k]) for k in range(5)]
    for cp in inward:
        cp.start()
    for k in range(5):
        inward[k].wait()
        outward[k].start()
    for cp in outward:
        cp.wait()


def settle(arrays):
    return pl.pallas_call(
        copy_kernel,
        out_shape=tuple(jax.ShapeDtypeStruct(a.shape, a.dtype) for a in arrays),
        in_specs=[ANY] * 5,
        out_specs=(ANY,) * 5,
        scratch_shapes=[pltpu.VMEM(a.shape, a.dtype) for a in arrays]
        + [pltpu.SemaphoreType.DMA((5,)), pltpu.SemaphoreType.DMA((5,))],
        name="settle",
    )(*arrays)


def local(features, in_proj, short_taps, long_filter, out_grad):
    return settle(hyena(in_proj, features, short_taps, out_grad, long_filter))


def solution(mesh):
    tokens = P(None, AXES)
    rows = P(AXES, None)
    return jax.shard_map(
        local,
        mesh=mesh,
        in_specs=(tokens, rows, P(), tokens, tokens),
        out_specs=(tokens, tokens, tokens, P(), rows),
        check_vma=False,
    )
```

```python
import math

import jax
import jax.numpy as jnp
from jax import lax
from jax.experimental import pallas as pl
from jax.experimental.pallas import tpu as pltpu
from jax.sharding import PartitionSpec as P

MESH = pl.DeviceIdType.MESH
BF = jnp.bfloat16
F32 = jnp.float32
ORDERS = (("x", "y", "z"), ("y", "z", "x"), ("z", "x", "y"))
AXES = ("narrow", "wide")


def place(pos):
    y = pos["y"]
    return (pos["z"] * 4 + lax.rem(y, 2) * 2 + pos["c"], (y // 2) * 4 + pos["x"])


def position():
    n = lax.axis_index("narrow")
    w = lax.axis_index("wide")
    pos = {
        "x": lax.rem(w, 4),
        "y": (w // 4) * 2 + lax.rem(n // 2, 2),
        "z": n // 4,
        "c": lax.rem(n, 2),
    }
    return n, w, pos


def shifted(pos, axis, by):
    other = dict(pos)
    other[axis] = lax.rem(pos[axis] + by + 4, 4)
    return place(other)


def other_core(pos):
    other = dict(pos)
    other["c"] = 1 - pos["c"]
    return place(other)


def shard_id(s):
    return (s // 8, lax.rem(s, 8))


def remote(src, dst, send, recv, device):
    return pltpu.make_async_remote_copy(
        src_ref=src, dst_ref=dst, send_sem=send, recv_sem=recv, device_id=device, device_id_type=MESH
    )


def greet(devices):
    barrier = pltpu.get_barrier_semaphore()
    for device in devices:
        pl.semaphore_signal(barrier, inc=1, device_id=device, device_id_type=MESH)
    pl.semaphore_wait(barrier, len(devices))


def piece_index(cls, z, yh, yl, x):
    at = {"x": x, "y": yh * 2 + yl, "z": z}
    d0, d1, d2 = ORDERS[cls]
    return (at[d2], at[d1], at[d0])


def dims(a, b):
    return (((a,), (b,)), ((), ()))


def lanes(rows):
    return lax.broadcasted_iota(jnp.int32, (rows, 128), 1)


def one_hot(rows, cols, test):
    r = lax.broadcasted_iota(jnp.int32, (rows, cols), 0)
    c = lax.broadcasted_iota(jnp.int32, (rows, cols), 1)
    return jnp.where(test(r, c), 1.0, 0.0).astype(BF)


def wide_block(g_ref, cls, yh, x):
    parts = []
    for z in range(4):
        for yl in range(2):
            for core in range(2):
                i2, i1, i0 = piece_index(cls, z, yh, yl, x)
                parts.append(g_ref[cls, core, i2, i1, i0])
    return jnp.concatenate(parts, axis=0)


def half(ref, phase, k):
    if phase == 0:
        return ref.at[:, pl.ds(k * 256, 256)]
    return ref.at[pl.ds(k * 2, 2)]


def build_toeplitz(tt, h_ref, ch):
    lane = lanes(128)
    row = lax.broadcasted_iota(jnp.int32, (128, 128), 0)
    upper = lane >= row

    def rolled(k):
        taps = jnp.broadcast_to(h_ref[ch, pl.ds(k, 1), :], (128, 128))
        return pltpu.roll(taps, 0, 1, stride=1, stride_axis=0)

    @pl.loop(0, 8)
    def _(g):
        prev = jnp.where(g > 0, rolled(jnp.maximum(16 * g - 1, 0)), 0.0)
        at = pl.ds(pl.multiple_of(g * 128, 128), 128)
        for i in range(16):
            cur = rolled(16 * g + i)
            tt[at, i * 128 : (i + 1) * 128] = jnp.where(upper, cur, prev).astype(BF)
            prev = cur


def spread_blocks(xs, col, x):
    lane = lanes(128)
    for i in range(16):
        moved = pltpu.roll(x, i, 1) if i else x
        xs[i * 128 : (i + 1) * 128, col * 128 : (col + 1) * 128] = jnp.where(lane < i, 0.0, moved).astype(BF)


def toeplitz_product(tt, xs, cols):
    lane = lanes(128)
    out = jnp.dot(tt[...], xs[:, 0 : cols * 128], preferred_element_type=F32)
    results = []
    for c in range(cols):
        at = slice(c * 128, (c + 1) * 128)
        acc = out[896:1024, at]
        for g in range(6, -1, -1):
            acc = jnp.where(lane < 16, 0.0, pltpu.roll(acc, 16, 1)) + out[g * 128 : (g + 1) * 128, at]
        results.append(acc.astype(BF))
    return results


def hyena_kernel(
    proj_hbm, feat_hbm, taps_hbm, og_hbm, lf_hbm,
    mixed_hbm, fgrad_hbm, fgout_hbm, tout_hbm, grad_hbm,
    mixed_ref, fgrad_ref, fgout_ref, tout_ref, grad_ref, outs,
    proj_ref, feat_ref, taps_ref, og_ref, lf_ref,
    stage, land, blk, rows, hland, fh, g_ref, fo_ref, p_ref, halo_ref, tcol,
    rowbuf, send_f, land_f, send_a, land_a, send_b, land_b, send_c, land_c,
    ogn, hf, gf, feat, featn, tt, cots, ahead_ref, xs, xc, pd_ref,
    pdo, pdc, p, ra3, rb3, rc3, rd3, ra2, rb2, rc2, rd2, rz, mid_f, mid_c,
    stage2, land2, tl, pdt, rowf, both,
    ins, s0, r0, ss, rs, ds, dr, hs, hr, fs, fr, xsend, xrecv, os, orr,
    ps, pr, ss2, rs2, s02, r02, tsn, trc, near, xs1, xr1, xs2, xr2,
):
    n, w, pos = position()
    c = pos["c"]
    s = n * 8 + w
    right_shard = shard_id(lax.rem(s + 1, 128))
    left_shard = shard_id(lax.rem(s + 127, 128))
    wide_peers = [(n, lax.rem(w + i, 8)) for i in range(1, 8)]
    line = {a: [shifted(pos, a, d) for d in (1, 2, 3)] for a in "xyz"}
    core = other_core(pos)
    copies = [
        pltpu.make_async_copy(a, b, ins.at[k])
        for k, (a, b) in enumerate(
            ((proj_hbm, proj_ref), (feat_hbm, feat_ref), (taps_hbm, taps_ref), (og_hbm, og_ref), (lf_hbm, lf_ref))
        )
    ]
    for cp in copies:
        cp.start()
    barrier = pltpu.get_barrier_semaphore()
    greeted = wide_peers + line["y"] + line["z"] + [core, right_shard, left_shard]
    for device in greeted:
        pl.semaphore_signal(barrier, inc=1, device_id=device, device_id_type=MESH)
    copies[0].wait()
    for q in range(8):
        stage[q, 0:6, :] = proj_ref[:, q * 512 : (q + 1) * 512].astype(F32)
        stage[q, 6:8, :] = jnp.zeros((2, 512), F32)
    pl.semaphore_wait(barrier, len(greeted))

    def tell(k, devices):
        for device in devices:
            pl.semaphore_signal(near.at[k], inc=1, device_id=device, device_id_type=MESH)

    started = []
    stores = []

    def store(k, src, dst):
        cp = pltpu.make_async_copy(src, dst, outs.at[k])
        cp.start()
        stores.append(cp)

    def push(src, dst, a, b, device):
        cp = remote(src, dst, a, b, device)
        cp.start()
        started.append(cp)
        return cp

    first = []
    for i in range(1, 8):
        q = lax.rem(w + i, 8)
        first.append(push(stage.at[q], land.at[w], s0.at[i], r0.at[i], (n, q)))
    tell(0, line["x"])
    land[w] = stage[w]
    for cp in first:
        cp.wait_recv()
    for q in range(8):
        blk[q * 6 : (q + 1) * 6, :] = land[q, 0:6, :]

    index = [[pos[a] for a in reversed(order)] for order in ORDERS]
    for cls in range(3):
        i2, i1, i0 = index[cls]
        g_ref[cls, c, i2, i1, i0] = blk[cls * 16 : (cls + 1) * 16, :].astype(BF)

    d2d = []

    def cross(cls, j, k):
        ref = g_ref.at[cls, c, j]
        d2d.append(push(ref, ref, ds.at[cls, k], dr.at[cls, k], core))

    def exchange(src, dst, k):
        ww = [lax.rem(w + j, 8) for j in range(8)]
        for j in range(1, 8):
            remote(src.at[n * 8 + ww[j]], dst.at[s], xsend.at[k], xrecv.at[k], (n, ww[j])).start()

        @pl.loop(1, 16)
        def _(i):
            nn = lax.rem(n + i, 16)
            for j in range(8):
                remote(src.at[nn * 8 + ww[j]], dst.at[s], xsend.at[k], xrecv.at[k], (nn, ww[j])).start()

        dst[s] = src[s]
        whole = pl.ds(0, 127)
        cp = remote(src.at[whole], dst.at[whole], xsend.at[k], xrecv.at[k], (n, w))
        started.append(cp)
        return cp

    def hand(src, mid, k):
        cps = []
        for i in range(1, 8):
            q = lax.rem(w + i, 8)
            cps.append(push(src.at[:, q], mid.at[w], xs1.at[k, i], xr1.at[k, i], (n, q)))
        mid[w] = src[:, w]
        return cps

    def pass_on(cps, mid, dst, k):
        for cp in cps:
            cp.wait_recv()
        out = []
        for i in range(1, 16):
            m = lax.rem(n + i, 16)
            out.append(push(mid.at[:, m], dst.at[n], xs2.at[k, i], xr2.at[k, i], (m, w)))
        dst[n] = mid[:, n]
        return out

    def pack(buf, parts):
        for r, value in parts.items():
            rowbuf[pl.ds(r, 128, stride=8), :] = value
        buf[...] = rowbuf[...].reshape(buf.shape).astype(BF)

    def unpack(buf):
        rowbuf[...] = buf[...].astype(F32).reshape(1024, 128)

    def plane(r):
        return rowbuf[pl.ds(r, 128, stride=8), :]

    def piece(cls, i2, i1, i0):
        return g_ref.at[cls, c, i2, i1, i0]

    def row_of(cls, i2, i1):
        return g_ref.at[cls, c, i2, i1]

    def near_by(cls, phase):
        axis = ORDERS[cls][phase]
        return shifted(pos, axis, 1), shifted(pos, axis, -1)

    def ring(cls, phase, k, ref, device):
        return push(ref, ref, ss.at[cls, phase, k], rs.at[cls, phase, k], device)

    def off(i, d):
        return lax.rem(i + d, 4)

    legs = []
    for cls in range(3):
        mine = piece(cls, *index[cls])
        legs.append([ring(cls, 0, d, mine, shifted(pos, ORDERS[cls][0], d)) for d in (1, 2, 3)])
    pl.semaphore_wait(near.at[0], 3)
    tell(1, line["y"])
    copies[1].wait()
    sel = one_hot(
        16, 128, lambda r, l: ((r < 2) & (l == r + 126)) | ((r >= 2) & (r < 4) & (l == r - 2))
    )
    edge = lax.dot_general(sel, feat_ref[...], dims(1, 1), preferred_element_type=F32)
    for k in range(4):
        for q in range(8):
            at = (k % 2) * 8 + q
            rowf[k // 2, at : at + 1, :] = edge[k : k + 1, q * 512 : (q + 1) * 512]
    rows[...] = rowf[...].astype(BF)
    firsts, legs = legs, []
    far = [[None] * 4 for _ in range(3)]

    def spread_row(cls, d):
        i2, i1, _ = index[cls]
        right, left = near_by(cls, 2)
        ref = row_of(cls, i2, off(i1, d))
        far[cls][d] = (ring(cls, 2, 2 * d, ref, right), ring(cls, 2, 2 * d + 1, ref, left))

    for cls in range(3):
        i2, i1, _ = index[cls]
        for cp in firsts[cls]:
            cp.wait_recv()
        right, left = near_by(cls, 1)
        mine = row_of(cls, i2, i1)
        legs.append((ring(cls, 1, 0, mine, right), ring(cls, 1, 1, mine, left)))
    for cls in range(3):
        spread_row(cls, 0)
    pl.semaphore_wait(near.at[1], 3)
    tell(2, [core])
    copies[4].wait()
    lf = lf_ref[...].astype(F32)
    zero = jnp.zeros((128, 128), F32)
    pack(send_f, {0: lf[0:128], 1: lf[128:256], **{r: zero for r in range(2, 8)}})
    lf_half = hand(send_f, mid_f, 0)
    ha = push(rows.at[0], hland.at[0], hs.at[0], hr.at[0], right_shard)
    hb = push(rows.at[1], hland.at[1], hs.at[1], hr.at[1], left_shard)
    halves = []
    for cls in range(3):
        i2, i1, _ = index[cls]
        right, left = near_by(cls, 1)
        legs[cls][0].wait_recv()
        e = ring(cls, 1, 2, half(row_of(cls, i2, off(i1, 3)), 1, 0), right)
        legs[cls][1].wait_recv()
        f = ring(cls, 1, 3, half(row_of(cls, i2, off(i1, 1)), 1, 1), left)
        halves.append((e, f))
    for cls in range(3):
        spread_row(cls, 3)
        spread_row(cls, 1)
    pl.semaphore_wait(near.at[2], 1)
    for cls in range(3):
        for cp in halves[cls]:
            cp.wait_recv()
        spread_row(cls, 2)
    for cls in range(3):
        cross(cls, index[cls][0], 0)
    lfx = pass_on(lf_half, mid_f, land_f, 0)
    fh[:, 0:128] = feat_ref[...]
    copies[2].wait()
    tc = jnp.concatenate([taps_ref[...], jnp.zeros((125, 768), F32)], axis=0)
    for k in range(6):
        tcol[k * 128 : (k + 1) * 128, :] = tc[:, k * 128 : (k + 1) * 128].T
    ha.wait_recv()
    hb.wait_recv()
    rowf[...] = hland[...].astype(F32)
    both[...] = jnp.zeros((16, 4096), F32)
    for k in range(4):
        for q in range(8):
            at = (k % 2) * 8 + q
            both[k : k + 1, q * 512 : (q + 1) * 512] = rowf[k // 2, at : at + 1, :]
    lo = jnp.where(s > 0, 0, 2)
    hi = jnp.where(s < 127, 4, 2)
    spread = one_hot(16, 128, lambda r, l: (r == l) & (r >= lo) & (r < hi))
    fh[:, 128:256] = lax.dot_general(
        both[...].astype(BF), spread, dims(0, 0), preferred_element_type=F32
    ).astype(BF)
    relays = []
    for d, k in ((0, 0), (3, 1), (1, 0), (2, 1)):
        for cls in range(3):
            i2, i1, _ = index[cls]
            far[cls][d][k].wait_recv()
            ref = row_of(cls, off(i2, 1 if k else 3), off(i1, d))
            relays.append(ring(cls, 2, 8 + d, ref, near_by(cls, 2)[k]))
    for cls in range(3):
        for d, k in ((0, 1), (3, 0), (1, 1), (2, 0)):
            far[cls][d][k].wait_recv()
        cross(cls, off(index[cls][0], 3), 1)
        cross(cls, off(index[cls][0], 1), 2)
    for cp in lfx:
        cp.wait_recv()
    unpack(land_f)
    for ch in range(2):
        hf[ch] = plane(ch)
    build_toeplitz(tt.at[0], hf, 0)
    for cp in relays:
        cp.wait_recv()
    for cls in range(3):
        cross(cls, off(index[cls][0], 2), 3)
    fcp = push(feat_ref, fo_ref, fs, fr, core)
    copies[3].wait()
    ocp = push(og_ref, ogn, os, orr, left_shard)
    for cp in d2d:
        cp.wait_recv()

    for cls in range(3):
        acc = None
        for q in range(8):
            lhs = wide_block(g_ref, cls, q // 4, q % 4)
            term = jnp.dot(lhs, fh[q * 512 : (q + 1) * 512, :], preferred_element_type=F32)
            acc = term if acc is None else acc + term
        for m in range(16):
            at = slice(m * 48 + cls * 16, m * 48 + cls * 16 + 16)
            p_ref[at, :] = acc[m * 16 : (m + 1) * 16, 0:128]
            halo_ref[at, :] = acc[m * 16 : (m + 1) * 16, 128:256]

    lane = lanes(256)
    for part in range(3):
        at = slice(part * 256, (part + 1) * 256)
        v = p_ref[at, :]
        halo = halo_ref[at, :]
        t0, t1, t2 = tcol[at, 0:1], tcol[at, 1:2], tcol[at, 2:3]
        v1 = jnp.where(lane < 1, pltpu.roll(halo, 127, 1), pltpu.roll(v, 1, 1))
        v2 = jnp.where(lane < 2, halo, pltpu.roll(v, 2, 1))
        feat[part] = t0 * v + t1 * v1 + t2 * v2
        n1 = jnp.where(lane < 1, pltpu.roll(v, 1, 1), pltpu.roll(halo, 127, 1))
        featn[part] = t0 * pltpu.roll(halo, 126, 1) + t1 * n1 + t2 * pltpu.roll(v, 2, 1)
    og = og_ref[...].astype(F32)
    gated = feat[1] * feat[2]
    cot = og * feat[0]
    pack(send_a, {0: gated[0:128], 1: gated[128:256], 2: cot[0:128], 3: cot[128:256]})
    go = exchange(send_a, land_a, 1)
    build_toeplitz(tt.at[1], hf, 1)
    go.wait_recv()
    unpack(land_a)

    anti = one_hot(128, 128, lambda r, l: r + l == 127)
    row = lax.broadcasted_iota(jnp.int32, (128, 128), 0)
    lane1 = lanes(128)
    for ch in range(2):
        gf[ch] = plane(ch)
        cots[ch] = plane(2 + ch).astype(BF)
    ahead_ref[...] = jnp.zeros((128, 128), F32)

    @pl.loop(0, 2)
    def _(ch):
        xg = lax.dot_general(anti, gf[ch].astype(BF), dims(1, 1), preferred_element_type=F32)
        back_in = lax.dot_general(cots[ch], anti, dims(0, 0), preferred_element_type=F32)
        spread_blocks(xs, 1, xg)
        spread_blocks(xs, 0, back_in)
        xc[ch] = xs[:, 0:128]
        yc, yg = toeplitz_product(tt.at[ch], xs, 2)
        conv = lax.dot_general(yg, anti, dims(0, 0), preferred_element_type=F32)
        gg = lax.dot_general(anti, yc, dims(1, 1), preferred_element_type=F32)
        rowbuf[pl.ds(ch, 128, stride=8), :] = conv
        rowbuf[pl.ds(2 + ch, 128, stride=8), :] = gg
        for r, value in ((0, conv), (4, gg)):
            nxt = pltpu.roll(jnp.where(row < 127, pltpu.roll(value, 127, 0), 0.0), r + 2 * ch, 1)
            keep = (lane1 >= r + 2 * ch) & (lane1 < r + 2 * ch + 2)
            ahead_ref[...] = jnp.where(keep, nxt, ahead_ref[...])

    ahead = ahead_ref[...]
    pack(send_b, {4: ahead})
    ret = exchange(send_b, land_b, 2)
    build_toeplitz(tt.at[0], gf, 0)
    ocp.wait_recv()
    ret.wait_recv()
    unpack(land_b)

    def channels(r):
        return jnp.concatenate([plane(r), plane(r + 1)], axis=0)

    conv, gg = channels(0), channels(2)
    ahead = plane(4)
    convn = jnp.concatenate([ahead, pltpu.roll(ahead, 126, 1)], axis=0)
    ggn = jnp.concatenate([pltpu.roll(ahead, 124, 1), pltpu.roll(ahead, 122, 1)], axis=0)
    mixed_ref[...] = (feat[0] * conv).astype(BF)
    store(0, mixed_ref, mixed_hbm)
    ogv = ogn[...].astype(F32)
    last = s == 127

    def derivative(part):
        if part == 0:
            return og * conv
        return gg * feat[3 - part]

    for part in range(3):
        at = slice(part * 256, (part + 1) * 256)
        fd = derivative(part)
        fdn = ogv * convn if part == 0 else ggn * featn[3 - part]
        fdn = jnp.where(last, 0.0, fdn)
        t0, t1, t2 = tcol[at, 0:1], tcol[at, 1:2], tcol[at, 2:3]
        f1 = jnp.where(lane < 127, pltpu.roll(fd, 127, 1), pltpu.roll(fdn, 127, 1))
        f2 = jnp.where(lane < 126, pltpu.roll(fd, 126, 1), pltpu.roll(fdn, 126, 1))
        pd_ref[at, :] = (t0 * fd + t1 * f1 + t2 * f2).astype(BF)
    pcp = push(pd_ref, pdo, ps, pr, core)

    for part in range(3):
        at = slice(part * 256, (part + 1) * 256)
        fd = derivative(part)
        v = p_ref[at, :]
        halo = halo_ref[at, :]
        v1 = jnp.where(lane < 1, pltpu.roll(halo, 127, 1), pltpu.roll(v, 1, 1))
        v2 = jnp.where(lane < 2, halo, pltpu.roll(v, 2, 1))
        total = jnp.zeros((256, 128), F32)
        for k, q in enumerate((v, v1, v2)):
            total = jnp.where(lane == k, jnp.sum(fd * q, axis=1, keepdims=True), total)
        tl[0, c, :, at] = total.T[0:8, :]

    def tap_send(k, peers, slot):
        return [
            push(tl.at[k, slot], tl.at[k, slot], tsn.at[k, i], trc.at[k, i], device)
            for i, device in enumerate(peers)
        ]

    def tap_sum(k, cps, count):
        for cp in cps:
            cp.wait_recv()
        total = tl[k, 0]
        for i in range(1, count):
            total = total + tl[k, i]
        return total

    tcp = tap_send(0, [core], c)
    fcp.wait_recv()
    pcp.wait_recv()
    for cls in range(3):
        for z in range(4):
            for yl in range(2):
                at = pl.ds(pl.multiple_of((z * 4 + yl * 2 + c) * 48 + cls * 16, 16), 16)
                to = cls * 128 + z * 32 + yl * 16
                pdc[to : to + 16, 0:128] = pd_ref[at, :]
                pdc[to : to + 16, 128:256] = pdo[at, :]

    def add(dst, src):
        dst[...] = (dst[...].astype(F32) + src[...].astype(F32)).astype(BF)

    def feat_part(qs):
        @pl.loop(qs.start, qs.stop)
        def _(q):
            total = None
            for cls in range(3):
                term = lax.dot_general(
                    pdt[:, cls * 256 : (cls + 1) * 256], wide_block(g_ref, cls, q // 4, lax.rem(q, 4)), dims(1, 0),
                    preferred_element_type=F32,
                )
                total = term if total is None else total + term
            fgrad_ref[pl.ds(pl.multiple_of(q * 512, 512), 512), :] = total.T.astype(BF)

    def back(cls, phase, k, src, dst, device):
        return push(src, dst, ss2.at[cls, phase, k], rs2.at[cls, phase, k], device)

    def prow(cls, d2, d1):
        i2, i1, _ = index[cls]
        return p.at[cls, off(i2, d2), off(i1, d1)]

    relay = ((2, 1), (0, 3))
    hops, came = [], []
    for cls in range(3):
        hops.append({})
        came.append({})
    for cls in range(3):

        @pl.loop(0, 8)
        def _(q):
            cols = pl.ds(pl.multiple_of(q * 512, 512), 512)
            part = lax.dot_general(
                pdc[cls * 128 : (cls + 1) * 128, :],
                jnp.concatenate([feat_ref[cols, :], fo_ref[cols, :]], axis=1),
                dims(1, 1),
                preferred_element_type=F32,
            ).astype(BF)
            for z in range(4):
                for yl in range(2):
                    k = z * 32 + yl * 16
                    i2, i1, i0 = piece_index(cls, z, q // 4, yl, lax.rem(q, 4))
                    p[cls, i2, i1, i0] = part[k : k + 16, :]
        right, left = near_by(cls, 2)
        for j in range(2):
            hops[cls][0, j] = back(cls, 2, j, prow(cls, 2, relay[j][0]), ra3.at[cls, j], right)
            hops[cls][1, j] = back(cls, 2, 2 + j, prow(cls, 2, relay[j][1]), rb3.at[cls, j], left)
        for j in range(2):
            d = relay[j][0]
            came[cls][1, d] = back(cls, 2, 8 + d, prow(cls, 3, d), rd3.at[cls, d], left)
            d = relay[j][1]
            came[cls][0, d] = back(cls, 2, 4 + d, prow(cls, 1, d), rc3.at[cls, d], right)
    pdt[...] = jnp.concatenate(
        [
            pd_ref[m * 48 + cls * 16 : m * 48 + cls * 16 + 16, :].astype(F32)
            for cls in range(3)
            for m in range(16)
        ],
        axis=0,
    ).T.astype(BF)
    build_toeplitz(tt.at[1], gf, 1)
    for j in range(2):
        for cls in range(3):
            right, left = near_by(cls, 2)
            d = relay[j][0]
            hops[cls][0, j].wait_recv()
            add(prow(cls, 1, d), ra3.at[cls, j])
            came[cls][0, d] = back(cls, 2, 4 + d, prow(cls, 1, d), rc3.at[cls, d], right)
            d = relay[j][1]
            hops[cls][1, j].wait_recv()
            add(prow(cls, 3, d), rb3.at[cls, j])
            came[cls][1, d] = back(cls, 2, 8 + d, prow(cls, 3, d), rd3.at[cls, d], left)
    tl[1, pos["x"]] = tap_sum(0, tcp, 2)
    tcp = tap_send(1, line["x"], pos["x"])

    @pl.loop(0, 2)
    def _(ch):
        (y,) = toeplitz_product(tt.at[ch], xc.at[ch], 1)
        rowbuf[pl.ds(ch, 128, stride=8), :] = lax.dot_general(anti, y, dims(1, 1), preferred_element_type=F32)

    pack(send_c, {})
    fg_half = hand(send_c, mid_c, 1)
    feat_part(range(2))

    def finish_row(cls, d):
        came[cls][0, d].wait_recv()
        came[cls][1, d].wait_recv()
        mine = prow(cls, 0, d)
        total = mine[...].astype(F32) + rc3[cls, d].astype(F32) + rd3[cls, d].astype(F32)
        mine[...] = total.astype(BF)

    legs = [{} for _ in range(3)]
    for cls in range(3):
        right, left = near_by(cls, 1)
        finish_row(cls, 2)
        far_row = prow(cls, 0, 2)
        legs[cls][0] = back(cls, 1, 0, half(far_row, 1, 0), ra2.at[cls], right)
        legs[cls][1] = back(cls, 1, 1, half(far_row, 1, 1), rb2.at[cls], left)
    for cls in range(3):
        right, left = near_by(cls, 1)
        finish_row(cls, 1)
        legs[cls][2] = back(cls, 1, 2, half(prow(cls, 0, 1), 1, 1), half(rc2.at[cls], 1, 1), right)
        finish_row(cls, 3)
        legs[cls][3] = back(cls, 1, 3, half(prow(cls, 0, 3), 1, 0), half(rd2.at[cls], 1, 0), left)
    for cls in range(3):
        finish_row(cls, 0)
    for cls in range(3):
        right, left = near_by(cls, 1)
        legs[cls][0].wait_recv()
        add(half(prow(cls, 0, 1), 1, 0), ra2.at[cls])
        legs[cls][4] = back(cls, 1, 4, half(prow(cls, 0, 1), 1, 0), half(rc2.at[cls], 1, 0), right)
        legs[cls][1].wait_recv()
        add(half(prow(cls, 0, 3), 1, 1), rb2.at[cls])
        legs[cls][5] = back(cls, 1, 5, half(prow(cls, 0, 3), 1, 1), half(rd2.at[cls], 1, 1), left)
    tl[2, pos["y"]] = tap_sum(1, tcp, 4)
    tcp = tap_send(2, line["y"], pos["y"])
    fgx = pass_on(fg_half, mid_c, land_c, 1)
    feat_part(range(2, 6))
    low = []

    def part_of(cls, d):
        i2, i1, i0 = index[cls]
        return p.at[cls, i2, i1, off(i0, d)]

    for cls in range(3):
        for k in range(2, 6):
            legs[cls][k].wait_recv()
        mine = prow(cls, 0, 0)
        total = mine[...].astype(F32) + rc2[cls].astype(F32) + rd2[cls].astype(F32)
        mine[...] = total.astype(BF)
        low.append(
            [
                back(cls, 0, d, part_of(cls, d), rz.at[cls, d - 1], shifted(pos, ORDERS[cls][0], d))
                for d in (1, 2, 3)
            ]
        )
    tl[3, pos["z"]] = tap_sum(2, tcp, 4)
    tcp = tap_send(3, line["z"], pos["z"])
    feat_part(range(6, 8))
    store(1, fgrad_ref, fgrad_hbm)
    for cls in range(3):
        total = part_of(cls, 0)[...].astype(F32)
        for k in range(3):
            low[cls][k].wait_recv()
            total = total + rz[cls, k].astype(F32)
        blk[cls * 16 : (cls + 1) * 16, :] = total

    for q in range(8):
        stage2[q, 0:6, :] = blk[q * 6 : (q + 1) * 6, :]
        stage2[q, 6:8, :] = jnp.zeros((2, 512), F32)
    final = []
    for i in range(1, 8):
        q = lax.rem(w + i, 8)
        final.append(push(stage2.at[q], land2.at[w], s02.at[i], r02.at[i], (n, q)))
    land2[w] = stage2[w]
    tout_ref[...] = tap_sum(3, tcp, 4)[0:3]
    store(3, tout_ref, tout_hbm)
    for cp in fgx:
        cp.wait_recv()
    unpack(land_c)
    fgout_ref[...] = channels(0).astype(BF)
    store(2, fgout_ref, fgout_hbm)
    for cp in final:
        cp.wait_recv()
    for q in range(8):
        grad_ref[:, q * 512 : (q + 1) * 512] = land2[q, 0:6, :]
    store(4, grad_ref, grad_hbm)
    for cp in started:
        cp.wait_send()
    for cp in stores:
        cp.wait()


ANY = pl.BlockSpec(memory_space=pl.ANY)


def hyena(in_proj, features, taps, out_grad, long_filter):
    sem = pltpu.SemaphoreType.DMA
    vm = pltpu.VMEM
    tile = (128, 8, 128)
    cut = (16, 8, 8, 128)
    return pl.pallas_call(
        hyena_kernel,
        out_shape=(
            jax.ShapeDtypeStruct((256, 128), BF),
            jax.ShapeDtypeStruct((4096, 128), BF),
            jax.ShapeDtypeStruct((256, 128), BF),
            jax.ShapeDtypeStruct((3, 768), F32),
            jax.ShapeDtypeStruct((6, 4096), F32),
        ),
        in_specs=[ANY] * 5,
        out_specs=(ANY,) * 5,
        scratch_shapes=[
            vm((256, 128), BF), vm((4096, 128), BF), vm((256, 128), BF), vm((3, 768), F32), vm((6, 4096), F32), sem((5,)),
            vm((6, 4096), BF), vm((4096, 128), BF), vm((3, 768), F32), vm((256, 128), BF), vm((256, 128), BF),
            vm((8, 8, 512), F32), vm((8, 8, 512), F32), vm((48, 512), F32),
            vm((2, 16, 512), BF), vm((2, 16, 512), BF), vm((4096, 256), BF),
            vm((3, 2, 4, 4, 4, 16, 512), BF), vm((4096, 128), BF),
            vm((768, 128), F32), vm((768, 128), F32), vm((768, 128), F32),
            vm((1024, 128), F32),
        ]
        + [vm(cut, BF)] * 2
        + [vm(tile, BF)] * 4
        + [vm(cut, BF)] * 2
        + [
            vm((256, 128), BF), vm((2, 128, 128), F32), vm((2, 128, 128), F32),
            vm((3, 256, 128), F32), vm((3, 256, 128), F32),
            vm((2, 1024, 2048), BF), vm((2, 128, 128), BF), vm((128, 128), F32), vm((2048, 256), BF), vm((2, 2048, 128), BF),
            vm((768, 128), BF),
            vm((768, 128), BF), vm((384, 256), BF), vm((3, 4, 4, 4, 16, 512), BF),
            vm((3, 2, 4, 16, 512), BF), vm((3, 2, 4, 16, 512), BF),
            vm((3, 4, 4, 16, 512), BF), vm((3, 4, 4, 16, 512), BF),
            vm((3, 2, 16, 512), BF), vm((3, 2, 16, 512), BF),
            vm((3, 4, 16, 512), BF), vm((3, 4, 16, 512), BF),
            vm((3, 3, 16, 512), BF), vm((8, 16, 8, 128), BF), vm((8, 16, 8, 128), BF),
            vm((8, 8, 512), F32), vm((8, 8, 512), F32), vm((4, 4, 8, 768), F32), vm((128, 768), BF), vm((2, 16, 512), F32), vm((16, 4096), F32),
            sem((5,)), sem((8,)), sem((8,)),
            sem((3, 3, 12)), sem((3, 3, 12)), sem((3, 4)), sem((3, 4)),
            sem((2,)), sem((2,)), sem, sem, sem((4,)), sem((4,)), sem, sem,
            sem, sem, sem((3, 3, 12)), sem((3, 3, 12)), sem((8,)), sem((8,)), sem((4, 3)), sem((4, 3)),
            pltpu.SemaphoreType.REGULAR((3,)),
            sem((2, 8)), sem((2, 8)), sem((2, 16)), sem((2, 16)),
        ],
        compiler_params=pltpu.CompilerParams(
            collective_id=1, has_side_effects=True, vmem_limit_bytes=58 * 1024 * 1024
        ),
        name="hyena",
    )(in_proj, features, taps, out_grad, long_filter)


def copy_kernel(*refs):
    sources, targets, held, (came, left) = refs[:5], refs[5:10], refs[10:15], refs[15:]
    inward = [pltpu.make_async_copy(sources[k], held[k], came.at[k]) for k in range(5)]
    outward = [pltpu.make_async_copy(held[k], targets[k], left.at[k]) for k in range(5)]
    for cp in inward:
        cp.start()
    for k in range(5):
        inward[k].wait()
        outward[k].start()
    for cp in outward:
        cp.wait()


def settle(arrays):
    return pl.pallas_call(
        copy_kernel,
        out_shape=tuple(jax.ShapeDtypeStruct(a.shape, a.dtype) for a in arrays),
        in_specs=[ANY] * 5,
        out_specs=(ANY,) * 5,
        scratch_shapes=[pltpu.VMEM(a.shape, a.dtype) for a in arrays]
        + [pltpu.SemaphoreType.DMA((5,)), pltpu.SemaphoreType.DMA((5,))],
        name="settle",
    )(*arrays)


def local(features, in_proj, short_taps, long_filter, out_grad):
    return settle(hyena(in_proj, features, short_taps, out_grad, long_filter))


def solution(mesh):
    tokens = P(None, AXES)
    rows = P(AXES, None)
    return jax.shard_map(
        local,
        mesh=mesh,
        in_specs=(tokens, rows, P(), tokens, tokens),
        out_specs=(tokens, tokens, tokens, P(), rows),
        check_vma=False,
    )
```

```python
import math

import jax
import jax.numpy as jnp
from jax import lax
from jax.experimental import pallas as pl
from jax.experimental.pallas import tpu as pltpu
from jax.sharding import PartitionSpec as P

MESH = pl.DeviceIdType.MESH
BF = jnp.bfloat16
F32 = jnp.float32
ORDERS = (("x", "y", "z"), ("y", "z", "x"), ("z", "x", "y"))
AXES = ("narrow", "wide")


def place(pos):
    y = pos["y"]
    return (pos["z"] * 4 + lax.rem(y, 2) * 2 + pos["c"], (y // 2) * 4 + pos["x"])


def position():
    n = lax.axis_index("narrow")
    w = lax.axis_index("wide")
    pos = {
        "x": lax.rem(w, 4),
        "y": (w // 4) * 2 + lax.rem(n // 2, 2),
        "z": n // 4,
        "c": lax.rem(n, 2),
    }
    return n, w, pos


def shifted(pos, axis, by):
    other = dict(pos)
    other[axis] = lax.rem(pos[axis] + by + 4, 4)
    return place(other)


def other_core(pos):
    other = dict(pos)
    other["c"] = 1 - pos["c"]
    return place(other)


def shard_id(s):
    return (s // 8, lax.rem(s, 8))


def remote(src, dst, send, recv, device):
    return pltpu.make_async_remote_copy(
        src_ref=src, dst_ref=dst, send_sem=send, recv_sem=recv, device_id=device, device_id_type=MESH
    )


def greet(devices):
    barrier = pltpu.get_barrier_semaphore()
    for device in devices:
        pl.semaphore_signal(barrier, inc=1, device_id=device, device_id_type=MESH)
    pl.semaphore_wait(barrier, len(devices))


def piece_index(cls, z, yh, yl, x):
    at = {"x": x, "y": yh * 2 + yl, "z": z}
    d0, d1, d2 = ORDERS[cls]
    return (at[d2], at[d1], at[d0])


def dims(a, b):
    return (((a,), (b,)), ((), ()))


def lanes(rows):
    return lax.broadcasted_iota(jnp.int32, (rows, 128), 1)


def one_hot(rows, cols, test):
    r = lax.broadcasted_iota(jnp.int32, (rows, cols), 0)
    c = lax.broadcasted_iota(jnp.int32, (rows, cols), 1)
    return jnp.where(test(r, c), 1.0, 0.0).astype(BF)


def wide_block(g_ref, cls, yh, x):
    parts = []
    for z in range(4):
        for yl in range(2):
            for core in range(2):
                i2, i1, i0 = piece_index(cls, z, yh, yl, x)
                parts.append(g_ref[cls, core, i2, i1, i0])
    return jnp.concatenate(parts, axis=0)


def half(ref, phase, k):
    if phase == 0:
        return ref.at[:, pl.ds(k * 256, 256)]
    return ref.at[pl.ds(k * 2, 2)]


def build_toeplitz(tt, h_ref, ch):
    lane = lanes(128)
    row = lax.broadcasted_iota(jnp.int32, (128, 128), 0)
    upper = lane >= row

    def rolled(k):
        taps = jnp.broadcast_to(h_ref[ch, pl.ds(k, 1), :], (128, 128))
        return pltpu.roll(taps, 0, 1, stride=1, stride_axis=0)

    @pl.loop(0, 8)
    def _(g):
        prev = jnp.where(g > 0, rolled(jnp.maximum(16 * g - 1, 0)), 0.0)
        at = pl.ds(pl.multiple_of(g * 128, 128), 128)
        for i in range(16):
            cur = rolled(16 * g + i)
            tt[at, i * 128 : (i + 1) * 128] = jnp.where(upper, cur, prev).astype(BF)
            prev = cur


def spread_blocks(xs, col, x):
    lane = lanes(128)
    for i in range(16):
        moved = pltpu.roll(x, i, 1) if i else x
        xs[i * 128 : (i + 1) * 128, col * 128 : (col + 1) * 128] = jnp.where(lane < i, 0.0, moved).astype(BF)


def toeplitz_product(tt, xs, cols):
    lane = lanes(128)
    out = jnp.dot(tt[...], xs[:, 0 : cols * 128], preferred_element_type=F32)
    results = []
    for c in range(cols):
        at = slice(c * 128, (c + 1) * 128)
        acc = out[896:1024, at]
        for g in range(6, -1, -1):
            acc = jnp.where(lane < 16, 0.0, pltpu.roll(acc, 16, 1)) + out[g * 128 : (g + 1) * 128, at]
        results.append(acc.astype(BF))
    return results


def hyena_kernel(
    proj_hbm, feat_hbm, taps_hbm, og_hbm, lf_hbm,
    mixed_hbm, fgrad_hbm, fgout_hbm, tout_hbm, grad_hbm,
    mixed_ref, fgrad_ref, fgout_ref, tout_ref, grad_ref, outs,
    proj_ref, feat_ref, taps_ref, og_ref, lf_ref,
    stage, land, blk, rows, hland, fh, g_ref, fo_ref, p_ref, halo_ref, tcol,
    rowbuf, send_f, land_f, send_a, land_a, send_b, land_b, send_c, land_c,
    ogn, hf, gf, feat, featn, tt, cots, ahead_ref, xs, xc, pd_ref,
    pdo, pdc, p, ra3, rb3, rc3, rd3, ra2, rb2, rc2, rd2, rz, mid_f, mid_c, turn_f, turn_c, rows_a, rows_b,
    stage2, land2, tl, pdt, rowf, both,
    ins, s0, r0, ss, rs, ds, dr, hs, hr, fs, fr, xsend, xrecv, os, orr,
    ps, pr, ss2, rs2, s02, r02, tsn, trc, near, xs1, xr1, xs2, xr2,
):
    n, w, pos = position()
    c = pos["c"]
    s = n * 8 + w
    right_shard = shard_id(lax.rem(s + 1, 128))
    left_shard = shard_id(lax.rem(s + 127, 128))
    wide_peers = [(n, lax.rem(w + i, 8)) for i in range(1, 8)]
    line = {a: [shifted(pos, a, d) for d in (1, 2, 3)] for a in "xyz"}
    core = other_core(pos)
    copies = [
        pltpu.make_async_copy(a, b, ins.at[k])
        for k, (a, b) in enumerate(
            ((proj_hbm, proj_ref), (feat_hbm, feat_ref), (taps_hbm, taps_ref), (og_hbm, og_ref), (lf_hbm, lf_ref))
        )
    ]
    for cp in copies:
        cp.start()
    barrier = pltpu.get_barrier_semaphore()
    greeted = wide_peers + line["y"] + line["z"] + [core, right_shard, left_shard]
    for device in greeted:
        pl.semaphore_signal(barrier, inc=1, device_id=device, device_id_type=MESH)
    copies[0].wait()
    for q in range(8):
        stage[q, 0:6, :] = proj_ref[:, q * 512 : (q + 1) * 512].astype(F32)
        stage[q, 6:8, :] = jnp.zeros((2, 512), F32)
    pl.semaphore_wait(barrier, len(greeted))

    def tell(k, devices):
        for device in devices:
            pl.semaphore_signal(near.at[k], inc=1, device_id=device, device_id_type=MESH)

    started = []
    stores = []

    def store(k, src, dst):
        cp = pltpu.make_async_copy(src, dst, outs.at[k])
        cp.start()
        stores.append(cp)

    def push(src, dst, a, b, device):
        cp = remote(src, dst, a, b, device)
        cp.start()
        started.append(cp)
        return cp

    first = []
    for i in range(1, 8):
        q = lax.rem(w + i, 8)
        first.append(push(stage.at[q], land.at[w], s0.at[i], r0.at[i], (n, q)))
    tell(0, line["x"])
    land[w] = stage[w]
    for cp in first:
        cp.wait_recv()
    for q in range(8):
        blk[q * 6 : (q + 1) * 6, :] = land[q, 0:6, :]

    index = [[pos[a] for a in reversed(order)] for order in ORDERS]
    for cls in range(3):
        i2, i1, i0 = index[cls]
        g_ref[cls, c, i2, i1, i0] = blk[cls * 16 : (cls + 1) * 16, :].astype(BF)

    d2d = []

    def cross(cls, j, k):
        ref = g_ref.at[cls, c, j]
        d2d.append(push(ref, ref, ds.at[cls, k], dr.at[cls, k], core))

    def exchange(src, dst, k):
        ww = [lax.rem(w + j, 8) for j in range(8)]
        for j in range(1, 8):
            remote(src.at[n * 8 + ww[j]], dst.at[s], xsend.at[k], xrecv.at[k], (n, ww[j])).start()

        @pl.loop(1, 16)
        def _(i):
            nn = lax.rem(n + i, 16)
            for j in range(8):
                remote(src.at[nn * 8 + ww[j]], dst.at[s], xsend.at[k], xrecv.at[k], (nn, ww[j])).start()

        dst[s] = src[s]
        whole = pl.ds(0, 127)
        cp = remote(src.at[whole], dst.at[whole], xsend.at[k], xrecv.at[k], (n, w))
        started.append(cp)
        return cp

    def deal(value, src):
        rows_a[...] = value
        for q in range(8):
            for r in range(2):
                rows_b[pl.ds(q * 32 + r, 16, stride=2), :] = rows_a[pl.ds(r * 128 + q, 16, stride=8), :]
        src[...] = rows_b[...].astype(BF).reshape(8, 32, 128)

    def hand(src, mid, k):
        cps = []
        for i in range(1, 8):
            q = lax.rem(w + i, 8)
            cps.append(push(src.at[q], mid.at[w], xs1.at[k, i], xr1.at[k, i], (n, q)))
        mid[w] = src[w]
        return cps

    def pass_on(cps, mid, turned, dst, k):
        for cp in cps:
            cp.wait_recv()
        rows_a[...] = mid[...].astype(F32).reshape(256, 128)
        for q in range(8):
            for r in range(2):
                rows_b[pl.ds(q * 2 + r, 16, stride=16), :] = rows_a[pl.ds(q * 32 + r, 16, stride=2), :]
        turned[...] = rows_b[...].astype(BF).reshape(16, 16, 128)
        out = []
        for i in range(1, 16):
            m = lax.rem(n + i, 16)
            out.append(push(turned.at[m], dst.at[n], xs2.at[k, i], xr2.at[k, i], (m, w)))
        dst[n] = turned[n]
        return out

    def gathered(cps, dst):
        for cp in cps:
            cp.wait_recv()
        rows_a[...] = dst[...].astype(F32).reshape(256, 128)
        return [rows_a[pl.ds(r, 128, stride=2), :] for r in range(2)]

    def pack(buf, parts):
        for r, value in parts.items():
            rowbuf[pl.ds(r, 128, stride=8), :] = value
        buf[...] = rowbuf[...].reshape(buf.shape).astype(BF)

    def unpack(buf):
        rowbuf[...] = buf[...].astype(F32).reshape(1024, 128)

    def plane(r):
        return rowbuf[pl.ds(r, 128, stride=8), :]

    def piece(cls, i2, i1, i0):
        return g_ref.at[cls, c, i2, i1, i0]

    def row_of(cls, i2, i1):
        return g_ref.at[cls, c, i2, i1]

    def near_by(cls, phase):
        axis = ORDERS[cls][phase]
        return shifted(pos, axis, 1), shifted(pos, axis, -1)

    def ring(cls, phase, k, ref, device):
        return push(ref, ref, ss.at[cls, phase, k], rs.at[cls, phase, k], device)

    def off(i, d):
        return lax.rem(i + d, 4)

    legs = []
    for cls in range(3):
        mine = piece(cls, *index[cls])
        legs.append([ring(cls, 0, d, mine, shifted(pos, ORDERS[cls][0], d)) for d in (1, 2, 3)])
    pl.semaphore_wait(near.at[0], 3)
    tell(1, line["y"])
    copies[1].wait()
    sel = one_hot(
        16, 128, lambda r, l: ((r < 2) & (l == r + 126)) | ((r >= 2) & (r < 4) & (l == r - 2))
    )
    edge = lax.dot_general(sel, feat_ref[...], dims(1, 1), preferred_element_type=F32)
    for k in range(4):
        for q in range(8):
            at = (k % 2) * 8 + q
            rowf[k // 2, at : at + 1, :] = edge[k : k + 1, q * 512 : (q + 1) * 512]
    rows[...] = rowf[...].astype(BF)
    firsts, legs = legs, []
    far = [[None] * 4 for _ in range(3)]

    def spread_row(cls, d):
        i2, i1, _ = index[cls]
        right, left = near_by(cls, 2)
        ref = row_of(cls, i2, off(i1, d))
        far[cls][d] = (ring(cls, 2, 2 * d, ref, right), ring(cls, 2, 2 * d + 1, ref, left))

    for cls in range(3):
        i2, i1, _ = index[cls]
        for cp in firsts[cls]:
            cp.wait_recv()
        right, left = near_by(cls, 1)
        mine = row_of(cls, i2, i1)
        legs.append((ring(cls, 1, 0, mine, right), ring(cls, 1, 1, mine, left)))
    for cls in range(3):
        spread_row(cls, 0)
    pl.semaphore_wait(near.at[1], 3)
    tell(2, [core])
    copies[4].wait()
    lf = lf_ref[...].astype(F32)
    rowbuf[...] = jnp.zeros((1024, 128), F32)
    deal(lf, send_f)
    lf_half = hand(send_f, mid_f, 0)
    ha = push(rows.at[0], hland.at[0], hs.at[0], hr.at[0], right_shard)
    hb = push(rows.at[1], hland.at[1], hs.at[1], hr.at[1], left_shard)
    halves = []
    for cls in range(3):
        i2, i1, _ = index[cls]
        right, left = near_by(cls, 1)
        legs[cls][0].wait_recv()
        e = ring(cls, 1, 2, half(row_of(cls, i2, off(i1, 3)), 1, 0), right)
        legs[cls][1].wait_recv()
        f = ring(cls, 1, 3, half(row_of(cls, i2, off(i1, 1)), 1, 1), left)
        halves.append((e, f))
    for cls in range(3):
        spread_row(cls, 3)
        spread_row(cls, 1)
    pl.semaphore_wait(near.at[2], 1)
    for cls in range(3):
        for cp in halves[cls]:
            cp.wait_recv()
        spread_row(cls, 2)
    for cls in range(3):
        cross(cls, index[cls][0], 0)
    lfx = pass_on(lf_half, mid_f, turn_f, land_f, 0)
    fh[:, 0:128] = feat_ref[...]
    copies[2].wait()
    tc = jnp.concatenate([taps_ref[...], jnp.zeros((125, 768), F32)], axis=0)
    for k in range(6):
        tcol[k * 128 : (k + 1) * 128, :] = tc[:, k * 128 : (k + 1) * 128].T
    ha.wait_recv()
    hb.wait_recv()
    rowf[...] = hland[...].astype(F32)
    both[...] = jnp.zeros((16, 4096), F32)
    for k in range(4):
        for q in range(8):
            at = (k % 2) * 8 + q
            both[k : k + 1, q * 512 : (q + 1) * 512] = rowf[k // 2, at : at + 1, :]
    lo = jnp.where(s > 0, 0, 2)
    hi = jnp.where(s < 127, 4, 2)
    spread = one_hot(16, 128, lambda r, l: (r == l) & (r >= lo) & (r < hi))
    fh[:, 128:256] = lax.dot_general(
        both[...].astype(BF), spread, dims(0, 0), preferred_element_type=F32
    ).astype(BF)
    relays = []
    for d, k in ((0, 0), (3, 1), (1, 0), (2, 1)):
        for cls in range(3):
            i2, i1, _ = index[cls]
            far[cls][d][k].wait_recv()
            ref = row_of(cls, off(i2, 1 if k else 3), off(i1, d))
            relays.append(ring(cls, 2, 8 + d, ref, near_by(cls, 2)[k]))
    for cls in range(3):
        for d, k in ((0, 1), (3, 0), (1, 1), (2, 0)):
            far[cls][d][k].wait_recv()
        cross(cls, off(index[cls][0], 3), 1)
        cross(cls, off(index[cls][0], 1), 2)
    for ch, taps in enumerate(gathered(lfx, land_f)):
        hf[ch] = taps
    build_toeplitz(tt.at[0], hf, 0)
    for cp in relays:
        cp.wait_recv()
    for cls in range(3):
        cross(cls, off(index[cls][0], 2), 3)
    fcp = push(feat_ref, fo_ref, fs, fr, core)
    copies[3].wait()
    ocp = push(og_ref, ogn, os, orr, left_shard)
    for cp in d2d:
        cp.wait_recv()

    for cls in range(3):
        acc = None
        for q in range(8):
            lhs = wide_block(g_ref, cls, q // 4, q % 4)
            term = jnp.dot(lhs, fh[q * 512 : (q + 1) * 512, :], preferred_element_type=F32)
            acc = term if acc is None else acc + term
        for m in range(16):
            at = slice(m * 48 + cls * 16, m * 48 + cls * 16 + 16)
            p_ref[at, :] = acc[m * 16 : (m + 1) * 16, 0:128]
            halo_ref[at, :] = acc[m * 16 : (m + 1) * 16, 128:256]

    lane = lanes(256)
    for part in range(3):
        at = slice(part * 256, (part + 1) * 256)
        v = p_ref[at, :]
        halo = halo_ref[at, :]
        t0, t1, t2 = tcol[at, 0:1], tcol[at, 1:2], tcol[at, 2:3]
        v1 = jnp.where(lane < 1, pltpu.roll(halo, 127, 1), pltpu.roll(v, 1, 1))
        v2 = jnp.where(lane < 2, halo, pltpu.roll(v, 2, 1))
        feat[part] = t0 * v + t1 * v1 + t2 * v2
        n1 = jnp.where(lane < 1, pltpu.roll(v, 1, 1), pltpu.roll(halo, 127, 1))
        featn[part] = t0 * pltpu.roll(halo, 126, 1) + t1 * n1 + t2 * pltpu.roll(v, 2, 1)
    og = og_ref[...].astype(F32)
    gated = feat[1] * feat[2]
    cot = og * feat[0]
    pack(send_a, {0: gated[0:128], 1: gated[128:256], 2: cot[0:128], 3: cot[128:256]})
    go = exchange(send_a, land_a, 1)
    build_toeplitz(tt.at[1], hf, 1)
    go.wait_recv()
    unpack(land_a)

    anti = one_hot(128, 128, lambda r, l: r + l == 127)
    row = lax.broadcasted_iota(jnp.int32, (128, 128), 0)
    lane1 = lanes(128)
    for ch in range(2):
        gf[ch] = plane(ch)
        cots[ch] = plane(2 + ch).astype(BF)
    ahead_ref[...] = jnp.zeros((128, 128), F32)

    @pl.loop(0, 2)
    def _(ch):
        xg = lax.dot_general(anti, gf[ch].astype(BF), dims(1, 1), preferred_element_type=F32)
        back_in = lax.dot_general(cots[ch], anti, dims(0, 0), preferred_element_type=F32)
        spread_blocks(xs, 1, xg)
        spread_blocks(xs, 0, back_in)
        xc[ch] = xs[:, 0:128]
        yc, yg = toeplitz_product(tt.at[ch], xs, 2)
        conv = lax.dot_general(yg, anti, dims(0, 0), preferred_element_type=F32)
        gg = lax.dot_general(anti, yc, dims(1, 1), preferred_element_type=F32)
        rowbuf[pl.ds(ch, 128, stride=8), :] = conv
        rowbuf[pl.ds(2 + ch, 128, stride=8), :] = gg
        for r, value in ((0, conv), (4, gg)):
            nxt = pltpu.roll(jnp.where(row < 127, pltpu.roll(value, 127, 0), 0.0), r + 2 * ch, 1)
            keep = (lane1 >= r + 2 * ch) & (lane1 < r + 2 * ch + 2)
            ahead_ref[...] = jnp.where(keep, nxt, ahead_ref[...])

    ahead = ahead_ref[...]
    pack(send_b, {4: ahead})
    ret = exchange(send_b, land_b, 2)
    build_toeplitz(tt.at[0], gf, 0)
    ocp.wait_recv()
    ret.wait_recv()
    unpack(land_b)

    def channels(r):
        return jnp.concatenate([plane(r), plane(r + 1)], axis=0)

    conv, gg = channels(0), channels(2)
    ahead = plane(4)
    convn = jnp.concatenate([ahead, pltpu.roll(ahead, 126, 1)], axis=0)
    ggn = jnp.concatenate([pltpu.roll(ahead, 124, 1), pltpu.roll(ahead, 122, 1)], axis=0)
    mixed_ref[...] = (feat[0] * conv).astype(BF)
    store(0, mixed_ref, mixed_hbm)
    ogv = ogn[...].astype(F32)
    last = s == 127

    def derivative(part):
        if part == 0:
            return og * conv
        return gg * feat[3 - part]

    for part in range(3):
        at = slice(part * 256, (part + 1) * 256)
        fd = derivative(part)
        fdn = ogv * convn if part == 0 else ggn * featn[3 - part]
        fdn = jnp.where(last, 0.0, fdn)
        t0, t1, t2 = tcol[at, 0:1], tcol[at, 1:2], tcol[at, 2:3]
        f1 = jnp.where(lane < 127, pltpu.roll(fd, 127, 1), pltpu.roll(fdn, 127, 1))
        f2 = jnp.where(lane < 126, pltpu.roll(fd, 126, 1), pltpu.roll(fdn, 126, 1))
        pd_ref[at, :] = (t0 * fd + t1 * f1 + t2 * f2).astype(BF)
    pcp = push(pd_ref, pdo, ps, pr, core)

    for part in range(3):
        at = slice(part * 256, (part + 1) * 256)
        fd = derivative(part)
        v = p_ref[at, :]
        halo = halo_ref[at, :]
        v1 = jnp.where(lane < 1, pltpu.roll(halo, 127, 1), pltpu.roll(v, 1, 1))
        v2 = jnp.where(lane < 2, halo, pltpu.roll(v, 2, 1))
        total = jnp.zeros((256, 128), F32)
        for k, q in enumerate((v, v1, v2)):
            total = jnp.where(lane == k, jnp.sum(fd * q, axis=1, keepdims=True), total)
        tl[0, c, :, at] = total.T[0:8, :]

    def tap_send(k, peers, slot):
        return [
            push(tl.at[k, slot], tl.at[k, slot], tsn.at[k, i], trc.at[k, i], device)
            for i, device in enumerate(peers)
        ]

    def tap_sum(k, cps, count):
        for cp in cps:
            cp.wait_recv()
        total = tl[k, 0]
        for i in range(1, count):
            total = total + tl[k, i]
        return total

    tcp = tap_send(0, [core], c)
    fcp.wait_recv()
    pcp.wait_recv()
    for cls in range(3):
        for z in range(4):
            for yl in range(2):
                at = pl.ds(pl.multiple_of((z * 4 + yl * 2 + c) * 48 + cls * 16, 16), 16)
                to = cls * 128 + z * 32 + yl * 16
                pdc[to : to + 16, 0:128] = pd_ref[at, :]
                pdc[to : to + 16, 128:256] = pdo[at, :]

    def add(dst, src):
        dst[...] = (dst[...].astype(F32) + src[...].astype(F32)).astype(BF)

    def feat_part(qs):
        @pl.loop(qs.start, qs.stop)
        def _(q):
            total = None
            for cls in range(3):
                term = lax.dot_general(
                    pdt[:, cls * 256 : (cls + 1) * 256], wide_block(g_ref, cls, q // 4, lax.rem(q, 4)), dims(1, 0),
                    preferred_element_type=F32,
                )
                total = term if total is None else total + term
            fgrad_ref[pl.ds(pl.multiple_of(q * 512, 512), 512), :] = total.T.astype(BF)

    def back(cls, phase, k, src, dst, device):
        return push(src, dst, ss2.at[cls, phase, k], rs2.at[cls, phase, k], device)

    def prow(cls, d2, d1):
        i2, i1, _ = index[cls]
        return p.at[cls, off(i2, d2), off(i1, d1)]

    relay = ((2, 1), (0, 3))
    hops, came = [], []
    for cls in range(3):
        hops.append({})
        came.append({})
    for cls in range(3):

        @pl.loop(0, 8)
        def _(q):
            cols = pl.ds(pl.multiple_of(q * 512, 512), 512)
            part = lax.dot_general(
                pdc[cls * 128 : (cls + 1) * 128, :],
                jnp.concatenate([feat_ref[cols, :], fo_ref[cols, :]], axis=1),
                dims(1, 1),
                preferred_element_type=F32,
            ).astype(BF)
            for z in range(4):
                for yl in range(2):
                    k = z * 32 + yl * 16
                    i2, i1, i0 = piece_index(cls, z, q // 4, yl, lax.rem(q, 4))
                    p[cls, i2, i1, i0] = part[k : k + 16, :]
        right, left = near_by(cls, 2)
        for j in range(2):
            hops[cls][0, j] = back(cls, 2, j, prow(cls, 2, relay[j][0]), ra3.at[cls, j], right)
            hops[cls][1, j] = back(cls, 2, 2 + j, prow(cls, 2, relay[j][1]), rb3.at[cls, j], left)
        for j in range(2):
            d = relay[j][0]
            came[cls][1, d] = back(cls, 2, 8 + d, prow(cls, 3, d), rd3.at[cls, d], left)
            d = relay[j][1]
            came[cls][0, d] = back(cls, 2, 4 + d, prow(cls, 1, d), rc3.at[cls, d], right)
    pdt[...] = jnp.concatenate(
        [
            pd_ref[m * 48 + cls * 16 : m * 48 + cls * 16 + 16, :].astype(F32)
            for cls in range(3)
            for m in range(16)
        ],
        axis=0,
    ).T.astype(BF)
    build_toeplitz(tt.at[1], gf, 1)
    for j in range(2):
        for cls in range(3):
            right, left = near_by(cls, 2)
            d = relay[j][0]
            hops[cls][0, j].wait_recv()
            add(prow(cls, 1, d), ra3.at[cls, j])
            came[cls][0, d] = back(cls, 2, 4 + d, prow(cls, 1, d), rc3.at[cls, d], right)
            d = relay[j][1]
            hops[cls][1, j].wait_recv()
            add(prow(cls, 3, d), rb3.at[cls, j])
            came[cls][1, d] = back(cls, 2, 8 + d, prow(cls, 3, d), rd3.at[cls, d], left)
    tl[1, pos["x"]] = tap_sum(0, tcp, 2)
    tcp = tap_send(1, line["x"], pos["x"])

    @pl.loop(0, 2)
    def _(ch):
        (y,) = toeplitz_product(tt.at[ch], xc.at[ch], 1)
        hf[ch] = lax.dot_general(anti, y, dims(1, 1), preferred_element_type=F32)

    deal(hf[...].reshape(256, 128), send_c)
    fg_half = hand(send_c, mid_c, 1)
    feat_part(range(2))

    def finish_row(cls, d):
        came[cls][0, d].wait_recv()
        came[cls][1, d].wait_recv()
        mine = prow(cls, 0, d)
        total = mine[...].astype(F32) + rc3[cls, d].astype(F32) + rd3[cls, d].astype(F32)
        mine[...] = total.astype(BF)

    legs = [{} for _ in range(3)]
    for cls in range(3):
        right, left = near_by(cls, 1)
        finish_row(cls, 2)
        far_row = prow(cls, 0, 2)
        legs[cls][0] = back(cls, 1, 0, half(far_row, 1, 0), ra2.at[cls], right)
        legs[cls][1] = back(cls, 1, 1, half(far_row, 1, 1), rb2.at[cls], left)
    for cls in range(3):
        right, left = near_by(cls, 1)
        finish_row(cls, 1)
        legs[cls][2] = back(cls, 1, 2, half(prow(cls, 0, 1), 1, 1), half(rc2.at[cls], 1, 1), right)
        finish_row(cls, 3)
        legs[cls][3] = back(cls, 1, 3, half(prow(cls, 0, 3), 1, 0), half(rd2.at[cls], 1, 0), left)
    for cls in range(3):
        finish_row(cls, 0)
    for cls in range(3):
        right, left = near_by(cls, 1)
        legs[cls][0].wait_recv()
        add(half(prow(cls, 0, 1), 1, 0), ra2.at[cls])
        legs[cls][4] = back(cls, 1, 4, half(prow(cls, 0, 1), 1, 0), half(rc2.at[cls], 1, 0), right)
        legs[cls][1].wait_recv()
        add(half(prow(cls, 0, 3), 1, 1), rb2.at[cls])
        legs[cls][5] = back(cls, 1, 5, half(prow(cls, 0, 3), 1, 1), half(rd2.at[cls], 1, 1), left)
    tl[2, pos["y"]] = tap_sum(1, tcp, 4)
    tcp = tap_send(2, line["y"], pos["y"])
    fgx = pass_on(fg_half, mid_c, turn_c, land_c, 1)
    feat_part(range(2, 6))
    low = []

    def part_of(cls, d):
        i2, i1, i0 = index[cls]
        return p.at[cls, i2, i1, off(i0, d)]

    for cls in range(3):
        for k in range(2, 6):
            legs[cls][k].wait_recv()
        mine = prow(cls, 0, 0)
        total = mine[...].astype(F32) + rc2[cls].astype(F32) + rd2[cls].astype(F32)
        mine[...] = total.astype(BF)
        low.append(
            [
                back(cls, 0, d, part_of(cls, d), rz.at[cls, d - 1], shifted(pos, ORDERS[cls][0], d))
                for d in (1, 2, 3)
            ]
        )
    tl[3, pos["z"]] = tap_sum(2, tcp, 4)
    tcp = tap_send(3, line["z"], pos["z"])
    feat_part(range(6, 8))
    store(1, fgrad_ref, fgrad_hbm)
    for cls in range(3):
        total = part_of(cls, 0)[...].astype(F32)
        for k in range(3):
            low[cls][k].wait_recv()
            total = total + rz[cls, k].astype(F32)
        blk[cls * 16 : (cls + 1) * 16, :] = total

    for q in range(8):
        stage2[q, 0:6, :] = blk[q * 6 : (q + 1) * 6, :]
        stage2[q, 6:8, :] = jnp.zeros((2, 512), F32)
    final = []
    for i in range(1, 8):
        q = lax.rem(w + i, 8)
        final.append(push(stage2.at[q], land2.at[w], s02.at[i], r02.at[i], (n, q)))
    land2[w] = stage2[w]
    tout_ref[...] = tap_sum(3, tcp, 4)[0:3]
    store(3, tout_ref, tout_hbm)
    fgout_ref[...] = jnp.concatenate(gathered(fgx, land_c), axis=0).astype(BF)
    store(2, fgout_ref, fgout_hbm)
    for cp in final:
        cp.wait_recv()
    for q in range(8):
        grad_ref[:, q * 512 : (q + 1) * 512] = land2[q, 0:6, :]
    store(4, grad_ref, grad_hbm)
    for cp in started:
        cp.wait_send()
    for cp in stores:
        cp.wait()


ANY = pl.BlockSpec(memory_space=pl.ANY)


def hyena(in_proj, features, taps, out_grad, long_filter):
    sem = pltpu.SemaphoreType.DMA
    vm = pltpu.VMEM
    tile = (128, 8, 128)
    return pl.pallas_call(
        hyena_kernel,
        out_shape=(
            jax.ShapeDtypeStruct((256, 128), BF),
            jax.ShapeDtypeStruct((4096, 128), BF),
            jax.ShapeDtypeStruct((256, 128), BF),
            jax.ShapeDtypeStruct((3, 768), F32),
            jax.ShapeDtypeStruct((6, 4096), F32),
        ),
        in_specs=[ANY] * 5,
        out_specs=(ANY,) * 5,
        scratch_shapes=[
            vm((256, 128), BF), vm((4096, 128), BF), vm((256, 128), BF), vm((3, 768), F32), vm((6, 4096), F32), sem((5,)),
            vm((6, 4096), BF), vm((4096, 128), BF), vm((3, 768), F32), vm((256, 128), BF), vm((256, 128), BF),
            vm((8, 8, 512), F32), vm((8, 8, 512), F32), vm((48, 512), F32),
            vm((2, 16, 512), BF), vm((2, 16, 512), BF), vm((4096, 256), BF),
            vm((3, 2, 4, 4, 4, 16, 512), BF), vm((4096, 128), BF),
            vm((768, 128), F32), vm((768, 128), F32), vm((768, 128), F32),
            vm((1024, 128), F32),
        ]
        + [vm((8, 32, 128), BF), vm((16, 16, 128), BF)]
        + [vm(tile, BF)] * 4
        + [vm((8, 32, 128), BF), vm((16, 16, 128), BF)]
        + [
            vm((256, 128), BF), vm((2, 128, 128), F32), vm((2, 128, 128), F32),
            vm((3, 256, 128), F32), vm((3, 256, 128), F32),
            vm((2, 1024, 2048), BF), vm((2, 128, 128), BF), vm((128, 128), F32), vm((2048, 256), BF), vm((2, 2048, 128), BF),
            vm((768, 128), BF),
            vm((768, 128), BF), vm((384, 256), BF), vm((3, 4, 4, 4, 16, 512), BF),
            vm((3, 2, 4, 16, 512), BF), vm((3, 2, 4, 16, 512), BF),
            vm((3, 4, 4, 16, 512), BF), vm((3, 4, 4, 16, 512), BF),
            vm((3, 2, 16, 512), BF), vm((3, 2, 16, 512), BF),
            vm((3, 4, 16, 512), BF), vm((3, 4, 16, 512), BF),
            vm((3, 3, 16, 512), BF), vm((8, 32, 128), BF), vm((8, 32, 128), BF),
            vm((16, 16, 128), BF), vm((16, 16, 128), BF), vm((256, 128), F32), vm((256, 128), F32),
            vm((8, 8, 512), F32), vm((8, 8, 512), F32), vm((4, 4, 8, 768), F32), vm((128, 768), BF), vm((2, 16, 512), F32), vm((16, 4096), F32),
            sem((5,)), sem((8,)), sem((8,)),
            sem((3, 3, 12)), sem((3, 3, 12)), sem((3, 4)), sem((3, 4)),
            sem((2,)), sem((2,)), sem, sem, sem((4,)), sem((4,)), sem, sem,
            sem, sem, sem((3, 3, 12)), sem((3, 3, 12)), sem((8,)), sem((8,)), sem((4, 3)), sem((4, 3)),
            pltpu.SemaphoreType.REGULAR((3,)),
            sem((2, 8)), sem((2, 8)), sem((2, 16)), sem((2, 16)),
        ],
        compiler_params=pltpu.CompilerParams(
            collective_id=1, has_side_effects=True, vmem_limit_bytes=58 * 1024 * 1024
        ),
        name="hyena",
    )(in_proj, features, taps, out_grad, long_filter)


def copy_kernel(*refs):
    sources, targets, held, (came, left) = refs[:5], refs[5:10], refs[10:15], refs[15:]
    inward = [pltpu.make_async_copy(sources[k], held[k], came.at[k]) for k in range(5)]
    outward = [pltpu.make_async_copy(held[k], targets[k], left.at[k]) for k in range(5)]
    for cp in inward:
        cp.start()
    for k in range(5):
        inward[k].wait()
        outward[k].start()
    for cp in outward:
        cp.wait()


def settle(arrays):
    return pl.pallas_call(
        copy_kernel,
        out_shape=tuple(jax.ShapeDtypeStruct(a.shape, a.dtype) for a in arrays),
        in_specs=[ANY] * 5,
        out_specs=(ANY,) * 5,
        scratch_shapes=[pltpu.VMEM(a.shape, a.dtype) for a in arrays]
        + [pltpu.SemaphoreType.DMA((5,)), pltpu.SemaphoreType.DMA((5,))],
        name="settle",
    )(*arrays)


def local(features, in_proj, short_taps, long_filter, out_grad):
    return settle(hyena(in_proj, features, short_taps, out_grad, long_filter))


def solution(mesh):
    tokens = P(None, AXES)
    rows = P(AXES, None)
    return jax.shard_map(
        local,
        mesh=mesh,
        in_specs=(tokens, rows, P(), tokens, tokens),
        out_specs=(tokens, tokens, tokens, P(), rows),
        check_vma=False,
    )
```

```python
import math

import jax
import jax.numpy as jnp
from jax import lax
from jax.experimental import pallas as pl
from jax.experimental.pallas import tpu as pltpu
from jax.sharding import PartitionSpec as P

MESH = pl.DeviceIdType.MESH
BF = jnp.bfloat16
F32 = jnp.float32
ORDERS = (("x", "y", "z"), ("y", "z", "x"), ("z", "x", "y"))
AXES = ("narrow", "wide")


def place(pos):
    y = pos["y"]
    return (pos["z"] * 4 + lax.rem(y, 2) * 2 + pos["c"], (y // 2) * 4 + pos["x"])


def position():
    n = lax.axis_index("narrow")
    w = lax.axis_index("wide")
    pos = {
        "x": lax.rem(w, 4),
        "y": (w // 4) * 2 + lax.rem(n // 2, 2),
        "z": n // 4,
        "c": lax.rem(n, 2),
    }
    return n, w, pos


def shifted(pos, axis, by):
    other = dict(pos)
    other[axis] = lax.rem(pos[axis] + by + 4, 4)
    return place(other)


def other_core(pos):
    other = dict(pos)
    other["c"] = 1 - pos["c"]
    return place(other)


def shard_id(s):
    return (s // 8, lax.rem(s, 8))


def remote(src, dst, send, recv, device):
    return pltpu.make_async_remote_copy(
        src_ref=src, dst_ref=dst, send_sem=send, recv_sem=recv, device_id=device, device_id_type=MESH
    )


def greet(devices):
    barrier = pltpu.get_barrier_semaphore()
    for device in devices:
        pl.semaphore_signal(barrier, inc=1, device_id=device, device_id_type=MESH)
    pl.semaphore_wait(barrier, len(devices))


def piece_index(cls, z, yh, yl, x):
    at = {"x": x, "y": yh * 2 + yl, "z": z}
    d0, d1, d2 = ORDERS[cls]
    return (at[d2], at[d1], at[d0])


def dims(a, b):
    return (((a,), (b,)), ((), ()))


def lanes(rows):
    return lax.broadcasted_iota(jnp.int32, (rows, 128), 1)


def one_hot(rows, cols, test):
    r = lax.broadcasted_iota(jnp.int32, (rows, cols), 0)
    c = lax.broadcasted_iota(jnp.int32, (rows, cols), 1)
    return jnp.where(test(r, c), 1.0, 0.0).astype(BF)


def wide_block(g_ref, cls, yh, x):
    parts = []
    for z in range(4):
        for yl in range(2):
            for core in range(2):
                i2, i1, i0 = piece_index(cls, z, yh, yl, x)
                parts.append(g_ref[cls, core, i2, i1, i0])
    return jnp.concatenate(parts, axis=0)


def half(ref, phase, k):
    if phase == 0:
        return ref.at[:, pl.ds(k * 256, 256)]
    return ref.at[pl.ds(k * 2, 2)]


def build_toeplitz(tt, h_ref, ch):
    lane = lanes(128)
    row = lax.broadcasted_iota(jnp.int32, (128, 128), 0)
    upper = lane >= row

    def rolled(k):
        taps = jnp.broadcast_to(h_ref[ch, pl.ds(k, 1), :], (128, 128))
        return pltpu.roll(taps, 0, 1, stride=1, stride_axis=0)

    @pl.loop(0, 8)
    def _(g):
        prev = jnp.where(g > 0, rolled(jnp.maximum(16 * g - 1, 0)), 0.0)
        at = pl.ds(pl.multiple_of(g * 128, 128), 128)
        for i in range(16):
            cur = rolled(16 * g + i)
            tt[at, i * 128 : (i + 1) * 128] = jnp.where(upper, cur, prev).astype(BF)
            prev = cur


def spread_blocks(xs, col, x):
    lane = lanes(128)
    for i in range(16):
        moved = pltpu.roll(x, i, 1) if i else x
        xs[i * 128 : (i + 1) * 128, col * 128 : (col + 1) * 128] = jnp.where(lane < i, 0.0, moved).astype(BF)


def toeplitz_product(tt, xs, cols):
    lane = lanes(128)
    out = jnp.dot(tt[...], xs[:, 0 : cols * 128], preferred_element_type=F32)
    results = []
    for c in range(cols):
        at = slice(c * 128, (c + 1) * 128)
        acc = out[896:1024, at]
        for g in range(6, -1, -1):
            acc = jnp.where(lane < 16, 0.0, pltpu.roll(acc, 16, 1)) + out[g * 128 : (g + 1) * 128, at]
        results.append(acc.astype(BF))
    return results


def hyena_kernel(
    proj_hbm, feat_hbm, taps_hbm, og_hbm, lf_hbm,
    mixed_hbm, fgrad_hbm, fgout_hbm, tout_hbm, grad_hbm,
    mixed_ref, fgrad_ref, fgout_ref, tout_ref, grad_ref, outs,
    proj_ref, feat_ref, taps_ref, og_ref, lf_ref,
    stage, land, blk, rows, hland, fh, g_ref, fo_ref, p_ref, halo_ref, tcol,
    rowbuf, send_f, land_f, send_a, land_a, send_b, land_b, send_c, land_c,
    ogn, hf, gf, feat, featn, tt, cots, ahead_ref, xs, xc, pd_ref,
    pdo, pdc, p, ra3, rb3, rc3, rd3, rq, rz, mid_f, mid_c, turn_f, turn_c, rows_a, rows_b,
    stage2, land2, tl, pdt, rowf, both,
    ins, s0, r0, ss, rs, ds, dr, hs, hr, fs, fr, xsend, xrecv, os, orr,
    ps, pr, ss2, rs2, s02, r02, tsn, trc, near, xs1, xr1, xs2, xr2,
):
    n, w, pos = position()
    c = pos["c"]
    s = n * 8 + w
    right_shard = shard_id(lax.rem(s + 1, 128))
    left_shard = shard_id(lax.rem(s + 127, 128))
    wide_peers = [(n, lax.rem(w + i, 8)) for i in range(1, 8)]
    line = {a: [shifted(pos, a, d) for d in (1, 2, 3)] for a in "xyz"}
    core = other_core(pos)
    copies = [
        pltpu.make_async_copy(a, b, ins.at[k])
        for k, (a, b) in enumerate(
            ((proj_hbm, proj_ref), (feat_hbm, feat_ref), (taps_hbm, taps_ref), (og_hbm, og_ref), (lf_hbm, lf_ref))
        )
    ]
    for cp in copies:
        cp.start()
    barrier = pltpu.get_barrier_semaphore()
    greeted = wide_peers + line["y"] + line["z"] + [core, right_shard, left_shard]
    for device in greeted:
        pl.semaphore_signal(barrier, inc=1, device_id=device, device_id_type=MESH)
    copies[0].wait()
    for q in range(8):
        stage[q, 0:6, :] = proj_ref[:, q * 512 : (q + 1) * 512].astype(F32)
        stage[q, 6:8, :] = jnp.zeros((2, 512), F32)
    pl.semaphore_wait(barrier, len(greeted))

    def tell(k, devices):
        for device in devices:
            pl.semaphore_signal(near.at[k], inc=1, device_id=device, device_id_type=MESH)

    started = []
    stores = []

    def store(k, src, dst):
        cp = pltpu.make_async_copy(src, dst, outs.at[k])
        cp.start()
        stores.append(cp)

    def push(src, dst, a, b, device):
        cp = remote(src, dst, a, b, device)
        cp.start()
        started.append(cp)
        return cp

    first = []
    for i in range(1, 8):
        q = lax.rem(w + i, 8)
        first.append(push(stage.at[q], land.at[w], s0.at[i], r0.at[i], (n, q)))
    tell(0, line["x"])
    land[w] = stage[w]
    for cp in first:
        cp.wait_recv()
    for q in range(8):
        blk[q * 6 : (q + 1) * 6, :] = land[q, 0:6, :]

    index = [[pos[a] for a in reversed(order)] for order in ORDERS]
    for cls in range(3):
        i2, i1, i0 = index[cls]
        g_ref[cls, c, i2, i1, i0] = blk[cls * 16 : (cls + 1) * 16, :].astype(BF)

    d2d = []

    def cross(cls, j, k):
        ref = g_ref.at[cls, c, j]
        d2d.append(push(ref, ref, ds.at[cls, k], dr.at[cls, k], core))

    def exchange(src, dst, k):
        ww = [lax.rem(w + j, 8) for j in range(8)]
        for j in range(1, 8):
            remote(src.at[n * 8 + ww[j]], dst.at[s], xsend.at[k], xrecv.at[k], (n, ww[j])).start()

        @pl.loop(1, 16)
        def _(i):
            nn = lax.rem(n + i, 16)
            for j in range(8):
                remote(src.at[nn * 8 + ww[j]], dst.at[s], xsend.at[k], xrecv.at[k], (nn, ww[j])).start()

        dst[s] = src[s]
        whole = pl.ds(0, 127)
        cp = remote(src.at[whole], dst.at[whole], xsend.at[k], xrecv.at[k], (n, w))
        started.append(cp)
        return cp

    def deal(value, src):
        rows_a[...] = value
        for q in range(8):
            for r in range(2):
                rows_b[pl.ds(q * 32 + r, 16, stride=2), :] = rows_a[pl.ds(r * 128 + q, 16, stride=8), :]
        src[...] = rows_b[...].astype(BF).reshape(8, 32, 128)

    def hand(src, mid, k):
        cps = []
        for i in range(1, 8):
            q = lax.rem(w + i, 8)
            cps.append(push(src.at[q], mid.at[w], xs1.at[k, i], xr1.at[k, i], (n, q)))
        mid[w] = src[w]
        return cps

    def pass_on(cps, mid, turned, dst, k):
        for cp in cps:
            cp.wait_recv()
        rows_a[...] = mid[...].astype(F32).reshape(256, 128)
        for q in range(8):
            for r in range(2):
                rows_b[pl.ds(q * 2 + r, 16, stride=16), :] = rows_a[pl.ds(q * 32 + r, 16, stride=2), :]
        turned[...] = rows_b[...].astype(BF).reshape(16, 16, 128)
        out = []
        for i in range(1, 16):
            m = lax.rem(n + i, 16)
            out.append(push(turned.at[m], dst.at[n], xs2.at[k, i], xr2.at[k, i], (m, w)))
        dst[n] = turned[n]
        return out

    def gathered(cps, dst):
        for cp in cps:
            cp.wait_recv()
        rows_a[...] = dst[...].astype(F32).reshape(256, 128)
        return [rows_a[pl.ds(r, 128, stride=2), :] for r in range(2)]

    def pack(buf, parts):
        for r, value in parts.items():
            rowbuf[pl.ds(r, 128, stride=8), :] = value
        buf[...] = rowbuf[...].reshape(buf.shape).astype(BF)

    def unpack(buf):
        rowbuf[...] = buf[...].astype(F32).reshape(1024, 128)

    def plane(r):
        return rowbuf[pl.ds(r, 128, stride=8), :]

    def piece(cls, i2, i1, i0):
        return g_ref.at[cls, c, i2, i1, i0]

    def row_of(cls, i2, i1):
        return g_ref.at[cls, c, i2, i1]

    def near_by(cls, phase):
        axis = ORDERS[cls][phase]
        return shifted(pos, axis, 1), shifted(pos, axis, -1)

    def ring(cls, phase, k, ref, device):
        return push(ref, ref, ss.at[cls, phase, k], rs.at[cls, phase, k], device)

    def off(i, d):
        return lax.rem(i + d, 4)

    legs = []
    for cls in range(3):
        mine = piece(cls, *index[cls])
        legs.append([ring(cls, 0, d, mine, shifted(pos, ORDERS[cls][0], d)) for d in (1, 2, 3)])
    pl.semaphore_wait(near.at[0], 3)
    tell(1, line["y"])
    copies[1].wait()
    sel = one_hot(
        16, 128, lambda r, l: ((r < 2) & (l == r + 126)) | ((r >= 2) & (r < 4) & (l == r - 2))
    )
    edge = lax.dot_general(sel, feat_ref[...], dims(1, 1), preferred_element_type=F32)
    for k in range(4):
        for q in range(8):
            at = (k % 2) * 8 + q
            rowf[k // 2, at : at + 1, :] = edge[k : k + 1, q * 512 : (q + 1) * 512]
    rows[...] = rowf[...].astype(BF)
    firsts, legs = legs, []
    far = [[None] * 4 for _ in range(3)]

    def spread_row(cls, d):
        i2, i1, _ = index[cls]
        right, left = near_by(cls, 2)
        ref = row_of(cls, i2, off(i1, d))
        far[cls][d] = (ring(cls, 2, 2 * d, ref, right), ring(cls, 2, 2 * d + 1, ref, left))

    for cls in range(3):
        i2, i1, _ = index[cls]
        for cp in firsts[cls]:
            cp.wait_recv()
        mine = row_of(cls, i2, i1)
        legs.append([ring(cls, 1, d, mine, shifted(pos, ORDERS[cls][1], d)) for d in (1, 3, 2)])
    for cls in range(3):
        spread_row(cls, 0)
    pl.semaphore_wait(near.at[1], 3)
    tell(2, [core])
    copies[4].wait()
    lf = lf_ref[...].astype(F32)
    rowbuf[...] = jnp.zeros((1024, 128), F32)
    deal(lf, send_f)
    lf_half = hand(send_f, mid_f, 0)
    ha = push(rows.at[0], hland.at[0], hs.at[0], hr.at[0], right_shard)
    hb = push(rows.at[1], hland.at[1], hs.at[1], hr.at[1], left_shard)
    pl.semaphore_wait(near.at[2], 1)
    for k, d in ((0, 3), (1, 1), (2, 2)):
        for cls in range(3):
            legs[cls][k].wait_recv()
            spread_row(cls, d)
    for cls in range(3):
        cross(cls, index[cls][0], 0)
    lfx = pass_on(lf_half, mid_f, turn_f, land_f, 0)
    fh[:, 0:128] = feat_ref[...]
    copies[2].wait()
    tc = jnp.concatenate([taps_ref[...], jnp.zeros((125, 768), F32)], axis=0)
    for k in range(6):
        tcol[k * 128 : (k + 1) * 128, :] = tc[:, k * 128 : (k + 1) * 128].T
    ha.wait_recv()
    hb.wait_recv()
    rowf[...] = hland[...].astype(F32)
    both[...] = jnp.zeros((16, 4096), F32)
    for k in range(4):
        for q in range(8):
            at = (k % 2) * 8 + q
            both[k : k + 1, q * 512 : (q + 1) * 512] = rowf[k // 2, at : at + 1, :]
    lo = jnp.where(s > 0, 0, 2)
    hi = jnp.where(s < 127, 4, 2)
    spread = one_hot(16, 128, lambda r, l: (r == l) & (r >= lo) & (r < hi))
    fh[:, 128:256] = lax.dot_general(
        both[...].astype(BF), spread, dims(0, 0), preferred_element_type=F32
    ).astype(BF)
    relays = []
    for d, k in ((0, 0), (3, 1), (1, 0), (2, 1)):
        for cls in range(3):
            i2, i1, _ = index[cls]
            far[cls][d][k].wait_recv()
            ref = row_of(cls, off(i2, 1 if k else 3), off(i1, d))
            relays.append(ring(cls, 2, 8 + d, ref, near_by(cls, 2)[k]))
    for cls in range(3):
        for d, k in ((0, 1), (3, 0), (1, 1), (2, 0)):
            far[cls][d][k].wait_recv()
        cross(cls, off(index[cls][0], 3), 1)
        cross(cls, off(index[cls][0], 1), 2)
    for ch, taps in enumerate(gathered(lfx, land_f)):
        hf[ch] = taps
    build_toeplitz(tt.at[0], hf, 0)
    for cp in relays:
        cp.wait_recv()
    for cls in range(3):
        cross(cls, off(index[cls][0], 2), 3)
    fcp = push(feat_ref, fo_ref, fs, fr, core)
    copies[3].wait()
    ocp = push(og_ref, ogn, os, orr, left_shard)
    for cp in d2d:
        cp.wait_recv()

    for cls in range(3):
        acc = None
        for q in range(8):
            lhs = wide_block(g_ref, cls, q // 4, q % 4)
            term = jnp.dot(lhs, fh[q * 512 : (q + 1) * 512, :], preferred_element_type=F32)
            acc = term if acc is None else acc + term
        for m in range(16):
            at = slice(m * 48 + cls * 16, m * 48 + cls * 16 + 16)
            p_ref[at, :] = acc[m * 16 : (m + 1) * 16, 0:128]
            halo_ref[at, :] = acc[m * 16 : (m + 1) * 16, 128:256]

    lane = lanes(256)
    for part in range(3):
        at = slice(part * 256, (part + 1) * 256)
        v = p_ref[at, :]
        halo = halo_ref[at, :]
        t0, t1, t2 = tcol[at, 0:1], tcol[at, 1:2], tcol[at, 2:3]
        v1 = jnp.where(lane < 1, pltpu.roll(halo, 127, 1), pltpu.roll(v, 1, 1))
        v2 = jnp.where(lane < 2, halo, pltpu.roll(v, 2, 1))
        feat[part] = t0 * v + t1 * v1 + t2 * v2
        n1 = jnp.where(lane < 1, pltpu.roll(v, 1, 1), pltpu.roll(halo, 127, 1))
        featn[part] = t0 * pltpu.roll(halo, 126, 1) + t1 * n1 + t2 * pltpu.roll(v, 2, 1)
    og = og_ref[...].astype(F32)
    gated = feat[1] * feat[2]
    cot = og * feat[0]
    pack(send_a, {0: gated[0:128], 1: gated[128:256], 2: cot[0:128], 3: cot[128:256]})
    go = exchange(send_a, land_a, 1)
    build_toeplitz(tt.at[1], hf, 1)
    go.wait_recv()
    unpack(land_a)

    anti = one_hot(128, 128, lambda r, l: r + l == 127)
    row = lax.broadcasted_iota(jnp.int32, (128, 128), 0)
    lane1 = lanes(128)
    for ch in range(2):
        gf[ch] = plane(ch)
        cots[ch] = plane(2 + ch).astype(BF)
    ahead_ref[...] = jnp.zeros((128, 128), F32)

    @pl.loop(0, 2)
    def _(ch):
        xg = lax.dot_general(anti, gf[ch].astype(BF), dims(1, 1), preferred_element_type=F32)
        back_in = lax.dot_general(cots[ch], anti, dims(0, 0), preferred_element_type=F32)
        spread_blocks(xs, 1, xg)
        spread_blocks(xs, 0, back_in)
        xc[ch] = xs[:, 0:128]
        yc, yg = toeplitz_product(tt.at[ch], xs, 2)
        conv = lax.dot_general(yg, anti, dims(0, 0), preferred_element_type=F32)
        gg = lax.dot_general(anti, yc, dims(1, 1), preferred_element_type=F32)
        rowbuf[pl.ds(ch, 128, stride=8), :] = conv
        rowbuf[pl.ds(2 + ch, 128, stride=8), :] = gg
        for r, value in ((0, conv), (4, gg)):
            nxt = pltpu.roll(jnp.where(row < 127, pltpu.roll(value, 127, 0), 0.0), r + 2 * ch, 1)
            keep = (lane1 >= r + 2 * ch) & (lane1 < r + 2 * ch + 2)
            ahead_ref[...] = jnp.where(keep, nxt, ahead_ref[...])

    ahead = ahead_ref[...]
    pack(send_b, {4: ahead})
    ret = exchange(send_b, land_b, 2)
    build_toeplitz(tt.at[0], gf, 0)
    ocp.wait_recv()
    ret.wait_recv()
    unpack(land_b)

    def channels(r):
        return jnp.concatenate([plane(r), plane(r + 1)], axis=0)

    conv, gg = channels(0), channels(2)
    ahead = plane(4)
    convn = jnp.concatenate([ahead, pltpu.roll(ahead, 126, 1)], axis=0)
    ggn = jnp.concatenate([pltpu.roll(ahead, 124, 1), pltpu.roll(ahead, 122, 1)], axis=0)
    mixed_ref[...] = (feat[0] * conv).astype(BF)
    store(0, mixed_ref, mixed_hbm)
    ogv = ogn[...].astype(F32)
    last = s == 127

    def derivative(part):
        if part == 0:
            return og * conv
        return gg * feat[3 - part]

    for part in range(3):
        at = slice(part * 256, (part + 1) * 256)
        fd = derivative(part)
        fdn = ogv * convn if part == 0 else ggn * featn[3 - part]
        fdn = jnp.where(last, 0.0, fdn)
        t0, t1, t2 = tcol[at, 0:1], tcol[at, 1:2], tcol[at, 2:3]
        f1 = jnp.where(lane < 127, pltpu.roll(fd, 127, 1), pltpu.roll(fdn, 127, 1))
        f2 = jnp.where(lane < 126, pltpu.roll(fd, 126, 1), pltpu.roll(fdn, 126, 1))
        pd_ref[at, :] = (t0 * fd + t1 * f1 + t2 * f2).astype(BF)
    pcp = push(pd_ref, pdo, ps, pr, core)

    for part in range(3):
        at = slice(part * 256, (part + 1) * 256)
        fd = derivative(part)
        v = p_ref[at, :]
        halo = halo_ref[at, :]
        v1 = jnp.where(lane < 1, pltpu.roll(halo, 127, 1), pltpu.roll(v, 1, 1))
        v2 = jnp.where(lane < 2, halo, pltpu.roll(v, 2, 1))
        total = jnp.zeros((256, 128), F32)
        for k, q in enumerate((v, v1, v2)):
            total = jnp.where(lane == k, jnp.sum(fd * q, axis=1, keepdims=True), total)
        tl[0, c, :, at] = total.T[0:8, :]

    def tap_send(k, peers, slot):
        return [
            push(tl.at[k, slot], tl.at[k, slot], tsn.at[k, i], trc.at[k, i], device)
            for i, device in enumerate(peers)
        ]

    def tap_sum(k, cps, count):
        for cp in cps:
            cp.wait_recv()
        total = tl[k, 0]
        for i in range(1, count):
            total = total + tl[k, i]
        return total

    tcp = tap_send(0, [core], c)
    fcp.wait_recv()
    pcp.wait_recv()
    for cls in range(3):
        for z in range(4):
            for yl in range(2):
                at = pl.ds(pl.multiple_of((z * 4 + yl * 2 + c) * 48 + cls * 16, 16), 16)
                to = cls * 128 + z * 32 + yl * 16
                pdc[to : to + 16, 0:128] = pd_ref[at, :]
                pdc[to : to + 16, 128:256] = pdo[at, :]

    def add(dst, src):
        dst[...] = (dst[...].astype(F32) + src[...].astype(F32)).astype(BF)

    def feat_part(qs):
        @pl.loop(qs.start, qs.stop)
        def _(q):
            total = None
            for cls in range(3):
                term = lax.dot_general(
                    pdt[:, cls * 256 : (cls + 1) * 256], wide_block(g_ref, cls, q // 4, lax.rem(q, 4)), dims(1, 0),
                    preferred_element_type=F32,
                )
                total = term if total is None else total + term
            fgrad_ref[pl.ds(pl.multiple_of(q * 512, 512), 512), :] = total.T.astype(BF)

    def back(cls, phase, k, src, dst, device):
        return push(src, dst, ss2.at[cls, phase, k], rs2.at[cls, phase, k], device)

    def prow(cls, d2, d1):
        i2, i1, _ = index[cls]
        return p.at[cls, off(i2, d2), off(i1, d1)]

    relay = ((2, 1), (0, 3))
    hops, came = [], []
    for cls in range(3):
        hops.append({})
        came.append({})
    for cls in range(3):

        @pl.loop(0, 8)
        def _(q):
            cols = pl.ds(pl.multiple_of(q * 512, 512), 512)
            part = lax.dot_general(
                pdc[cls * 128 : (cls + 1) * 128, :],
                jnp.concatenate([feat_ref[cols, :], fo_ref[cols, :]], axis=1),
                dims(1, 1),
                preferred_element_type=F32,
            ).astype(BF)
            for z in range(4):
                for yl in range(2):
                    k = z * 32 + yl * 16
                    i2, i1, i0 = piece_index(cls, z, q // 4, yl, lax.rem(q, 4))
                    p[cls, i2, i1, i0] = part[k : k + 16, :]
        right, left = near_by(cls, 2)
        for j in range(2):
            hops[cls][0, j] = back(cls, 2, j, prow(cls, 2, relay[j][0]), ra3.at[cls, j], right)
            hops[cls][1, j] = back(cls, 2, 2 + j, prow(cls, 2, relay[j][1]), rb3.at[cls, j], left)
        for j in range(2):
            d = relay[j][0]
            came[cls][1, d] = back(cls, 2, 8 + d, prow(cls, 3, d), rd3.at[cls, d], left)
            d = relay[j][1]
            came[cls][0, d] = back(cls, 2, 4 + d, prow(cls, 1, d), rc3.at[cls, d], right)
    pdt[...] = jnp.concatenate(
        [
            pd_ref[m * 48 + cls * 16 : m * 48 + cls * 16 + 16, :].astype(F32)
            for cls in range(3)
            for m in range(16)
        ],
        axis=0,
    ).T.astype(BF)
    build_toeplitz(tt.at[1], gf, 1)
    for j in range(2):
        for cls in range(3):
            right, left = near_by(cls, 2)
            d = relay[j][0]
            hops[cls][0, j].wait_recv()
            add(prow(cls, 1, d), ra3.at[cls, j])
            came[cls][0, d] = back(cls, 2, 4 + d, prow(cls, 1, d), rc3.at[cls, d], right)
            d = relay[j][1]
            hops[cls][1, j].wait_recv()
            add(prow(cls, 3, d), rb3.at[cls, j])
            came[cls][1, d] = back(cls, 2, 8 + d, prow(cls, 3, d), rd3.at[cls, d], left)
    tl[1, pos["x"]] = tap_sum(0, tcp, 2)
    tcp = tap_send(1, line["x"], pos["x"])

    @pl.loop(0, 2)
    def _(ch):
        (y,) = toeplitz_product(tt.at[ch], xc.at[ch], 1)
        hf[ch] = lax.dot_general(anti, y, dims(1, 1), preferred_element_type=F32)

    deal(hf[...].reshape(256, 128), send_c)
    fg_half = hand(send_c, mid_c, 1)
    feat_part(range(2))

    def finish_row(cls, d):
        came[cls][0, d].wait_recv()
        came[cls][1, d].wait_recv()
        mine = prow(cls, 0, d)
        total = mine[...].astype(F32) + rc3[cls, d].astype(F32) + rd3[cls, d].astype(F32)
        mine[...] = total.astype(BF)

    legs = [[] for _ in range(3)]
    for d in (2, 1, 3):
        for cls in range(3):
            finish_row(cls, d)
            device = shifted(pos, ORDERS[cls][1], d)
            legs[cls].append(back(cls, 1, d, prow(cls, 0, d), rq.at[cls, d - 1], device))
    for cls in range(3):
        finish_row(cls, 0)
    tl[2, pos["y"]] = tap_sum(1, tcp, 4)
    tcp = tap_send(2, line["y"], pos["y"])
    fgx = pass_on(fg_half, mid_c, turn_c, land_c, 1)
    feat_part(range(2, 6))
    low = []

    def part_of(cls, d):
        i2, i1, i0 = index[cls]
        return p.at[cls, i2, i1, off(i0, d)]

    for cls in range(3):
        mine = prow(cls, 0, 0)
        total = mine[...].astype(F32)
        for cp in legs[cls]:
            cp.wait_recv()
        for k in range(3):
            total = total + rq[cls, k].astype(F32)
        mine[...] = total.astype(BF)
        low.append(
            [
                back(cls, 0, d, part_of(cls, d), rz.at[cls, d - 1], shifted(pos, ORDERS[cls][0], d))
                for d in (1, 2, 3)
            ]
        )
    tl[3, pos["z"]] = tap_sum(2, tcp, 4)
    tcp = tap_send(3, line["z"], pos["z"])
    feat_part(range(6, 8))
    store(1, fgrad_ref, fgrad_hbm)
    for cls in range(3):
        total = part_of(cls, 0)[...].astype(F32)
        for k in range(3):
            low[cls][k].wait_recv()
            total = total + rz[cls, k].astype(F32)
        blk[cls * 16 : (cls + 1) * 16, :] = total

    for q in range(8):
        stage2[q, 0:6, :] = blk[q * 6 : (q + 1) * 6, :]
        stage2[q, 6:8, :] = jnp.zeros((2, 512), F32)
    final = []
    for i in range(1, 8):
        q = lax.rem(w + i, 8)
        final.append(push(stage2.at[q], land2.at[w], s02.at[i], r02.at[i], (n, q)))
    land2[w] = stage2[w]
    tout_ref[...] = tap_sum(3, tcp, 4)[0:3]
    store(3, tout_ref, tout_hbm)
    fgout_ref[...] = jnp.concatenate(gathered(fgx, land_c), axis=0).astype(BF)
    store(2, fgout_ref, fgout_hbm)
    for cp in final:
        cp.wait_recv()
    for q in range(8):
        grad_ref[:, q * 512 : (q + 1) * 512] = land2[q, 0:6, :]
    store(4, grad_ref, grad_hbm)
    for cp in started:
        cp.wait_send()
    for cp in stores:
        cp.wait()


ANY = pl.BlockSpec(memory_space=pl.ANY)


def hyena(in_proj, features, taps, out_grad, long_filter):
    sem = pltpu.SemaphoreType.DMA
    vm = pltpu.VMEM
    tile = (128, 8, 128)
    return pl.pallas_call(
        hyena_kernel,
        out_shape=(
            jax.ShapeDtypeStruct((256, 128), BF),
            jax.ShapeDtypeStruct((4096, 128), BF),
            jax.ShapeDtypeStruct((256, 128), BF),
            jax.ShapeDtypeStruct((3, 768), F32),
            jax.ShapeDtypeStruct((6, 4096), F32),
        ),
        in_specs=[ANY] * 5,
        out_specs=(ANY,) * 5,
        scratch_shapes=[
            vm((256, 128), BF), vm((4096, 128), BF), vm((256, 128), BF), vm((3, 768), F32), vm((6, 4096), F32), sem((5,)),
            vm((6, 4096), BF), vm((4096, 128), BF), vm((3, 768), F32), vm((256, 128), BF), vm((256, 128), BF),
            vm((8, 8, 512), F32), vm((8, 8, 512), F32), vm((48, 512), F32),
            vm((2, 16, 512), BF), vm((2, 16, 512), BF), vm((4096, 256), BF),
            vm((3, 2, 4, 4, 4, 16, 512), BF), vm((4096, 128), BF),
            vm((768, 128), F32), vm((768, 128), F32), vm((768, 128), F32),
            vm((1024, 128), F32),
        ]
        + [vm((8, 32, 128), BF), vm((16, 16, 128), BF)]
        + [vm(tile, BF)] * 4
        + [vm((8, 32, 128), BF), vm((16, 16, 128), BF)]
        + [
            vm((256, 128), BF), vm((2, 128, 128), F32), vm((2, 128, 128), F32),
            vm((3, 256, 128), F32), vm((3, 256, 128), F32),
            vm((2, 1024, 2048), BF), vm((2, 128, 128), BF), vm((128, 128), F32), vm((2048, 256), BF), vm((2, 2048, 128), BF),
            vm((768, 128), BF),
            vm((768, 128), BF), vm((384, 256), BF), vm((3, 4, 4, 4, 16, 512), BF),
            vm((3, 2, 4, 16, 512), BF), vm((3, 2, 4, 16, 512), BF),
            vm((3, 4, 4, 16, 512), BF), vm((3, 4, 4, 16, 512), BF),
            vm((3, 3, 4, 16, 512), BF),
            vm((3, 3, 16, 512), BF), vm((8, 32, 128), BF), vm((8, 32, 128), BF),
            vm((16, 16, 128), BF), vm((16, 16, 128), BF), vm((256, 128), F32), vm((256, 128), F32),
            vm((8, 8, 512), F32), vm((8, 8, 512), F32), vm((4, 4, 8, 768), F32), vm((128, 768), BF), vm((2, 16, 512), F32), vm((16, 4096), F32),
            sem((5,)), sem((8,)), sem((8,)),
            sem((3, 3, 12)), sem((3, 3, 12)), sem((3, 4)), sem((3, 4)),
            sem((2,)), sem((2,)), sem, sem, sem((4,)), sem((4,)), sem, sem,
            sem, sem, sem((3, 3, 12)), sem((3, 3, 12)), sem((8,)), sem((8,)), sem((4, 3)), sem((4, 3)),
            pltpu.SemaphoreType.REGULAR((3,)),
            sem((2, 8)), sem((2, 8)), sem((2, 16)), sem((2, 16)),
        ],
        compiler_params=pltpu.CompilerParams(
            collective_id=1, has_side_effects=True, vmem_limit_bytes=58 * 1024 * 1024
        ),
        name="hyena",
    )(in_proj, features, taps, out_grad, long_filter)


def copy_kernel(*refs):
    sources, targets, held, (came, left) = refs[:5], refs[5:10], refs[10:15], refs[15:]
    inward = [pltpu.make_async_copy(sources[k], held[k], came.at[k]) for k in range(5)]
    outward = [pltpu.make_async_copy(held[k], targets[k], left.at[k]) for k in range(5)]
    for cp in inward:
        cp.start()
    for k in range(5):
        inward[k].wait()
        outward[k].start()
    for cp in outward:
        cp.wait()


def settle(arrays):
    return pl.pallas_call(
        copy_kernel,
        out_shape=tuple(jax.ShapeDtypeStruct(a.shape, a.dtype) for a in arrays),
        in_specs=[ANY] * 5,
        out_specs=(ANY,) * 5,
        scratch_shapes=[pltpu.VMEM(a.shape, a.dtype) for a in arrays]
        + [pltpu.SemaphoreType.DMA((5,)), pltpu.SemaphoreType.DMA((5,))],
        name="settle",
    )(*arrays)


def local(features, in_proj, short_taps, long_filter, out_grad):
    return settle(hyena(in_proj, features, short_taps, out_grad, long_filter))


def solution(mesh):
    tokens = P(None, AXES)
    rows = P(AXES, None)
    return jax.shard_map(
        local,
        mesh=mesh,
        in_specs=(tokens, rows, P(), tokens, tokens),
        out_specs=(tokens, tokens, tokens, P(), rows),
        check_vma=False,
    )
```

```python
import math

import jax
import jax.numpy as jnp
from jax import lax
from jax.experimental import pallas as pl
from jax.experimental.pallas import tpu as pltpu
from jax.sharding import PartitionSpec as P

MESH = pl.DeviceIdType.MESH
BF = jnp.bfloat16
F32 = jnp.float32
ORDERS = (("x", "y", "z"), ("y", "z", "x"), ("z", "x", "y"))
AXES = ("narrow", "wide")


def place(pos):
    y = pos["y"]
    return (pos["z"] * 4 + lax.rem(y, 2) * 2 + pos["c"], (y // 2) * 4 + pos["x"])


def position():
    n = lax.axis_index("narrow")
    w = lax.axis_index("wide")
    pos = {
        "x": lax.rem(w, 4),
        "y": (w // 4) * 2 + lax.rem(n // 2, 2),
        "z": n // 4,
        "c": lax.rem(n, 2),
    }
    return n, w, pos


def shifted(pos, axis, by):
    other = dict(pos)
    other[axis] = lax.rem(pos[axis] + by + 4, 4)
    return place(other)


def other_core(pos):
    other = dict(pos)
    other["c"] = 1 - pos["c"]
    return place(other)


def shard_id(s):
    return (s // 8, lax.rem(s, 8))


def remote(src, dst, send, recv, device):
    return pltpu.make_async_remote_copy(
        src_ref=src, dst_ref=dst, send_sem=send, recv_sem=recv, device_id=device, device_id_type=MESH
    )


def greet(devices):
    barrier = pltpu.get_barrier_semaphore()
    for device in devices:
        pl.semaphore_signal(barrier, inc=1, device_id=device, device_id_type=MESH)
    pl.semaphore_wait(barrier, len(devices))


def piece_index(cls, z, yh, yl, x):
    at = {"x": x, "y": yh * 2 + yl, "z": z}
    d0, d1, d2 = ORDERS[cls]
    return (at[d2], at[d1], at[d0])


def dims(a, b):
    return (((a,), (b,)), ((), ()))


def lanes(rows):
    return lax.broadcasted_iota(jnp.int32, (rows, 128), 1)


def one_hot(rows, cols, test):
    r = lax.broadcasted_iota(jnp.int32, (rows, cols), 0)
    c = lax.broadcasted_iota(jnp.int32, (rows, cols), 1)
    return jnp.where(test(r, c), 1.0, 0.0).astype(BF)


def wide_block(g_ref, cls, yh, x):
    parts = []
    for z in range(4):
        for yl in range(2):
            for core in range(2):
                i2, i1, i0 = piece_index(cls, z, yh, yl, x)
                parts.append(g_ref[cls, core, i2, i1, i0])
    return jnp.concatenate(parts, axis=0)


def half(ref, phase, k):
    if phase == 0:
        return ref.at[:, pl.ds(k * 256, 256)]
    return ref.at[pl.ds(k * 2, 2)]


def build_toeplitz(tt, h_ref, ch):
    lane = lanes(128)
    row = lax.broadcasted_iota(jnp.int32, (128, 128), 0)
    upper = lane >= row

    def rolled(k):
        taps = jnp.broadcast_to(h_ref[ch, pl.ds(k, 1), :], (128, 128))
        return pltpu.roll(taps, 0, 1, stride=1, stride_axis=0)

    @pl.loop(0, 8)
    def _(g):
        prev = jnp.where(g > 0, rolled(jnp.maximum(16 * g - 1, 0)), 0.0)
        at = pl.ds(pl.multiple_of(g * 128, 128), 128)
        for i in range(16):
            cur = rolled(16 * g + i)
            tt[at, i * 128 : (i + 1) * 128] = jnp.where(upper, cur, prev).astype(BF)
            prev = cur


def spread_blocks(xs, col, x):
    lane = lanes(128)
    for i in range(16):
        moved = pltpu.roll(x, i, 1) if i else x
        xs[i * 128 : (i + 1) * 128, col * 128 : (col + 1) * 128] = jnp.where(lane < i, 0.0, moved).astype(BF)


def toeplitz_product(tt, xs, cols):
    lane = lanes(128)
    out = jnp.dot(tt[...], xs[:, 0 : cols * 128], preferred_element_type=F32)
    results = []
    for c in range(cols):
        at = slice(c * 128, (c + 1) * 128)
        acc = out[896:1024, at]
        for g in range(6, -1, -1):
            acc = jnp.where(lane < 16, 0.0, pltpu.roll(acc, 16, 1)) + out[g * 128 : (g + 1) * 128, at]
        results.append(acc.astype(BF))
    return results


def hyena_kernel(
    proj_hbm, feat_hbm, taps_hbm, og_hbm, lf_hbm,
    mixed_hbm, fgrad_hbm, fgout_hbm, tout_hbm, grad_hbm,
    mixed_ref, fgrad_ref, fgout_ref, tout_ref, grad_ref, outs,
    proj_ref, feat_ref, taps_ref, og_ref, lf_ref,
    stage, land, blk, rows, hland, fh, g_ref, fo_ref, p_ref, halo_ref, tcol,
    rowbuf, send_f, land_f, send_a, land_a, send_b, land_b, send_c, land_c,
    ogn, hf, gf, feat, featn, tt, cots, ahead_ref, xs, xc, pd_ref,
    pdo, pdc, p, ra3, rb3, rc3, rd3, rq, rz, mid_f, mid_c, turn_f, turn_c, rows_a, rows_b,
    stage2, land2, tl, pdt, rowf, both,
    ins, s0, r0, ss, rs, ds, dr, hs, hr, fs, fr, xsend, xrecv, os, orr,
    ps, pr, ss2, rs2, s02, r02, tsn, trc, near, xs1, xr1, xs2, xr2,
):
    n, w, pos = position()
    c = pos["c"]
    s = n * 8 + w
    right_shard = shard_id(lax.rem(s + 1, 128))
    left_shard = shard_id(lax.rem(s + 127, 128))
    wide_peers = [(n, lax.rem(w + i, 8)) for i in range(1, 8)]
    line = {a: [shifted(pos, a, d) for d in (1, 2, 3)] for a in "xyz"}
    core = other_core(pos)
    copies = [
        pltpu.make_async_copy(a, b, ins.at[k])
        for k, (a, b) in enumerate(
            ((proj_hbm, proj_ref), (feat_hbm, feat_ref), (taps_hbm, taps_ref), (og_hbm, og_ref), (lf_hbm, lf_ref))
        )
    ]
    for cp in copies:
        cp.start()
    barrier = pltpu.get_barrier_semaphore()
    greeted = wide_peers + line["y"] + line["z"] + [core, right_shard, left_shard]
    for device in greeted:
        pl.semaphore_signal(barrier, inc=1, device_id=device, device_id_type=MESH)
    copies[0].wait()
    for q in range(8):
        stage[q, 0:6, :] = proj_ref[:, q * 512 : (q + 1) * 512].astype(F32)
        stage[q, 6:8, :] = jnp.zeros((2, 512), F32)
    pl.semaphore_wait(barrier, len(greeted))

    def tell(k, devices):
        for device in devices:
            pl.semaphore_signal(near.at[k], inc=1, device_id=device, device_id_type=MESH)

    started = []
    stores = []

    def store(k, src, dst):
        cp = pltpu.make_async_copy(src, dst, outs.at[k])
        cp.start()
        stores.append(cp)

    def push(src, dst, a, b, device):
        cp = remote(src, dst, a, b, device)
        cp.start()
        started.append(cp)
        return cp

    first = []
    for i in range(1, 8):
        q = lax.rem(w + i, 8)
        first.append(push(stage.at[q], land.at[w], s0.at[i], r0.at[i], (n, q)))
    tell(0, line["x"])
    land[w] = stage[w]
    for cp in first:
        cp.wait_recv()
    for q in range(8):
        blk[q * 6 : (q + 1) * 6, :] = land[q, 0:6, :]

    index = [[pos[a] for a in reversed(order)] for order in ORDERS]
    for cls in range(3):
        i2, i1, i0 = index[cls]
        g_ref[cls, c, i2, i1, i0] = blk[cls * 16 : (cls + 1) * 16, :].astype(BF)

    d2d = []

    def cross(cls, j, k):
        ref = g_ref.at[cls, c, j]
        d2d.append(push(ref, ref, ds.at[cls, k], dr.at[cls, k], core))

    def exchange(src, dst, k):
        ww = [lax.rem(w + j, 8) for j in range(8)]
        for j in range(1, 8):
            remote(src.at[n * 8 + ww[j]], dst.at[s], xsend.at[k], xrecv.at[k], (n, ww[j])).start()

        @pl.loop(1, 16)
        def _(i):
            nn = lax.rem(n + i, 16)
            for j in range(8):
                remote(src.at[nn * 8 + ww[j]], dst.at[s], xsend.at[k], xrecv.at[k], (nn, ww[j])).start()

        dst[s] = src[s]
        whole = pl.ds(0, 127)
        cp = remote(src.at[whole], dst.at[whole], xsend.at[k], xrecv.at[k], (n, w))
        started.append(cp)
        return cp

    def deal(value, src):
        rows_a[...] = value
        for q in range(8):
            for r in range(2):
                rows_b[pl.ds(q * 32 + r, 16, stride=2), :] = rows_a[pl.ds(r * 128 + q, 16, stride=8), :]
        src[...] = rows_b[...].astype(BF).reshape(8, 32, 128)

    def hand(src, mid, k):
        cps = []
        for i in range(1, 8):
            q = lax.rem(w + i, 8)
            cps.append(push(src.at[q], mid.at[w], xs1.at[k, i], xr1.at[k, i], (n, q)))
        mid[w] = src[w]
        return cps

    def pass_on(cps, mid, turned, dst, k):
        for cp in cps:
            cp.wait_recv()
        rows_a[...] = mid[...].astype(F32).reshape(256, 128)
        for q in range(8):
            for r in range(2):
                rows_b[pl.ds(q * 2 + r, 16, stride=16), :] = rows_a[pl.ds(q * 32 + r, 16, stride=2), :]
        turned[...] = rows_b[...].astype(BF).reshape(16, 16, 128)
        out = []
        for i in range(1, 16):
            m = lax.rem(n + i, 16)
            out.append(push(turned.at[m], dst.at[n], xs2.at[k, i], xr2.at[k, i], (m, w)))
        dst[n] = turned[n]
        return out

    def gathered(cps, dst):
        for cp in cps:
            cp.wait_recv()
        rows_a[...] = dst[...].astype(F32).reshape(256, 128)
        return [rows_a[pl.ds(r, 128, stride=2), :] for r in range(2)]

    def pack(buf, parts):
        for r, value in parts.items():
            rowbuf[pl.ds(r, 128, stride=8), :] = value
        buf[...] = rowbuf[...].reshape(buf.shape).astype(BF)

    def unpack(buf):
        rowbuf[...] = buf[...].astype(F32).reshape(1024, 128)

    def plane(r):
        return rowbuf[pl.ds(r, 128, stride=8), :]

    def piece(cls, i2, i1, i0):
        return g_ref.at[cls, c, i2, i1, i0]

    def row_of(cls, i2, i1):
        return g_ref.at[cls, c, i2, i1]

    def near_by(cls, phase):
        axis = ORDERS[cls][phase]
        return shifted(pos, axis, 1), shifted(pos, axis, -1)

    def ring(cls, phase, k, ref, device):
        return push(ref, ref, ss.at[cls, phase, k], rs.at[cls, phase, k], device)

    def off(i, d):
        return lax.rem(i + d, 4)

    legs = []
    for cls in range(3):
        mine = piece(cls, *index[cls])
        legs.append([ring(cls, 0, d, mine, shifted(pos, ORDERS[cls][0], d)) for d in (1, 2, 3)])
    pl.semaphore_wait(near.at[0], 3)
    tell(1, line["y"])
    copies[1].wait()
    sel = one_hot(
        16, 128, lambda r, l: ((r < 2) & (l == r + 126)) | ((r >= 2) & (r < 4) & (l == r - 2))
    )
    edge = lax.dot_general(sel, feat_ref[...], dims(1, 1), preferred_element_type=F32)
    for k in range(4):
        for q in range(8):
            at = (k % 2) * 8 + q
            rowf[k // 2, at : at + 1, :] = edge[k : k + 1, q * 512 : (q + 1) * 512]
    rows[...] = rowf[...].astype(BF)
    firsts, legs = legs, []
    far = [[None] * 4 for _ in range(3)]

    def spread_row(cls, d):
        i2, i1, _ = index[cls]
        right, left = near_by(cls, 2)
        ref = row_of(cls, i2, off(i1, d))
        far[cls][d] = (ring(cls, 2, 2 * d, ref, right), ring(cls, 2, 2 * d + 1, ref, left))

    for cls in range(3):
        i2, i1, _ = index[cls]
        for cp in firsts[cls]:
            cp.wait_recv()
        mine = row_of(cls, i2, i1)
        legs.append([ring(cls, 1, d, mine, shifted(pos, ORDERS[cls][1], d)) for d in (1, 3, 2)])
    for cls in range(3):
        spread_row(cls, 0)
    pl.semaphore_wait(near.at[1], 3)
    tell(2, [core])
    copies[4].wait()
    lf = lf_ref[...].astype(F32)
    rowbuf[...] = jnp.zeros((1024, 128), F32)
    deal(lf, send_f)
    lf_half = hand(send_f, mid_f, 0)
    ha = push(rows.at[0], hland.at[0], hs.at[0], hr.at[0], right_shard)
    hb = push(rows.at[1], hland.at[1], hs.at[1], hr.at[1], left_shard)
    pl.semaphore_wait(near.at[2], 1)
    for k, d in ((0, 3), (1, 1), (2, 2)):
        for cls in range(3):
            legs[cls][k].wait_recv()
            spread_row(cls, d)
    for cls in range(3):
        cross(cls, index[cls][0], 0)
    lfx = pass_on(lf_half, mid_f, turn_f, land_f, 0)
    fh[:, 0:128] = feat_ref[...]
    copies[2].wait()
    tc = jnp.concatenate([taps_ref[...], jnp.zeros((125, 768), F32)], axis=0)
    for k in range(6):
        tcol[k * 128 : (k + 1) * 128, :] = tc[:, k * 128 : (k + 1) * 128].T
    ha.wait_recv()
    hb.wait_recv()
    rowf[...] = hland[...].astype(F32)
    both[...] = jnp.zeros((16, 4096), F32)
    for k in range(4):
        for q in range(8):
            at = (k % 2) * 8 + q
            both[k : k + 1, q * 512 : (q + 1) * 512] = rowf[k // 2, at : at + 1, :]
    lo = jnp.where(s > 0, 0, 2)
    hi = jnp.where(s < 127, 4, 2)
    spread = one_hot(16, 128, lambda r, l: (r == l) & (r >= lo) & (r < hi))
    fh[:, 128:256] = lax.dot_general(
        both[...].astype(BF), spread, dims(0, 0), preferred_element_type=F32
    ).astype(BF)
    relays = []
    for d, k in ((0, 0), (3, 1), (1, 0), (2, 1)):
        for cls in range(3):
            i2, i1, _ = index[cls]
            far[cls][d][k].wait_recv()
            ref = row_of(cls, off(i2, 1 if k else 3), off(i1, d))
            relays.append(ring(cls, 2, 8 + d, ref, near_by(cls, 2)[k]))
    for cls in range(3):
        for d, k in ((0, 1), (3, 0), (1, 1), (2, 0)):
            far[cls][d][k].wait_recv()
        cross(cls, off(index[cls][0], 3), 1)
        cross(cls, off(index[cls][0], 1), 2)
    for ch, taps in enumerate(gathered(lfx, land_f)):
        hf[ch] = taps
    build_toeplitz(tt.at[0], hf, 0)
    for cp in relays:
        cp.wait_recv()
    for cls in range(3):
        cross(cls, off(index[cls][0], 2), 3)
    fcp = push(feat_ref, fo_ref, fs, fr, core)
    copies[3].wait()
    ocp = push(og_ref, ogn, os, orr, left_shard)
    for cp in d2d:
        cp.wait_recv()

    for cls in range(3):
        acc = None
        for q in range(8):
            lhs = wide_block(g_ref, cls, q // 4, q % 4)
            term = jnp.dot(lhs, fh[q * 512 : (q + 1) * 512, :], preferred_element_type=F32)
            acc = term if acc is None else acc + term
        for m in range(16):
            at = slice(m * 48 + cls * 16, m * 48 + cls * 16 + 16)
            p_ref[at, :] = acc[m * 16 : (m + 1) * 16, 0:128]
            halo_ref[at, :] = acc[m * 16 : (m + 1) * 16, 128:256]

    lane = lanes(256)
    for part in range(3):
        at = slice(part * 256, (part + 1) * 256)
        v = p_ref[at, :]
        halo = halo_ref[at, :]
        t0, t1, t2 = tcol[at, 0:1], tcol[at, 1:2], tcol[at, 2:3]
        v1 = jnp.where(lane < 1, pltpu.roll(halo, 127, 1), pltpu.roll(v, 1, 1))
        v2 = jnp.where(lane < 2, halo, pltpu.roll(v, 2, 1))
        feat[part] = t0 * v + t1 * v1 + t2 * v2
        n1 = jnp.where(lane < 1, pltpu.roll(v, 1, 1), pltpu.roll(halo, 127, 1))
        featn[part] = t0 * pltpu.roll(halo, 126, 1) + t1 * n1 + t2 * pltpu.roll(v, 2, 1)
    og = og_ref[...].astype(F32)
    gated = feat[1] * feat[2]
    cot = og * feat[0]
    pack(send_a, {0: gated[0:128], 1: gated[128:256], 2: cot[0:128], 3: cot[128:256]})
    go = exchange(send_a, land_a, 1)
    build_toeplitz(tt.at[1], hf, 1)
    go.wait_recv()
    unpack(land_a)

    anti = one_hot(128, 128, lambda r, l: r + l == 127)
    row = lax.broadcasted_iota(jnp.int32, (128, 128), 0)
    lane1 = lanes(128)
    for ch in range(2):
        gf[ch] = plane(ch)
        cots[ch] = plane(2 + ch).astype(BF)
    ahead_ref[...] = jnp.zeros((128, 128), F32)

    @pl.loop(0, 2)
    def _(ch):
        xg = lax.dot_general(anti, gf[ch].astype(BF), dims(1, 1), preferred_element_type=F32)
        back_in = lax.dot_general(cots[ch], anti, dims(0, 0), preferred_element_type=F32)
        spread_blocks(xs, 1, xg)
        spread_blocks(xs, 0, back_in)
        xc[ch] = xs[:, 0:128]
        yc, yg = toeplitz_product(tt.at[ch], xs, 2)
        conv = lax.dot_general(yg, anti, dims(0, 0), preferred_element_type=F32)
        gg = lax.dot_general(anti, yc, dims(1, 1), preferred_element_type=F32)
        rowbuf[pl.ds(ch, 128, stride=8), :] = conv
        rowbuf[pl.ds(2 + ch, 128, stride=8), :] = gg
        for r, value in ((0, conv), (4, gg)):
            nxt = pltpu.roll(jnp.where(row < 127, pltpu.roll(value, 127, 0), 0.0), r + 2 * ch, 1)
            keep = (lane1 >= r + 2 * ch) & (lane1 < r + 2 * ch + 2)
            ahead_ref[...] = jnp.where(keep, nxt, ahead_ref[...])

    ahead = ahead_ref[...]
    pack(send_b, {4: ahead})
    ret = exchange(send_b, land_b, 2)
    build_toeplitz(tt.at[0], gf, 0)
    ocp.wait_recv()
    ret.wait_recv()
    unpack(land_b)

    def channels(r):
        return jnp.concatenate([plane(r), plane(r + 1)], axis=0)

    conv, gg = channels(0), channels(2)
    ahead = plane(4)
    convn = jnp.concatenate([ahead, pltpu.roll(ahead, 126, 1)], axis=0)
    ggn = jnp.concatenate([pltpu.roll(ahead, 124, 1), pltpu.roll(ahead, 122, 1)], axis=0)
    mixed_ref[...] = (feat[0] * conv).astype(BF)
    store(0, mixed_ref, mixed_hbm)
    ogv = ogn[...].astype(F32)
    last = s == 127

    def derivative(part):
        if part == 0:
            return og * conv
        return gg * feat[3 - part]

    for part in range(3):
        at = slice(part * 256, (part + 1) * 256)
        fd = derivative(part)
        fdn = ogv * convn if part == 0 else ggn * featn[3 - part]
        fdn = jnp.where(last, 0.0, fdn)
        t0, t1, t2 = tcol[at, 0:1], tcol[at, 1:2], tcol[at, 2:3]
        f1 = jnp.where(lane < 127, pltpu.roll(fd, 127, 1), pltpu.roll(fdn, 127, 1))
        f2 = jnp.where(lane < 126, pltpu.roll(fd, 126, 1), pltpu.roll(fdn, 126, 1))
        pd_ref[at, :] = (t0 * fd + t1 * f1 + t2 * f2).astype(BF)
    pcp = push(pd_ref, pdo, ps, pr, core)

    for part in range(3):
        at = slice(part * 256, (part + 1) * 256)
        fd = derivative(part)
        v = p_ref[at, :]
        halo = halo_ref[at, :]
        v1 = jnp.where(lane < 1, pltpu.roll(halo, 127, 1), pltpu.roll(v, 1, 1))
        v2 = jnp.where(lane < 2, halo, pltpu.roll(v, 2, 1))
        total = jnp.zeros((256, 128), F32)
        for k, q in enumerate((v, v1, v2)):
            total = jnp.where(lane == k, jnp.sum(fd * q, axis=1, keepdims=True), total)
        tl[0, c, :, at] = total.T[0:8, :]

    def tap_send(k, peers, slot):
        return [
            push(tl.at[k, slot], tl.at[k, slot], tsn.at[k, i], trc.at[k, i], device)
            for i, device in enumerate(peers)
        ]

    def tap_sum(k, cps, count):
        for cp in cps:
            cp.wait_recv()
        total = tl[k, 0]
        for i in range(1, count):
            total = total + tl[k, i]
        return total

    tcp = tap_send(0, [core], c)
    fcp.wait_recv()
    pcp.wait_recv()
    for cls in range(3):
        for z in range(4):
            for yl in range(2):
                at = pl.ds(pl.multiple_of((z * 4 + yl * 2 + c) * 48 + cls * 16, 16), 16)
                to = cls * 128 + z * 32 + yl * 16
                pdc[to : to + 16, 0:128] = pd_ref[at, :]
                pdc[to : to + 16, 128:256] = pdo[at, :]

    def add(dst, src):
        dst[...] = (dst[...].astype(F32) + src[...].astype(F32)).astype(BF)

    def feat_part(qs):
        @pl.loop(qs.start, qs.stop)
        def _(q):
            total = None
            for cls in range(3):
                term = lax.dot_general(
                    pdt[:, cls * 256 : (cls + 1) * 256], wide_block(g_ref, cls, q // 4, lax.rem(q, 4)), dims(1, 0),
                    preferred_element_type=F32,
                )
                total = term if total is None else total + term
            fgrad_ref[pl.ds(pl.multiple_of(q * 512, 512), 512), :] = total.T.astype(BF)

    def back(cls, phase, k, src, dst, device):
        return push(src, dst, ss2.at[cls, phase, k], rs2.at[cls, phase, k], device)

    def prow(cls, d2, d1):
        i2, i1, _ = index[cls]
        return p.at[cls, off(i2, d2), off(i1, d1)]

    relay = ((2, 1), (0, 3))
    hops, came = [], []
    for cls in range(3):
        hops.append({})
        came.append({})
    for cls in range(3):

        @pl.loop(0, 8)
        def _(q):
            cols = pl.ds(pl.multiple_of(q * 512, 512), 512)
            part = lax.dot_general(
                pdc[cls * 128 : (cls + 1) * 128, :],
                jnp.concatenate([feat_ref[cols, :], fo_ref[cols, :]], axis=1),
                dims(1, 1),
                preferred_element_type=F32,
            ).astype(BF)
            for z in range(4):
                for yl in range(2):
                    k = z * 32 + yl * 16
                    i2, i1, i0 = piece_index(cls, z, q // 4, yl, lax.rem(q, 4))
                    p[cls, i2, i1, i0] = part[k : k + 16, :]
        right, left = near_by(cls, 2)
        for j in range(2):
            hops[cls][0, j] = back(cls, 2, j, prow(cls, 2, relay[j][0]), ra3.at[cls, j], right)
            hops[cls][1, j] = back(cls, 2, 2 + j, prow(cls, 2, relay[j][1]), rb3.at[cls, j], left)
        for j in range(2):
            d = relay[j][0]
            came[cls][1, d] = back(cls, 2, 8 + d, prow(cls, 3, d), rd3.at[cls, d], left)
            d = relay[j][1]
            came[cls][0, d] = back(cls, 2, 4 + d, prow(cls, 1, d), rc3.at[cls, d], right)
    pdt[...] = jnp.concatenate(
        [
            pd_ref[m * 48 + cls * 16 : m * 48 + cls * 16 + 16, :].astype(F32)
            for cls in range(3)
            for m in range(16)
        ],
        axis=0,
    ).T.astype(BF)
    build_toeplitz(tt.at[1], gf, 1)
    for j in range(2):
        for cls in range(3):
            right, left = near_by(cls, 2)
            d = relay[j][0]
            hops[cls][0, j].wait_recv()
            add(prow(cls, 1, d), ra3.at[cls, j])
            came[cls][0, d] = back(cls, 2, 4 + d, prow(cls, 1, d), rc3.at[cls, d], right)
            d = relay[j][1]
            hops[cls][1, j].wait_recv()
            add(prow(cls, 3, d), rb3.at[cls, j])
            came[cls][1, d] = back(cls, 2, 8 + d, prow(cls, 3, d), rd3.at[cls, d], left)
    tl[1, pos["x"]] = tap_sum(0, tcp, 2)
    tcp = tap_send(1, line["x"], pos["x"])

    @pl.loop(0, 2)
    def _(ch):
        (y,) = toeplitz_product(tt.at[ch], xc.at[ch], 1)
        hf[ch] = lax.dot_general(anti, y, dims(1, 1), preferred_element_type=F32)

    deal(hf[...].reshape(256, 128), send_c)
    fg_half = hand(send_c, mid_c, 1)
    feat_part(range(2))

    def finish_row(cls, d):
        came[cls][0, d].wait_recv()
        came[cls][1, d].wait_recv()
        mine = prow(cls, 0, d)
        total = mine[...].astype(F32) + rc3[cls, d].astype(F32) + rd3[cls, d].astype(F32)
        mine[...] = total.astype(BF)

    legs = [[] for _ in range(3)]
    for d in (2, 1, 3):
        for cls in range(3):
            finish_row(cls, d)
            device = shifted(pos, ORDERS[cls][1], d)
            legs[cls].append(back(cls, 1, d, prow(cls, 0, d), rq.at[cls, d - 1], device))
    for cls in range(3):
        finish_row(cls, 0)
    tl[2, pos["y"]] = tap_sum(1, tcp, 4)
    tcp = tap_send(2, line["y"], pos["y"])
    fgx = pass_on(fg_half, mid_c, turn_c, land_c, 1)
    feat_part(range(2, 6))
    low = []

    def part_of(cls, d):
        i2, i1, i0 = index[cls]
        return p.at[cls, i2, i1, off(i0, d)]

    for cls in range(3):
        mine = prow(cls, 0, 0)
        total = mine[...].astype(F32)
        for cp in legs[cls]:
            cp.wait_recv()
        for k in range(3):
            total = total + rq[cls, k].astype(F32)
        mine[...] = total.astype(BF)
        low.append(
            [
                back(cls, 0, d, part_of(cls, d), rz.at[cls, d - 1], shifted(pos, ORDERS[cls][0], d))
                for d in (1, 2, 3)
            ]
        )
    tl[3, pos["z"]] = tap_sum(2, tcp, 4)
    tcp = tap_send(3, line["z"], pos["z"])
    feat_part(range(6, 8))
    store(1, fgrad_ref, fgrad_hbm)
    for cls in range(3):
        total = part_of(cls, 0)[...].astype(F32)
        for k in range(3):
            low[cls][k].wait_recv()
            total = total + rz[cls, k].astype(F32)
        blk[cls * 16 : (cls + 1) * 16, :] = total

    for q in range(8):
        stage2[q, 0:6, :] = blk[q * 6 : (q + 1) * 6, :]
        stage2[q, 6:8, :] = jnp.zeros((2, 512), F32)
    final = []
    for i in range(1, 8):
        q = lax.rem(w + i, 8)
        final.append(push(stage2.at[q], land2.at[w], s02.at[i], r02.at[i], (n, q)))
    land2[w] = stage2[w]
    tout_ref[...] = tap_sum(3, tcp, 4)[0:3]
    store(3, tout_ref, tout_hbm)
    fgout_ref[...] = jnp.concatenate(gathered(fgx, land_c), axis=0).astype(BF)
    store(2, fgout_ref, fgout_hbm)
    for cp in final:
        cp.wait_recv()
    for q in range(8):
        grad_ref[:, q * 512 : (q + 1) * 512] = land2[q, 0:6, :]
    store(4, grad_ref, grad_hbm)
    for cp in started:
        cp.wait_send()
    for cp in stores:
        cp.wait()


ANY = pl.BlockSpec(memory_space=pl.ANY)


def hyena(in_proj, features, taps, out_grad, long_filter):
    sem = pltpu.SemaphoreType.DMA
    vm = pltpu.VMEM
    tile = (128, 8, 128)
    return pl.pallas_call(
        hyena_kernel,
        out_shape=(
            jax.ShapeDtypeStruct((256, 128), BF),
            jax.ShapeDtypeStruct((4096, 128), BF),
            jax.ShapeDtypeStruct((256, 128), BF),
            jax.ShapeDtypeStruct((3, 768), F32),
            jax.ShapeDtypeStruct((6, 4096), F32),
        ),
        in_specs=[ANY] * 5,
        out_specs=(ANY,) * 5,
        scratch_shapes=[
            vm((256, 128), BF), vm((4096, 128), BF), vm((256, 128), BF), vm((3, 768), F32), vm((6, 4096), F32), sem((5,)),
            vm((6, 4096), BF), vm((4096, 128), BF), vm((3, 768), F32), vm((256, 128), BF), vm((256, 128), BF),
            vm((8, 8, 512), F32), vm((8, 8, 512), F32), vm((48, 512), F32),
            vm((2, 16, 512), BF), vm((2, 16, 512), BF), vm((4096, 256), BF),
            vm((3, 2, 4, 4, 4, 16, 512), BF), vm((4096, 128), BF),
            vm((768, 128), F32), vm((768, 128), F32), vm((768, 128), F32),
            vm((1024, 128), F32),
        ]
        + [vm((8, 32, 128), BF), vm((16, 16, 128), BF)]
        + [vm(tile, BF)] * 4
        + [vm((8, 32, 128), BF), vm((16, 16, 128), BF)]
        + [
            vm((256, 128), BF), vm((2, 128, 128), F32), vm((2, 128, 128), F32),
            vm((3, 256, 128), F32), vm((3, 256, 128), F32),
            vm((2, 1024, 2048), BF), vm((2, 128, 128), BF), vm((128, 128), F32), vm((2048, 256), BF), vm((2, 2048, 128), BF),
            vm((768, 128), BF),
            vm((768, 128), BF), vm((384, 256), BF), vm((3, 4, 4, 4, 16, 512), BF),
            vm((3, 2, 4, 16, 512), BF), vm((3, 2, 4, 16, 512), BF),
            vm((3, 4, 4, 16, 512), BF), vm((3, 4, 4, 16, 512), BF),
            vm((3, 3, 4, 16, 512), BF),
            vm((3, 3, 16, 512), BF), vm((8, 32, 128), BF), vm((8, 32, 128), BF),
            vm((16, 16, 128), BF), vm((16, 16, 128), BF), vm((256, 128), F32), vm((256, 128), F32),
            vm((8, 8, 512), F32), vm((8, 8, 512), F32), vm((4, 4, 8, 768), F32), vm((128, 768), BF), vm((2, 16, 512), F32), vm((16, 4096), F32),
            sem((5,)), sem((8,)), sem((8,)),
            sem((3, 3, 12)), sem((3, 3, 12)), sem((3, 4)), sem((3, 4)),
            sem((2,)), sem((2,)), sem, sem, sem((4,)), sem((4,)), sem, sem,
            sem, sem, sem((3, 3, 12)), sem((3, 3, 12)), sem((8,)), sem((8,)), sem((4, 3)), sem((4, 3)),
            pltpu.SemaphoreType.REGULAR((3,)),
            sem((2, 8)), sem((2, 8)), sem((2, 16)), sem((2, 16)),
        ],
        compiler_params=pltpu.CompilerParams(
            collective_id=1, has_side_effects=True, vmem_limit_bytes=58 * 1024 * 1024
        ),
        name="hyena",
    )(in_proj, features, taps, out_grad, long_filter)


def copy_kernel(*refs):
    sources, targets, held, (came, left) = refs[:5], refs[5:10], refs[10:15], refs[15:]
    spans = [(1, pl.ds(1024 * i, 1024)) for i in range(4)] + [(k, slice(None)) for k in (0, 2, 3, 4)]
    inward, outward = [], []
    for i, (k, at) in enumerate(spans):
        inward.append(pltpu.make_async_copy(sources[k].at[at], held[k].at[at], came.at[i]))
        outward.append(pltpu.make_async_copy(held[k].at[at], targets[k].at[at], left.at[i]))
    for cp in inward:
        cp.start()
    for i in range(8):
        inward[i].wait()
        outward[i].start()
    for cp in outward:
        cp.wait()


def settle(arrays):
    return pl.pallas_call(
        copy_kernel,
        out_shape=tuple(jax.ShapeDtypeStruct(a.shape, a.dtype) for a in arrays),
        in_specs=[ANY] * 5,
        out_specs=(ANY,) * 5,
        scratch_shapes=[pltpu.VMEM(a.shape, a.dtype) for a in arrays]
        + [pltpu.SemaphoreType.DMA((8,)), pltpu.SemaphoreType.DMA((8,))],
        name="settle",
    )(*arrays)


def local(features, in_proj, short_taps, long_filter, out_grad):
    return settle(hyena(in_proj, features, short_taps, out_grad, long_filter))


def solution(mesh):
    tokens = P(None, AXES)
    rows = P(AXES, None)
    return jax.shard_map(
        local,
        mesh=mesh,
        in_specs=(tokens, rows, P(), tokens, tokens),
        out_specs=(tokens, tokens, tokens, P(), rows),
        check_vma=False,
    )
```
